32 devices in a mesh: batch: 8 (over z, y), branch: 4 (over x, core).
Axes of the slice: x: 2, y: 2, z: 4, core: 2. Of those that a mesh axis runs over, the one named last changes fastest.
Arguments:
- inputs: bfloat16 [16384, 1024], P('batch'), may hold values from -6 to 6
- ln_gain: float32 [1024], replicated, may hold values from 0.5 to 1.5
- ln_shift: float32 [1024], replicated, may hold values from -1 to 1
- qkv_weight: bfloat16 [1024, 3072], P(None, 'branch'), may hold values from -0.1875 to 0.1875
- qkv_bias: float32 [3072], P('branch'), may hold values from -0.12 to 0.12
- out_weight: bfloat16 [1024, 1024], P('branch'), may hold values from -3 to 3
- up_weight: bfloat16 [1024, 4096], P(None, 'branch'), may hold values from -0.1875 to 0.1875
- up_bias: float32 [4096], P('branch'), may hold values from -1 to 1
- down_weight: bfloat16 [4096, 1024], P('branch'), may hold values from -0.09375 to 0.09375
- out_bias: float32 [1024], replicated, may hold values from -1 to 1
- feature_samples: float32 [64, 64], replicated, may hold values from -4 to 4
- lengths: int32 [8], replicated, may hold values from 1 to 15360, as said below
- cotangent: bfloat16 [16384, 1024], P('batch'), may hold values from -6 to 6
Outputs:
- output: bfloat16 [16384, 1024], P(('batch', 'branch'))
- input_grad: float32 [16384, 1024], P(('batch', 'branch'))
- gain_grad: float32 [1024], replicated
- shift_grad: float32 [1024], replicated
- qkv_weight_grad: float32 [1024, 3072], P('batch', 'branch')
- qkv_bias_grad: float32 [3072], replicated
- out_weight_grad: float32 [1024, 1024], P('branch', 'batch')
- up_weight_grad: float32 [1024, 4096], P('batch', 'branch')
- up_bias_grad: float32 [4096], replicated
- down_weight_grad: float32 [4096, 1024], P('branch', 'batch')
- out_bias_grad: float32 [1024], replicated
The draws below stay inside these ranges and needn't reach their ends.
Inputs may be any that keep to these rules, and one draw needn't show every extreme that they name: `lengths`: the 8 sequences fill the 16384 tokens in order; exactly one has 15360 tokens, the others together 16384 - 15360.
All inputs are finite; a program needn't handle non-finite values.
Results may differ from the reference program's by a relative error of at most 0.012.
The reference program's roundings to bfloat16 on the way count: a program that leaves them out, or rounds other values in their place, can miss the bound.
Values sent between devices are 32-bit elements; how exact they have to be, the bound alone decides.
No kernel may reach another device: no remote copies, remote signals or barrier semaphores. Data moves between devices by JAX's collectives and lax.ppermute only.
A program may use at most 256 MiB of HBM per device.

```python
import math
import jax
import jax.numpy as jnp
from jax import lax

D = 1024
HEADS = 16
HEAD = 64
ROT = 16
FF = 4096
FEAT = 64
GROUP = 64
TOK_DEV = 2048
SEQS = 8
TOKENS = 16384
LONGEST = 15360


def draw_lengths(key, part):
    key = jax.random.fold_in(key, 7)
    cut_key, spot_key = jax.random.split(key)
    short_total = TOK_DEV // 2
    cuts = jnp.sort(jax.random.permutation(cut_key, short_total - 1)[:SEQS - 2] + 1).astype(jnp.int32)
    bounds = jnp.concatenate([jnp.zeros((1,), jnp.int32), cuts, jnp.full((1,), short_total, jnp.int32)])
    shorts = (bounds[1:] - bounds[:-1]).astype(jnp.int32)
    spot = jax.random.randint(spot_key, (), 0, SEQS).astype(jnp.int32)
    index_all = jnp.arange(SEQS, dtype=jnp.int32)
    shifted = jnp.clip(jnp.where(index_all > spot, index_all - 1, index_all), 0, SEQS - 2)
    return jnp.where(index_all == spot, jnp.int32(LONGEST), shorts[shifted]).astype(jnp.int32)


def with_spikes(entries, stream_key, source, target, blocks, factor):
    def block_of(dim):
        return (jnp.arange(entries.shape[dim]) // (entries.shape[dim] // blocks)).reshape((-1,) + (1,) * (entries.ndim - 1 - dim))

    near = jax.random.permutation(stream_key, blocks)[block_of(target)]
    second = (block_of(target) + blocks // 2) % blocks
    return jnp.where((block_of(source) == near) | (block_of(source) == second), factor * entries, entries)


def level_of(own_key, shape, cuts, smallest, largest):
    level, own = 1.0, jax.random.fold_in(own_key, 6)
    for dim, shards_of in cuts:
        draws = jnp.exp(jax.random.uniform(jax.random.fold_in(own, dim), (shards_of,), jnp.float32, smallest / len(cuts), largest / len(cuts)))
        level = level * jnp.repeat(draws, shape[dim] // shards_of).reshape([-1 if axis == dim else 1 for axis in range(len(shape))])
    return level


def noise(key, extent, deviation, reach, cuts=(), kind=jnp.bfloat16):
    loudness = level_of(key, extent, cuts, -0.22, 0.18) if cuts else 1.0
    values = jax.random.normal(key, extent, jnp.float32) * deviation * loudness
    return jnp.minimum(jnp.maximum(values, -reach), reach).astype(kind)


def noise_with(rng, extent, spread, bound, cuts, heavy, held_as=jnp.bfloat16):
    values = spread * jax.random.normal(rng, extent, jnp.float32)
    if cuts:
        values = values * level_of(rng, extent, cuts, -0.22, 0.18)
    return jnp.clip(with_spikes(values, jax.random.fold_in(rng, 3), *heavy), -bound, bound).astype(held_as)


def setup_inputs(seed: int = 0) -> dict:
    streams_of = jax.random.split(jax.random.key(seed), 14)
    inputs = noise(streams_of[0], (TOKENS, D), 1.0, 6.0, ((0, 8),))
    ln_gain = jnp.clip(1.0 + 0.1 * jax.random.normal(streams_of[1], (D,), jnp.float32), 0.5, 1.5)
    ln_shift = noise(streams_of[2], (D,), 0.2, 1.0, (), jnp.float32)
    qkv_weight = noise(streams_of[3], (D, 3 * D), D ** -0.5, 0.1875, ((1, 4),))
    qkv_bias = noise(streams_of[4], (3 * D,), 0.02, 0.12, ((0, 4),), jnp.float32)
    out_weight = noise(streams_of[5], (D, D), (max(D // 256, 1)) ** -0.5, 3.0, ((0, 4),))
    up_weight = noise(streams_of[6], (D, FF), D ** -0.5, 0.1875, ((1, 4),))
    up_bias = noise(streams_of[7], (FF,), 0.2, 1.0, ((0, 4),), jnp.float32)
    down_weight = noise(streams_of[8], (FF, D), FF ** -0.5, 0.09375, ((0, 4),))
    out_bias = noise(streams_of[9], (D,), 0.2, 1.0, (), jnp.float32)
    feature_samples = noise(streams_of[10], (FEAT, HEAD), 1.0, 4.0, (), jnp.float32)
    lengths = draw_lengths(jax.random.fold_in(streams_of[13], 71), 0)
    cotangent = noise_with(streams_of[12], (TOKENS, D), 1.0, 6.0, ((0, 8),), (0, 1, 8, 2.0))
    return {"inputs": inputs, "ln_gain": ln_gain, "ln_shift": ln_shift, "qkv_weight": qkv_weight, "qkv_bias": qkv_bias, "out_weight": out_weight, "up_weight": up_weight, "up_bias": up_bias, "down_weight": down_weight, "out_bias": out_bias, "feature_samples": feature_samples, "lengths": lengths, "cotangent": cotangent}


highest = lax.Precision.HIGHEST
epsilon = 1e-05

@jax.custom_vjp
def low(v):
    return lax.optimization_barrier(v.astype(jnp.bfloat16)).astype(jnp.float32)

@jax.custom_vjp
def low_back(v):
    return v

def low_keep(v):
    return (low(v), None)

def low_pass(kept, grad):
    return (grad,)

def back_keep(v):
    return (v, None)

def back_low(kept, grad):
    return (low(grad),)
low.defvjp(low_keep, low_pass)
low_back.defvjp(back_keep, back_low)

def dct_table(order_size):
    row_ids = jnp.arange(order_size, dtype=jnp.float32)[:, None]
    col_ids = jnp.arange(order_size, dtype=jnp.float32)[None, :]
    table = jnp.cos(math.pi * (col_ids + 0.5) * row_ids / order_size) * math.sqrt(2.0 / order_size)
    return jnp.where(row_ids == 0.0, table * math.sqrt(0.5), table)

def rotate(values_in, in_seq_place, rotary, direction):
    half_rot = rotary // 2
    frequency = 10000.0 ** (-2.0 * jnp.arange(half_rot, dtype=jnp.float32) / rotary)
    angles = in_seq_place.astype(jnp.float32)[:, None] * frequency[None, :]
    cosine = jnp.cos(angles)[:, None, :]
    sine_part = direction * jnp.sin(angles)[:, None, :]
    leading = values_in[..., :half_rot]
    trailing = values_in[..., half_rot:rotary]
    return jnp.concatenate([leading * cosine - trailing * sine_part, trailing * cosine + leading * sine_part, values_in[..., rotary:]], axis=-1)

def attend(feat_q, feat_k, value_rows, segment):
    blocks = feat_q.shape[0] // GROUP
    head_count = feat_q.shape[1]

    def grouped(tensor):
        return tensor.reshape((blocks, GROUP) + tensor.shape[1:])
    index_c = jnp.arange(GROUP)
    causal = index_c[:, None] >= index_c[None, :]

    def group_step(carry, block):
        kv_state, norm_sum, prior_seg = carry
        block_q, block_k, block_v, block_seg = block
        window = (causal & (block_seg[:, None] == block_seg[None, :])).astype(jnp.float32)
        scores = jnp.einsum('thf,shf->hts', block_q, block_k, precision=highest) * window[None]
        numerator = jnp.einsum('hts,shd->thd', scores, block_v, precision=highest)
        denominator = jnp.einsum('hts->th', scores)
        carried = (block_seg == prior_seg).astype(jnp.float32)
        numerator = numerator + carried[:, None, None] * jnp.einsum('thf,hfd->thd', block_q, kv_state, precision=highest)
        denominator = denominator + carried[:, None] * jnp.einsum('thf,hf->th', block_q, norm_sum, precision=highest)
        last_seg = block_seg[-1].astype(jnp.int32)
        tail_mask = (block_seg == last_seg).astype(jnp.float32)
        retain = (prior_seg == last_seg).astype(jnp.float32)
        kv_state = retain * kv_state + jnp.einsum('shf,s,shd->hfd', block_k, tail_mask, block_v, precision=highest)
        norm_sum = retain * norm_sum + jnp.einsum('shf,s->hf', block_k, tail_mask)
        return ((kv_state, norm_sum, last_seg), numerator / denominator[:, :, None])
    initial = (jnp.zeros((head_count, feat_q.shape[2], value_rows.shape[2]), jnp.float32), jnp.zeros((head_count, feat_q.shape[2]), jnp.float32), jnp.int32(-1))
    blocks_in = (grouped(feat_q), grouped(feat_k), grouped(value_rows), grouped(segment))
    _, result = lax.scan(jax.checkpoint(group_step), initial, blocks_in)
    return result.reshape(feat_q.shape[0], head_count, value_rows.shape[2])

def reference(inputs, ln_gain, ln_shift, qkv_weight, qkv_bias, out_weight, up_weight, up_bias, down_weight, out_bias, feature_samples, lengths, cotangent):
    tok_count = inputs.shape[0]
    seq_ends = jnp.cumsum(lengths, dtype=jnp.int32).astype(jnp.int32)
    position = jnp.arange(tok_count, dtype=jnp.int32)
    passed = position[:, None] >= seq_ends[None, :]
    segment = lax.optimization_barrier(jnp.sum(passed.astype(jnp.int32), axis=1, dtype=jnp.int32)).astype(jnp.int32)
    in_seq_place = (position - lax.optimization_barrier(jnp.sum(jnp.where(passed, lengths[None, :], 0), axis=1, dtype=jnp.int32))).astype(jnp.int32)
    root_four = HEAD ** 0.25

    def layer(float_inputs, gain, shift, w_qkv, b_qkv, w_out, w_up, b_up, w_down, b_out):
        samples_dct = jnp.dot(feature_samples, dct_table(HEAD), precision=highest)

        def featurize(turned):
            argument = jnp.einsum('thd,fd->thf', turned, samples_dct, precision=highest) / root_four - lax.optimization_barrier(jnp.sum(turned * turned, axis=-1, keepdims=True)) / (2.0 * math.sqrt(HEAD))
            return jnp.exp(argument) / math.sqrt(FEAT)
        centered = float_inputs - lax.optimization_barrier(jnp.mean(float_inputs, axis=1, keepdims=True))
        unit_rows = centered * lax.rsqrt(lax.optimization_barrier(jnp.mean(centered * centered, axis=1, keepdims=True)) + epsilon)
        normed = low(unit_rows * gain + shift)
        projected = low(low_back(jnp.dot(normed, w_qkv, precision=highest) + b_qkv))
        triple = projected.reshape(tok_count, HEADS, 3, HEAD)
        q_turn = rotate(triple[:, :, 0], in_seq_place, ROT, 1.0)
        k_turn = rotate(triple[:, :, 1], in_seq_place, ROT, 1.0)
        attended = attend(featurize(q_turn), featurize(k_turn), triple[:, :, 2], segment)
        mixed_rows = low(attended.reshape(tok_count, D))
        pre_act = low_back(jnp.dot(normed, w_up, precision=highest) + b_up)
        hidden = low(jax.nn.gelu(pre_act, approximate=False))
        branch_total = jnp.dot(mixed_rows, w_out, precision=highest) + jnp.dot(hidden, w_down, precision=highest)
        return float_inputs + branch_total + b_out
    output, pullback = jax.vjp(layer, inputs.astype(jnp.float32), ln_gain, ln_shift, qkv_weight.astype(jnp.float32), qkv_bias, out_weight.astype(jnp.float32), up_weight.astype(jnp.float32), up_bias, down_weight.astype(jnp.float32), out_bias)
    grads = pullback(cotangent.astype(jnp.float32))
    return (output.astype(jnp.bfloat16), grads[0], grads[1], grads[2], grads[3], grads[4], grads[5], grads[6], grads[7], grads[8], grads[9])
```

```python
import math

import numpy as np

import jax
import jax.numpy as jnp
from jax import lax
from jax.experimental import pallas as pl
from jax.experimental.pallas import tpu as pltpu
from jax.sharding import PartitionSpec as P

ROT = 16
CHUNK = 256
ROWS = 512
LANE = 128
epsilon = 1e-05
f32 = jnp.float32
bf16 = jnp.bfloat16
HALF_ROOT = math.sqrt(0.5)
GAUSS = 1.0 / math.sqrt(2.0 * math.pi)
VMEM_BYTES = 60 * 2**20


def nn(a, b):
    return lax.dot_general(a, b, (((1,), (0,)), ((), ())), preferred_element_type=f32)


def nt(a, b):
    return lax.dot_general(a, b, (((1,), (1,)), ((), ())), preferred_element_type=f32)


def tn(a, b):
    return lax.dot_general(a, b, (((0,), (0,)), ((), ())), preferred_element_type=f32)


def two(value):
    high = value.astype(bf16)
    return high, (value - high.astype(f32)).astype(bf16)


def exact3(dot, a, b):
    return dot(a[0], b[0]) + (dot(a[1], b[0]) + dot(a[0], b[1]))


def params(flops, moved, exps=0):
    return {
        "compiler_params": pltpu.CompilerParams(vmem_limit_bytes=VMEM_BYTES),
        "cost_estimate": pl.CostEstimate(
            flops=int(flops), bytes_accessed=int(moved), transcendentals=int(exps)
        ),
    }


def whole(*shape):
    return pl.BlockSpec(shape, lambda *ids: (0,) * len(shape))


SMEM = pl.BlockSpec(memory_space=pltpu.SMEM)


def dct_table(size):
    row = np.arange(size)[:, None]
    col = np.arange(size)[None, :]
    table = np.cos(math.pi * (col + 0.5) * row / size) * math.sqrt(2.0 / size)
    table[0] *= math.sqrt(0.5)
    return table.astype(np.float32)


def expand_table(head):
    half = ROT // 2
    table = np.zeros((ROT, 3 * LANE), np.float32)
    for lane in range(LANE):
        place = lane % head
        if place < half:
            table[place, lane] = 1.0
            table[half + place, LANE + lane] = -1.0
        elif place < ROT:
            table[place - half, lane] = 1.0
            table[place, 2 * LANE + lane] = 1.0
    return np.concatenate([table] * 3, axis=0)


def seq_start(info, place):
    start = jnp.zeros_like(place)
    for j in range(info.shape[0] - 4):
        end = info[4 + j]
        start = jnp.where(place >= end, end, start)
    return start


def head_block(head, rows, cols):
    r = lax.broadcasted_iota(jnp.int32, (rows, cols), 0) // head
    c = lax.broadcasted_iota(jnp.int32, (rows, cols), 1) // head
    return r == c


def head_lanes(head, h, width):
    return (lax.broadcasted_iota(jnp.int32, (1, width), 1) // head) == h


def turn_tables(cs, expand, head, width):
    wide = tn(cs, expand)
    lane = lax.broadcasted_iota(jnp.int32, (1, LANE), 1) % head
    cosine = wide[:, :LANE] + jnp.where(lane < ROT, 0.0, 1.0)
    times = width // LANE

    def tile(part):
        return jnp.concatenate([part] * times, axis=1)

    return tile(cosine), tile(wide[:, LANE : 2 * LANE]), tile(wide[:, 2 * LANE :])


def turn(value, tables, sign):
    cosine, up, down = tables
    width = value.shape[1]
    half = ROT // 2
    moved = pltpu.roll(value, width - half, 1) * up + pltpu.roll(value, half, 1) * down
    return value * cosine + moved if sign > 0 else value * cosine - moved


def fold_state(full, head, width):
    block = head_block(head, width, width)
    s_part = jnp.where(block, full[:, :width], 0.0)
    n_part = jnp.where(block, full[:, width:], 0.0)
    s_fold = sum(s_part[:, i * LANE : (i + 1) * LANE] for i in range(width // LANE))
    n_fold = sum(n_part[:, i * LANE : (i + 1) * LANE] for i in range(width // LANE))
    return s_fold + pltpu.roll(n_fold, LANE // 2, 1)


def unfold_state(packed, head, width):
    block = head_block(head, width, width)
    times = width // LANE
    s_part = jnp.concatenate([packed] * times, axis=1)
    n_part = jnp.concatenate([pltpu.roll(packed, LANE // 2, 1)] * times, axis=1)
    return jnp.concatenate([jnp.where(block, s_part, 0.0), jnp.where(block, n_part, 0.0)], axis=1)


def block_at(i, bit, side):
    low = i & ((1 << bit) - 1)
    return ((i >> bit) << (bit + 1)) + low + side * (1 << bit)


def feed_kernel(first, bit, info, x, gain, shift, up_w, up_b, down_w, cot, *refs):
    if first:
        normed_o, hidden_o, gpre_o, send_o, keep_o, ub_o, cb_o, down_acc, up_acc = refs
    else:
        hidden_o, gpre_o, send_o, keep_o, ub_o, down_acc, up_acc = refs
    step = pl.program_id(0)
    rows = cot.shape[0]
    width = up_w.shape[1]

    @pl.when(step == 0)
    def _():
        down_acc[...] = jnp.zeros_like(down_acc)
        up_acc[...] = jnp.zeros_like(up_acc)
        ub_o[...] = jnp.zeros_like(ub_o)
        if first:
            cb_o[...] = jnp.zeros_like(cb_o)

    if first:
        xf = x[...].astype(f32)
        centered = xf - jnp.mean(xf, axis=1, keepdims=True)
        inv = lax.rsqrt(jnp.mean(centered * centered, axis=1, keepdims=True) + epsilon)
        normed = (centered * inv * gain[...] + shift[...]).astype(bf16)
        normed_o[...] = normed
    else:
        normed = x[...]
    c = cot[...]
    pre = nn(normed, up_w[...]) + up_b[...]
    grad_hidden = nt(c, down_w[...])
    phi = 0.5 + 0.5 * lax.erf(pre * HALF_ROOT)
    hidden = (pre * phi).astype(bf16)
    hidden_o[...] = hidden
    down_acc[...] += tn(hidden, c)
    slope = phi + pre * jnp.exp(-0.5 * pre * pre) * GAUSS
    gpre = (grad_hidden * slope).astype(bf16)
    gpre_o[...] = gpre
    up_acc[...] += tn(normed, gpre)
    ub_o[...] += jnp.sum(gpre.astype(f32).reshape(rows // 8, 8, width), axis=0)
    if first:
        cb_o[...] += jnp.sum(c.astype(f32).reshape(rows // 8, 8, c.shape[1]), axis=0)

    @pl.when(step == pl.num_programs(0) - 1)
    def _():
        mine = info[1]
        for out, side in ((send_o, 1 - mine), (keep_o, mine)):
            for i in range(out.shape[0]):
                at = pl.multiple_of(block_at(i, bit, side) * LANE, LANE)
                out[i, :width, :] = down_acc[:, pl.ds(at, LANE)]
                for j in range(width // LANE):
                    out[i, width + j * LANE : width + (j + 1) * LANE, :] = up_acc[
                        pl.ds(at, LANE), j * LANE : (j + 1) * LANE
                    ]


def feed(part, bit, info, x, gain, shift, up_w, up_b, down_w, cot):
    first = part == 0
    tokens, model = cot.shape
    width = up_w.shape[1] // 2
    blocks = model // LANE // 2
    row = lambda n: pl.BlockSpec((ROWS, n), lambda i: (i, 0))
    piece = jax.ShapeDtypeStruct((blocks, width + (width // LANE) * LANE, LANE), f32)
    shapes = [
        jax.ShapeDtypeStruct((tokens, width), bf16),
        jax.ShapeDtypeStruct((tokens, width), bf16),
        piece,
        piece,
        jax.ShapeDtypeStruct((8, width), f32),
    ]
    specs = [row(width), row(width), whole(*piece.shape), whole(*piece.shape), whole(8, width)]
    if first:
        shapes = [jax.ShapeDtypeStruct((tokens, model), bf16), *shapes]
        specs = [row(model), *specs, whole(8, model)]
        shapes.append(jax.ShapeDtypeStruct((8, model), f32))

    def body(*refs):
        feed_kernel(first, bit, *refs)

    return pl.pallas_call(
        body,
        grid=(tokens // ROWS,),
        in_specs=[
            SMEM,
            row(model),
            whole(1, model),
            whole(1, model),
            pl.BlockSpec((model, width), lambda i: (0, part)),
            pl.BlockSpec((1, width), lambda i: (0, part)),
            pl.BlockSpec((width, model), lambda i: (part, 0)),
            row(model),
        ],
        out_specs=specs,
        out_shape=shapes,
        scratch_shapes=[pltpu.VMEM((width, model), f32), pltpu.VMEM((model, width), f32)],
        name="feed_forward",
        **params(8 * tokens * model * width, 16 * tokens * model, 2 * tokens * width),
    )(info, x, gain, shift, up_w, up_b, down_w, cot)


def project_kernel(
    head, info, normed, w_in, b_in, cs, expand, samples, dct_t, cot, out_w,
    qf_o, kf_o, v_o, qt_o, kt_o, ga_o, w_o, basis_o, state_o, w_s, b_s, basis_s, state_s,
):
    step = pl.program_id(0)
    width = out_w.shape[0]
    heads = width // head
    rows = normed.shape[0]

    @pl.when(step == 0)
    def _():
        for part in range(3):
            at = [(3 * h + part) * head for h in range(heads)]
            w_s[:, part * width : (part + 1) * width] = jnp.concatenate(
                [w_in[:, a : a + head] for a in at], axis=1
            )
            b_s[:, part * width : (part + 1) * width] = jnp.concatenate(
                [b_in[:, a : a + head] for a in at], axis=1
            )
        basis = lax.dot_general(
            dct_t[...], samples[...], (((1,), (1,)), ((), ())),
            preferred_element_type=f32, precision=lax.Precision.HIGHEST,
        )
        basis = basis * (1.0 / head**0.25)
        wide = jnp.concatenate([jnp.concatenate([basis] * heads, axis=1)] * heads, axis=0)
        basis_s[...] = jnp.where(head_block(head, width, width), wide, 0.0)
        basis_o[...] = basis_s[...]
        w_o[...] = w_s[...]
        state_s[...] = jnp.zeros_like(state_s)

    projected = (nn(normed[...], w_s[...]) + b_s[...]).astype(bf16)
    tables = turn_tables(cs[...], expand[...], head, width)
    basis = two(basis_s[...])
    ones = jnp.where(head_block(head, width, width), 1.0 / (2.0 * math.sqrt(head)), 0.0).astype(bf16)

    def features(part):
        turned = turn(part.astype(f32), tables, 1)
        square = two(turned * turned)
        argument = exact3(nn, two(turned), basis) - (nn(square[0], ones) + nn(square[1], ones))
        return turned.astype(bf16), (jnp.exp(argument) * (1.0 / math.sqrt(samples.shape[0]))).astype(bf16)

    k_turn, k_feat = features(projected[:, width : 2 * width])
    value = projected[:, 2 * width :]
    q_turn, q_feat = features(projected[:, :width])
    qf_o[...], kf_o[...], v_o[...], qt_o[...], kt_o[...] = q_feat, k_feat, value, q_turn, k_turn
    ga_o[...] = nt(cot[...], out_w[...])
    place = info[0] + step * rows + lax.broadcasted_iota(jnp.int32, (rows, 1), 0)
    tail = jnp.where(place >= info[2], 1.0, 0.0).astype(bf16)
    state_s[...] += tn(k_feat * tail, jnp.concatenate([value, jnp.ones_like(value)], axis=1))

    @pl.when(step == pl.num_programs(0) - 1)
    def _():
        state_o[...] = fold_state(state_s[...], head, width)


def project(head, info, normed, w_in, b_in, cs, expand, samples, dct_t, cot, out_w):
    tokens, model = normed.shape
    width = out_w.shape[0]
    row = lambda n: pl.BlockSpec((ROWS, n), lambda i: (i, 0))
    narrow = jax.ShapeDtypeStruct((tokens, width), bf16)

    def body(*refs):
        project_kernel(head, *refs)

    return pl.pallas_call(
        body,
        grid=(tokens // ROWS,),
        in_specs=[
            SMEM,
            row(model),
            whole(*w_in.shape),
            whole(*b_in.shape),
            pl.BlockSpec((cs.shape[0], ROWS), lambda i: (0, i)),
            whole(*expand.shape),
            whole(*samples.shape),
            whole(*dct_t.shape),
            row(model),
            whole(*out_w.shape),
        ],
        out_specs=[row(width)] * 6
        + [whole(*w_in.shape), whole(width, width), whole(width, LANE)],
        out_shape=[narrow] * 5
        + [
            jax.ShapeDtypeStruct((tokens, width), f32),
            jax.ShapeDtypeStruct(w_in.shape, bf16),
            jax.ShapeDtypeStruct((width, width), f32),
            jax.ShapeDtypeStruct((width, LANE), f32),
        ],
        scratch_shapes=[
            pltpu.VMEM(w_in.shape, bf16),
            pltpu.VMEM(b_in.shape, f32),
            pltpu.VMEM((width, width), f32),
            pltpu.VMEM((width, 2 * width), f32),
        ],
        name="project",
        **params(8 * tokens * model * width + 20 * tokens * width * width, 16 * tokens * model, 2 * tokens * width),
    )(info, normed, w_in, b_in, cs, expand, samples, dct_t, cot, out_w)


def turned_grad(grad_feat, feat, turned, basis, tables, head, width):
    weighted = two(grad_feat * feat.astype(f32))
    ones = jnp.where(head_block(head, width, width), 1.0 / math.sqrt(head), 0.0).astype(bf16)
    total = nn(weighted[0], ones) + nn(weighted[1], ones)
    grad = exact3(nt, weighted, basis) - total * turned.astype(f32)
    return turn(grad, tables, -1).astype(bf16)


def attend_kernel(
    head, bit, per_step, info, qf, kf, v, qt, ga, cs, expand, basis_i, state_i, normed, cot,
    mixed_o, gq_o, gk_o, gv_o, back_o, total_o, send_o, keep_o, qb_o, state_s, q_acc, o_acc, total_s,
):
    step = pl.program_id(0)
    width = qf.shape[1]
    heads = width // head

    @pl.when(step == 0)
    def _():
        state_s[...] = unfold_state(state_i[...], head, width)
        q_acc[...] = jnp.zeros_like(q_acc)
        o_acc[...] = jnp.zeros_like(o_acc)
        total_s[...] = jnp.zeros_like(total_s)
        qb_o[...] = jnp.zeros_like(qb_o)

    basis = two(basis_i[...])
    block = head_block(head, width, width)
    both = jnp.concatenate([block, block], axis=1)
    ones = jnp.where(block, 1.0, 0.0).astype(bf16)
    lanes = [jnp.where(head_lanes(head, h, width), 1.0, 0.0).astype(bf16) for h in range(heads)]
    state = state_s[...]
    total = total_s[...]
    for sub in range(per_step):
        at = slice(sub * CHUNK, (sub + 1) * CHUNK)
        begin = info[0] + (step * per_step + sub) * CHUNK
        last = seq_start(info, begin + CHUNK - 1)
        row = lax.broadcasted_iota(jnp.int32, (CHUNK, 1), 0)
        start = seq_start(info, begin + row)
        col = lax.broadcasted_iota(jnp.int32, (CHUNK, CHUNK), 1)
        window = (col <= lax.broadcasted_iota(jnp.int32, (CHUNK, CHUNK), 0)) & (col + begin >= start)
        carried = jnp.where(start < begin, 1.0, 0.0)
        q, k, value = qf[at, :], kf[at, :], v[at, :]
        state_two = two(state)
        from_state = nn(q, state_two[0]) + nn(q, state_two[1])
        sums = carried * from_state
        scores = []
        for h in range(heads):
            score = jnp.where(window, nt(q * lanes[h], k), 0.0).astype(bf16)
            scores.append(score)
            right = jnp.concatenate([value * lanes[h], jnp.broadcast_to(lanes[h], value.shape)], axis=1)
            sums = sums + nn(score, right)
        over = 1.0 / sums[:, width:]
        attended = sums[:, :width] * over
        mixed = attended.astype(bf16)
        mixed_o[at, :] = mixed
        grad_att = ga[at, :]
        g_num = grad_att * over
        product = two(grad_att * attended)
        g_den = -(nn(product[0], ones) + nn(product[1], ones)) * over
        g_low = g_num.astype(bf16)
        g_both = two(jnp.concatenate([g_num, g_den * (1.0 / head)], axis=1))
        grad_fq = carried * exact3(nt, g_both, state_two)
        grad_fk = jnp.zeros((CHUNK, width), f32)
        grad_v = jnp.zeros((CHUNK, width), f32)
        for h in range(heads):
            g_head = g_low * lanes[h]
            mixing = nt(g_head, value) + g_den[:, h * head : h * head + 1]
            mixing = jnp.where(window, mixing, 0.0).astype(bf16)
            grad_fq = grad_fq + nn(mixing, k * lanes[h])
            grad_fk = grad_fk + tn(mixing, q * lanes[h])
            grad_v = grad_v + tn(scores[h], g_head)
        gk_o[at, :] = grad_fk
        gv_o[at, :] = grad_v
        carried_g = (carried * jnp.concatenate([g_num, g_den], axis=1)).astype(bf16)
        back = tn(q, carried_g)
        back_o[sub] = fold_state(back, head, width)
        live = jnp.where(seq_start(info, begin - 1) < info[0], 1.0, 0.0)
        total = total + live * back
        tail = jnp.where(begin + row >= last, 1.0, 0.0).astype(bf16)
        retain = jnp.where(last < begin, 1.0, 0.0)
        added = tn(k * tail, jnp.concatenate([value, jnp.ones_like(value)], axis=1))
        state = retain * state + jnp.where(both, added, 0.0)
        tables = turn_tables(cs[:, at], expand[...], head, width)
        gq = turned_grad(grad_fq, q, qt[at, :], basis, tables, head, width)
        gq_o[at, :] = gq
        qb_o[...] += jnp.sum(gq.astype(f32).reshape(CHUNK // 8, 8, width), axis=0)
        q_acc[...] += tn(normed[at, :], gq)
        o_acc[...] += tn(mixed, cot[at, :])
    state_s[...] = state
    total_s[...] = total

    @pl.when(step == pl.num_programs(0) - 1)
    def _():
        total_o[...] = fold_state(total, head, width)
        mine = info[1]
        for out, side in ((send_o, 1 - mine), (keep_o, mine)):
            for i in range(out.shape[0]):
                spot = pl.multiple_of(block_at(i, bit, side) * LANE, LANE)
                out[i, :width, :] = o_acc[:, pl.ds(spot, LANE)]
                for j in range(width // LANE):
                    out[i, width + j * LANE : width + (j + 1) * LANE, :] = q_acc[
                        pl.ds(spot, LANE), j * LANE : (j + 1) * LANE
                    ]


def attend(head, bit, info, qf, kf, v, qt, ga, cs, expand, basis, state, normed, cot):
    tokens, width = qf.shape
    model = cot.shape[1]
    per_step = 2
    rows = per_step * CHUNK
    chunks = tokens // CHUNK
    row = lambda n: pl.BlockSpec((rows, n), lambda i: (i, 0))
    piece = jax.ShapeDtypeStruct((model // LANE // 2, 2 * width, LANE), f32)

    def body(*refs):
        attend_kernel(head, bit, per_step, *refs)

    return pl.pallas_call(
        body,
        grid=(tokens // rows,),
        in_specs=[
            SMEM,
            *[row(width)] * 5,
            pl.BlockSpec((cs.shape[0], rows), lambda i: (0, i)),
            whole(*expand.shape),
            whole(width, width),
            whole(width, LANE),
            row(model),
            row(model),
        ],
        out_specs=[
            *[row(width)] * 4,
            pl.BlockSpec((per_step, width, LANE), lambda i: (i, 0, 0)),
            whole(width, LANE),
            whole(*piece.shape),
            whole(*piece.shape),
            whole(8, width),
        ],
        out_shape=[
            jax.ShapeDtypeStruct((tokens, width), bf16),
            jax.ShapeDtypeStruct((tokens, width), bf16),
            jax.ShapeDtypeStruct((tokens, width), f32),
            jax.ShapeDtypeStruct((tokens, width), f32),
            jax.ShapeDtypeStruct((chunks, width, LANE), f32),
            jax.ShapeDtypeStruct((width, LANE), f32),
            piece,
            piece,
            jax.ShapeDtypeStruct((8, width), f32),
        ],
        scratch_shapes=[
            pltpu.VMEM((width, 2 * width), f32),
            pltpu.VMEM((model, width), f32),
            pltpu.VMEM((width, model), f32),
            pltpu.VMEM((width, 2 * width), f32),
        ],
        name="attend",
        **params(4 * tokens * model * width + 120 * tokens * width * width, 20 * tokens * width + 4 * tokens * model),
    )(info, qf, kf, v, qt, ga, cs, expand, basis, state, normed, cot)


def keys_kernel(
    head, bit, per_step, info, kf, v, kt, gk, gv, back, cs, expand, basis_i, state_i, normed,
    gkv_o, send_o, keep_o, kvb_o, state_s, acc,
):
    step = pl.program_id(0)
    width = kf.shape[1]

    @pl.when(step == 0)
    def _():
        state_s[...] = unfold_state(state_i[...], head, width)
        acc[...] = jnp.zeros_like(acc)
        kvb_o[...] = jnp.zeros_like(kvb_o)

    basis = two(basis_i[...])
    state = state_s[...]
    for sub in reversed(range(per_step)):
        at = slice(sub * CHUNK, (sub + 1) * CHUNK)
        begin = info[0] + ((pl.num_programs(0) - 1 - step) * per_step + sub) * CHUNK
        last = seq_start(info, begin + CHUNK - 1)
        row = lax.broadcasted_iota(jnp.int32, (CHUNK, 1), 0)
        tail = jnp.where(begin + row >= last, 1.0, 0.0)
        k, value = kf[at, :], v[at, :]
        state_two = two(state)
        right = jnp.concatenate([value, jnp.full(value.shape, 1.0 / head, bf16)], axis=1)
        grad_fk = gk[at, :] + tail * (nt(right, state_two[0]) + nt(right, state_two[1]))
        grad_v = gv[at, :] + tail * (
            nn(k, state_two[0][:, :width]) + nn(k, state_two[1][:, :width])
        )
        retain = jnp.where(last < begin, 1.0, 0.0)
        state = unfold_state(back[sub], head, width) + retain * state
        tables = turn_tables(cs[:, at], expand[...], head, width)
        grad_k = turned_grad(grad_fk, k, kt[at, :], basis, tables, head, width)
        both = jnp.concatenate([grad_k, grad_v.astype(bf16)], axis=1)
        gkv_o[at, :] = both
        kvb_o[...] += jnp.sum(both.astype(f32).reshape(CHUNK // 8, 8, 2 * width), axis=0)
        acc[...] += tn(normed[at, :], both)
    state_s[...] = state

    @pl.when(step == pl.num_programs(0) - 1)
    def _():
        mine = info[1]
        for out, side in ((send_o, 1 - mine), (keep_o, mine)):
            for i in range(out.shape[0]):
                spot = pl.multiple_of(block_at(i, bit, side) * LANE, LANE)
                for j in range(2 * width // LANE):
                    out[i, j * LANE : (j + 1) * LANE, :] = acc[
                        pl.ds(spot, LANE), j * LANE : (j + 1) * LANE
                    ]


def keys(head, bit, info, kf, v, kt, gk, gv, back, cs, expand, basis, state, normed):
    tokens, width = kf.shape
    model = normed.shape[1]
    per_step = 2
    rows = per_step * CHUNK
    steps = tokens // rows
    row = lambda n: pl.BlockSpec((rows, n), lambda i: (steps - 1 - i, 0))
    piece = jax.ShapeDtypeStruct((model // LANE // 2, 2 * width, LANE), f32)

    def body(*refs):
        keys_kernel(head, bit, per_step, *refs)

    return pl.pallas_call(
        body,
        grid=(steps,),
        in_specs=[
            SMEM,
            *[row(width)] * 5,
            pl.BlockSpec((per_step, width, LANE), lambda i: (steps - 1 - i, 0, 0)),
            pl.BlockSpec((cs.shape[0], rows), lambda i: (0, steps - 1 - i)),
            whole(*expand.shape),
            whole(width, width),
            whole(width, LANE),
            row(model),
        ],
        out_specs=[row(2 * width), whole(*piece.shape), whole(*piece.shape), whole(8, 2 * width)],
        out_shape=[
            jax.ShapeDtypeStruct((tokens, 2 * width), bf16),
            piece,
            piece,
            jax.ShapeDtypeStruct((8, 2 * width), f32),
        ],
        scratch_shapes=[pltpu.VMEM((width, 2 * width), f32), pltpu.VMEM((model, 2 * width), f32)],
        name="keys",
        **params(4 * tokens * model * width + 40 * tokens * width * width, 20 * tokens * width + 2 * tokens * model),
    )(info, kf, v, kt, gk, gv, back, cs, expand, basis, state, normed)


def outward_kernel(hidden0, hidden1, mixed, down_w, out_w, out):
    half = hidden0.shape[1]
    out[...] = (
        nn(hidden0[...], down_w[:half, :]) + nn(hidden1[...], down_w[half:, :])
    ) + nn(mixed[...], out_w[...])


def outward(hidden0, hidden1, mixed, down_w, out_w):
    tokens, half = hidden0.shape
    model = down_w.shape[1]
    row = lambda n: pl.BlockSpec((ROWS, n), lambda i: (i, 0))
    return pl.pallas_call(
        outward_kernel,
        grid=(tokens // ROWS,),
        in_specs=[row(half), row(half), row(mixed.shape[1]), whole(*down_w.shape), whole(*out_w.shape)],
        out_specs=row(model),
        out_shape=jax.ShapeDtypeStruct((tokens, model), f32),
        name="outward",
        **params(2 * tokens * model * (2 * half + mixed.shape[1]), 8 * tokens * model),
    )(hidden0, hidden1, mixed, down_w, out_w)


def inward_kernel(gpre0, gpre1, gq, up_w, qkv_w, out):
    half, width = gpre0.shape[1], gq.shape[1]
    out[...] = (
        nt(gpre0[...], up_w[:, :half]) + nt(gpre1[...], up_w[:, half:])
    ) + nt(gq[...], qkv_w[:, :width])


def inward(gpre0, gpre1, gq, up_w, qkv_w):
    tokens, half = gpre0.shape
    model = up_w.shape[0]
    row = lambda n: pl.BlockSpec((ROWS, n), lambda i: (i, 0))
    return pl.pallas_call(
        inward_kernel,
        grid=(tokens // ROWS,),
        in_specs=[row(half), row(half), row(gq.shape[1]), whole(*up_w.shape), whole(*qkv_w.shape)],
        out_specs=row(model),
        out_shape=jax.ShapeDtypeStruct((tokens, model), f32),
        name="inward",
        **params(2 * tokens * model * (2 * half + gq.shape[1]), 8 * tokens * model),
    )(gpre0, gpre1, gq, up_w, qkv_w)


def close_kernel(info, prior, gkv, qkv_w, x, send_o, keep_o, gain_o, shift_o):
    step = pl.program_id(0)
    steps = pl.num_programs(0)
    width = gkv.shape[1] // 2
    rows, model = prior.shape

    @pl.when(step == 0)
    def _():
        gain_o[...] = jnp.zeros_like(gain_o)
        shift_o[...] = jnp.zeros_like(shift_o)

    grad = prior[...] + nt(gkv[...], qkv_w[:, width:])

    @pl.when(step < steps // 2)
    def _():
        send_o[...] = grad

    @pl.when(step >= steps // 2)
    def _():
        keep_o[...] = grad

    xf = x[...].astype(f32)
    centered = xf - jnp.mean(xf, axis=1, keepdims=True)
    unit = centered * lax.rsqrt(jnp.mean(centered * centered, axis=1, keepdims=True) + epsilon)
    gain_o[...] += jnp.sum((grad * unit).reshape(rows // 8, 8, model), axis=0)
    shift_o[...] += jnp.sum(grad.reshape(rows // 8, 8, model), axis=0)


def close(info, prior, gkv, qkv_w, x, shares):
    tokens, model = prior.shape
    per_share = tokens // shares // CHUNK
    half = shares // 2 * per_share

    def rows_of(i, info):
        other = jnp.where(i < half, 1 - info[3], info[3])
        within = i % half
        return (2 * (within // per_share) + other) * per_share + within % per_share, 0

    row = lambda n: pl.BlockSpec((CHUNK, n), rows_of)
    return pl.pallas_call(
        close_kernel,
        grid_spec=pltpu.PrefetchScalarGridSpec(
            num_scalar_prefetch=1,
            grid=(2 * half,),
            in_specs=[row(model), row(gkv.shape[1]), whole(*qkv_w.shape), row(model)],
            out_specs=[
                pl.BlockSpec((CHUNK, model), lambda i, info: (jnp.minimum(i, half - 1), 0)),
                pl.BlockSpec((CHUNK, model), lambda i, info: (jnp.maximum(i - half, 0), 0)),
                whole(8, model),
                whole(8, model),
            ],
        ),
        out_shape=[
            jax.ShapeDtypeStruct((tokens // 2, model), f32),
            jax.ShapeDtypeStruct((tokens // 2, model), f32),
            jax.ShapeDtypeStruct((8, model), f32),
            jax.ShapeDtypeStruct((8, model), f32),
        ],
        name="close",
        **params(2 * tokens * model * gkv.shape[1], 10 * tokens * model),
    )(info, prior, gkv, qkv_w, x)


def swapped(value, axis, distance):
    size = lax.axis_size(axis)
    return lax.ppermute(value, axis, [(i, i ^ distance) for i in range(size)])


def shifted(value, axis, distance):
    size = lax.axis_size(axis)
    pairs = [(i, i + distance) for i in range(size) if 0 <= i + distance < size]
    return lax.ppermute(value, axis, pairs)


def halve(value, bit, mine):
    blocks = value.shape[0]
    split = value.reshape((blocks >> (bit + 1), 2, 1 << bit) + value.shape[1:])
    pick = lambda side: lax.dynamic_index_in_dim(split, side, 1, keepdims=False).reshape(
        (blocks // 2,) + value.shape[1:]
    )
    return pick(1 - mine), pick(mine)


def reduce_blocks(send, keep, order, low):
    index = lax.axis_index("batch") // low
    bits = list(order)
    first = True
    while bits:
        bit = bits.pop(0)
        place = sum(1 for b in [0, 1, 2] if b < bit and b in bits)
        if not first:
            send, keep = halve(keep, place, (index >> bit) & 1)
        first = False
        keep = keep + swapped(send, "batch", low << bit)
    return keep[0]


def finish(part, dim, low):
    if low == 1:
        return part
    size = lax.axis_size("batch")
    groups = [[j * low + i for i in range(low)] for j in range(size // low)]
    return lax.psum_scatter(
        part, "batch", scatter_dimension=dim, axis_index_groups=groups, tiled=True
    )


def entering(local, first_pos, tokens, start_of, size):
    span, total, k = local, None, 1
    here = start_of(first_pos + tokens - 1)
    before = start_of(first_pos - 1)
    while k < size:
        came = shifted(span, "batch", k)
        reach = first_pos - (k - 1) * tokens
        taken = jnp.where(before < reach, came, 0.0)
        total = taken if total is None else total + taken
        if 2 * k < size:
            span = span + jnp.where(here < reach, came, 0.0)
        k *= 2
    return total


def leaving(local, first_pos, tokens, start_of, size):
    span, total, k = local, None, 1
    while k < size:
        came = shifted(span, "batch", -k)
        far = start_of(first_pos + k * tokens - 1)
        taken = jnp.where(far < first_pos + tokens, came, 0.0)
        total = taken if total is None else total + taken
        if 2 * k < size:
            span = span + jnp.where(far < first_pos, came, 0.0)
        k *= 2
    return total


def per_device(
    inputs, ln_gain, ln_shift, qkv_weight, qkv_bias, out_weight, up_weight, up_bias, down_weight,
    out_bias, feature_samples, lengths, cotangent,
):
    tokens, model = inputs.shape
    head = feature_samples.shape[1]
    width = out_weight.shape[0]
    heads = width // head
    batch = lax.axis_size("batch")
    branch = lax.axis_size("branch")
    batch_pos = lax.axis_index("batch")
    branch_pos = lax.axis_index("branch")
    share = tokens // branch
    low = batch // (model // LANE)
    order = (0, 1, 2)
    block_index = batch_pos // low
    first_pos = batch_pos * tokens
    ends = jnp.cumsum(lengths, dtype=jnp.int32)

    def start_of(place):
        return jnp.max(jnp.where(place >= ends, ends, 0))

    info = jnp.concatenate(
        [
            jnp.stack(
                [
                    first_pos,
                    (block_index >> order[0]) & 1,
                    start_of(first_pos + tokens - 1),
                    branch_pos & 1,
                ]
            ).astype(jnp.int32),
            ends,
        ]
    )
    position = first_pos + jnp.arange(tokens, dtype=jnp.int32)
    begun = jnp.max(jnp.where(position[None, :] >= ends[:, None], ends[:, None], 0), axis=0)
    in_seq_place = (position - begun).astype(f32)
    frequency = 10000.0 ** (-2.0 * jnp.arange(ROT // 2, dtype=f32) / ROT)
    angles = in_seq_place[None, :] * frequency[:, None]
    circle = jnp.concatenate([jnp.cos(angles), jnp.sin(angles)], axis=0)
    level0 = lax.reduce_precision(circle, 8, 7)
    level1 = lax.reduce_precision(circle - level0, 8, 7)
    level2 = circle - level0 - level1
    cs = jnp.concatenate([level0, level1, level2], axis=0).astype(bf16)
    expand = jnp.asarray(expand_table(head), bf16)
    dct_t = jnp.asarray(dct_table(head).T)
    gain = ln_gain.reshape(1, model)
    shift = ln_shift.reshape(1, model)
    up_b = up_bias.reshape(1, -1)

    normed, hidden0, gpre0, send0, keep0, ub0, cb = feed(
        0, order[0], info, inputs, gain, shift, up_weight, up_b, down_weight, cotangent
    )
    qf, kf, value, qt, kt, ga, w_perm, basis, local_state = project(
        head, info, normed, qkv_weight, qkv_bias.reshape(1, -1), cs, expand, feature_samples,
        dct_t, cotangent, out_weight,
    )
    in_state = entering(local_state, first_pos, tokens, start_of, batch)
    hidden1, gpre1, send1, keep1, ub1 = feed(
        1, order[0], info, normed, gain, shift, up_weight, up_b, down_weight, cotangent
    )
    mixed, gq, gk, gv, back, back_total, send2, keep2, qb = attend(
        head, order[0], info, qf, kf, value, qt, ga, cs, expand, basis, in_state, normed, cotangent
    )
    out_state = leaving(back_total, first_pos, tokens, start_of, batch)
    branch_part = outward(hidden0, hidden1, mixed, down_weight, out_weight)
    branch_sum = lax.psum_scatter(branch_part, "branch", scatter_dimension=0, tiled=True)
    prior = inward(gpre0, gpre1, gq, up_weight, w_perm)
    gkv, send3, keep3, kvb = keys(
        head, order[0], info, kf, value, kt, gk, gv, back, cs, expand, basis, out_state, normed
    )
    far, near, gain_part, shift_part = close(info, prior, gkv, w_perm, inputs, branch)

    pair = near + swapped(far, "branch", 1)
    pair = pair.reshape(branch // 2, share, model)
    step = 1
    while step < branch // 2:
        side = (branch_pos >> 1) // step & 1
        other, pair = halve(pair, 0, side)
        pair = pair + swapped(other, "branch", 2 * step)
        step *= 2
    grad_normed = pair.reshape(share, model)

    piece0 = reduce_blocks(send0, keep0, order, low)
    piece1 = reduce_blocks(send1, keep1, order, low)
    piece2 = reduce_blocks(send2, keep2, order, low)
    piece3 = reduce_blocks(send3, keep3, order, low)
    half = hidden0.shape[1]

    def columns(rows):
        count = rows.shape[0] // LANE
        return rows.reshape(count, LANE, LANE).transpose(1, 0, 2).reshape(LANE, count * LANE)

    down_sum = finish(jnp.concatenate([piece0[:half], piece1[:half]], axis=0), 1, low)
    up_sum = finish(jnp.concatenate([columns(piece0[half:]), columns(piece1[half:])], axis=1), 0, low)
    out_sum = finish(piece2[:width], 1, low)

    def by_head(parts):
        rows = parts[0].shape[0]
        stacked = jnp.stack([p.reshape(rows, heads, head) for p in parts], axis=2)
        return stacked.reshape(rows, 3 * width)

    kv_columns = columns(piece3)
    qkv_sum = finish(
        by_head([columns(piece2[width:]), kv_columns[:, :width], kv_columns[:, width:]]), 0, low
    )

    cot_part = jnp.sum(cb, axis=0) * jnp.where(branch_pos == 0, 1.0, 0.0)
    kv_part = jnp.sum(kvb, axis=0)[None]
    qkv_part = by_head([jnp.sum(qb, axis=0)[None], kv_part[:, :width], kv_part[:, width:]])[0]
    up_part = jnp.concatenate([jnp.sum(ub0, axis=0), jnp.sum(ub1, axis=0)])

    def spread(part):
        return lax.dynamic_update_slice_in_dim(
            jnp.zeros((part.shape[0] * branch,), f32), part, branch_pos * part.shape[0], 0
        )

    small = jnp.concatenate(
        [jnp.sum(gain_part, axis=0), jnp.sum(shift_part, axis=0), cot_part, spread(qkv_part), spread(up_part)]
    ).reshape(-1, LANE)
    for axis, size in (("branch", branch), ("batch", batch)):
        step = 1
        while step < size:
            small = small + swapped(small, axis, step)
            step *= 2
    small = small.reshape(-1)
    cuts = np.cumsum([model, model, model, 3 * width * branch])
    gain_grad, shift_grad, out_bias_grad, qkv_bias_grad, up_bias_grad = jnp.split(small, cuts)

    row_start = branch_pos * share
    own_inputs = lax.dynamic_slice_in_dim(inputs, row_start, share, 0).astype(f32)
    own_cot = lax.dynamic_slice_in_dim(cotangent, row_start, share, 0).astype(f32)
    output = (own_inputs + branch_sum + out_bias).astype(bf16)
    centered = own_inputs - jnp.mean(own_inputs, axis=1, keepdims=True)
    own_inv = lax.rsqrt(jnp.mean(centered * centered, axis=1, keepdims=True) + epsilon)
    own_unit = centered * own_inv
    grad_unit = grad_normed * ln_gain
    input_grad = (
        own_inv
        * (
            grad_unit
            - jnp.mean(grad_unit, axis=1, keepdims=True)
            - own_unit * jnp.mean(grad_unit * own_unit, axis=1, keepdims=True)
        )
        + own_cot
    )
    return (
        output,
        input_grad,
        gain_grad,
        shift_grad,
        qkv_sum,
        qkv_bias_grad,
        out_sum,
        up_sum,
        up_bias_grad,
        down_sum,
        out_bias_grad,
    )


def solution(mesh):
    placed = (
        P("batch", None),
        P(),
        P(),
        P(None, "branch"),
        P("branch"),
        P("branch", None),
        P(None, "branch"),
        P("branch"),
        P("branch", None),
        P(),
        P(),
        P(),
        P("batch", None),
    )
    return jax.shard_map(
        per_device,
        mesh=mesh,
        in_specs=placed,
        out_specs=(
            P(("batch", "branch"), None),
            P(("batch", "branch"), None),
            P(),
            P(),
            P("batch", "branch"),
            P(),
            P("branch", "batch"),
            P("batch", "branch"),
            P(),
            P("branch", "batch"),
            P(),
        ),
        check_vma=False,
    )
```

```python
import math

import numpy as np

import jax
import jax.numpy as jnp
from jax import lax
from jax.experimental import pallas as pl
from jax.experimental.pallas import tpu as pltpu
from jax.sharding import PartitionSpec as P

ROT = 16
CHUNK = 256
ROWS = 512
LANE = 128
epsilon = 1e-05
f32 = jnp.float32
bf16 = jnp.bfloat16
HALF_ROOT = math.sqrt(0.5)
GAUSS = 1.0 / math.sqrt(2.0 * math.pi)
VMEM_BYTES = 64 * 2**20
LONG = 2**40
SHORT = 2**35
PARTS = ((3, 1), (0, 3))


def nn(a, b):
    return lax.dot_general(a, b, (((1,), (0,)), ((), ())), preferred_element_type=f32)


def nt(a, b):
    return lax.dot_general(a, b, (((1,), (1,)), ((), ())), preferred_element_type=f32)


def tn(a, b):
    return lax.dot_general(a, b, (((0,), (0,)), ((), ())), preferred_element_type=f32)


def two(value):
    high = value.astype(bf16)
    return high, (value - high.astype(f32)).astype(bf16)


def exact3(dot, a, b):
    return dot(a[0], b[0]) + (dot(a[1], b[0]) + dot(a[0], b[1]))


def beside(*parts):
    return jnp.concatenate(parts, axis=1)


def below(*parts):
    return jnp.concatenate(parts, axis=0)


class Order:
    def __init__(self):
        self.last = ()

    def __call__(
        self, body, args, in_specs, out_specs, out_shape, after=(), through=(), flops=0, **rest
    ):
        given, results = len(args), len(out_shape)
        skipped = [*self.last, *after, *through]

        def without(*refs):
            outs = refs[given + len(skipped) :]
            body(*refs[:given], *outs[:results], *outs[results + len(through) :])

        place = pl.BlockSpec(memory_space=pl.ANY)
        first = given + len(skipped) - len(through)
        outs = pl.pallas_call(
            without,
            in_specs=[*in_specs, *[place] * len(skipped)],
            out_specs=[*out_specs, *[place] * len(through)],
            out_shape=[*out_shape, *[shaped(t.shape, t.dtype) for t in through]],
            input_output_aliases={first + i: results + i for i in range(len(through))},
            compiler_params=pltpu.CompilerParams(vmem_limit_bytes=VMEM_BYTES),
            cost_estimate=pl.CostEstimate(flops=flops, bytes_accessed=0, transcendentals=0),
            **rest,
        )(*args, *skipped)
        self.last = (outs[0],)
        return outs


def hold(call, arrays, after=()):
    def body(out):
        out[...] = jnp.zeros_like(out)

    return call(body, (), [], [whole(8, LANE)], [shaped((8, LANE))], after, arrays, grid=(1,), name="hold")[1:]


def shaped(shape, dtype=f32):
    return jax.ShapeDtypeStruct(tuple(shape), dtype)


def whole(*shape):
    return pl.BlockSpec(shape, lambda *ids: (0,) * len(shape))


def rows_at(rows, width):
    return pl.BlockSpec((rows, width), lambda i: (i, 0))


SMEM = pl.BlockSpec(memory_space=pltpu.SMEM)


def dct_table(size):
    row = np.arange(size)[:, None]
    col = np.arange(size)[None, :]
    table = np.cos(math.pi * (col + 0.5) * row / size) * math.sqrt(2.0 / size)
    table[0] *= math.sqrt(0.5)
    return table.astype(np.float32)


def expand_table(head):
    half = ROT // 2
    table = np.zeros((ROT, 3 * LANE), np.float32)
    for lane in range(LANE):
        place = lane % head
        if place < half:
            table[place, lane] = 1.0
            table[half + place, LANE + lane] = -1.0
        elif place < ROT:
            table[place - half, lane] = 1.0
            table[place, 2 * LANE + lane] = 1.0
    return np.concatenate([table] * 3, axis=0)


def ends_of(lengths):
    ends, total = [], jnp.int32(0)
    for j in range(lengths.shape[0]):
        total = total + lengths[j]
        ends.append(total)
    return ends


def seq_start(ends, place):
    start = jnp.zeros_like(place)
    for end in ends:
        start = jnp.where(place >= end, end, start)
    return start


def iota(shape, dim):
    return lax.broadcasted_iota(jnp.int32, shape, dim)


def head_block(head, rows, cols):
    return iota((rows, cols), 0) // head == iota((rows, cols), 1) // head


def turn_tables(cs, expand, head, width):
    wide = tn(cs, expand)
    lane = iota((1, LANE), 1) % head
    cosine = wide[:, :LANE] + jnp.where(lane < ROT, 0.0, 1.0)
    times = width // LANE
    return tuple(
        beside(*[part] * times) for part in (cosine, wide[:, LANE : 2 * LANE], wide[:, 2 * LANE :])
    )


def turn(value, tables, sign):
    cosine, up, down = tables
    width = value.shape[1]
    half = ROT // 2
    moved = pltpu.roll(value, width - half, 1) * up + pltpu.roll(value, half, 1) * down
    return value * cosine + moved if sign > 0 else value * cosine - moved


def fold_state(full, head, width):
    block = head_block(head, width, width)
    s_part = jnp.where(block, full[:, :width], 0.0)
    n_part = jnp.where(block, full[:, width:], 0.0)
    s_fold = sum(s_part[:, i * LANE : (i + 1) * LANE] for i in range(width // LANE))
    n_fold = sum(n_part[:, i * LANE : (i + 1) * LANE] for i in range(width // LANE))
    return s_fold + pltpu.roll(n_fold, LANE // 2, 1)


def unfold_state(packed, head, width):
    block = head_block(head, width, width)
    times = width // LANE
    s_part = beside(*[packed] * times)
    n_part = beside(*[pltpu.roll(packed, LANE // 2, 1)] * times)
    return beside(jnp.where(block, s_part, 0.0), jnp.where(block, n_part, 0.0))


def deal(outs, order, low, write):
    mine = lax.axis_index("batch") // low
    first, second, third = (1 << bit for bit in order)
    wanted = [base + i * third for base in (first + second, first, second, 0) for i in range(2)]
    slots = [(out, i) for out in outs for i in range(out.shape[0])]
    for (out, i), block in zip(slots, wanted):
        write(out, i, pl.multiple_of((mine ^ block) * LANE, LANE))


def feed_step(normed, c, up_w, up_b, down_w, hidden_o, gpre_o, ub_o, down_acc, up_acc):
    rows, width = hidden_o.shape
    pre = nn(normed, up_w[...]) + up_b[...]
    grad_hidden = nt(c, down_w[...])
    phi = 0.5 + 0.5 * lax.erf(pre * HALF_ROOT)
    hidden = (pre * phi).astype(bf16)
    hidden_o[...] = hidden
    down_acc[...] += tn(hidden, c)
    slope = phi + pre * jnp.exp(-0.5 * pre * pre) * GAUSS
    gpre = (grad_hidden * slope).astype(bf16)
    gpre_o[...] = gpre
    up_acc[...] += tn(normed, gpre)
    ub_o[...] += jnp.sum(gpre.astype(f32).reshape(rows // 8, 8, width), axis=0)


def clear(*refs):
    for ref in refs:
        ref[...] = jnp.zeros_like(ref)


def write_down(out, i, at, down_acc):
    out[i, : down_acc.shape[0], :] = down_acc[:, pl.ds(at, LANE)]


def write_up(out, i, at, up_acc):
    width = up_acc.shape[1]
    first = out.shape[1] - width
    for j in range(0, width, LANE):
        out[i, first + j : first + j + LANE, :] = up_acc[pl.ds(at, LANE), j : j + LANE]


def feed_specs(tokens, model, units, part):
    first, quarters = PARTS[part]
    width = units // 4 * quarters
    part = first // quarters
    ins = [
        pl.BlockSpec((model, width), lambda i: (0, part)),
        pl.BlockSpec((1, width), lambda i: (0, part)),
        pl.BlockSpec((width, model), lambda i: (part, 0)),
        rows_at(ROWS, model),
    ]
    outs = [rows_at(ROWS, width)] * 2 + [whole(8, width)]
    shapes = [shaped((tokens, width), bf16)] * 2 + [shaped((8, width))]
    scratch = [pltpu.VMEM((width, model), f32), pltpu.VMEM((model, width), f32)]
    return width, ins, outs, shapes, scratch


def feed(call, orders, low, normed, up_w, up_b, down_w, cot, **rest):
    tokens, model = cot.shape
    width, ins, outs, shapes, scratch = feed_specs(tokens, model, up_w.shape[1], 1)
    firsts, piece = shaped((4, width, LANE)), shaped((2, width, LANE))
    pieces_out = [firsts, piece, piece] * 2

    def body(normed, up_w, up_b, down_w, cot, hidden_o, gpre_o, ub_o, *refs):
        *pieces, down_acc, up_acc = refs
        step = pl.program_id(0)

        @pl.when(step == 0)
        def _():
            clear(down_acc, up_acc, ub_o)

        feed_step(
            normed[...], cot[...], up_w, up_b, down_w, hidden_o, gpre_o, ub_o, down_acc, up_acc
        )

        @pl.when(step == pl.num_programs(0) - 1)
        def _():
            deal(pieces[:3], orders[0], low, lambda *at: write_down(*at, down_acc))
            deal(pieces[3:], orders[1], low, lambda *at: write_up(*at, up_acc))

    return call(
        body,
        (normed, up_w, up_b, down_w, cot),
        [rows_at(ROWS, model), *ins],
        outs + [whole(*a.shape) for a in pieces_out],
        shapes + pieces_out,
        **rest,
        grid=(tokens // ROWS,),
        scratch_shapes=scratch,
        name="feed_forward",
    )


def take_columns(w_in, head, heads, part):
    return beside(*[w_in[:, (3 * h + part) * head : (3 * h + part + 1) * head] for h in range(heads)])


def features(part, tables, basis, head, feats):
    width = part.shape[1]
    turned = turn(part.astype(f32), tables, 1)
    square = two(turned * turned)
    ones = jnp.where(head_block(head, width, width), 1.0 / (2.0 * math.sqrt(head)), 0.0).astype(bf16)
    argument = exact3(nn, two(turned), basis) - (nn(square[0], ones) + nn(square[1], ones))
    return turned.astype(bf16), (jnp.exp(argument) * (1.0 / math.sqrt(feats))).astype(bf16)


def rotary_table(ends, first_pos, rows, tokens, out):
    half = ROT // 2
    order = iota((half, rows), 0)
    frequency = jnp.zeros((half, rows), f32)
    for j in range(half):
        value = float(np.float32(10000.0) ** np.float32(-2.0 * j / ROT))
        frequency = jnp.where(order == j, value, frequency)
    for i in range(tokens // rows):
        place = first_pos + i * rows + iota((half, rows), 1)
        angle = (place - seq_start(ends, place)).astype(f32) * frequency
        circle = below(jnp.cos(angle), jnp.sin(angle))
        high, rest = two(circle)
        middle, lowest = two(circle - high.astype(f32))
        out[i] = below(high, middle, lowest)


def front(
    call, head, lengths, x, gain, shift, up_w, up_b, down_w, cot, qkv_w, qkv_b, expand,
    samples, dct_t,
):
    tokens, model = x.shape
    width = qkv_w.shape[1] // 3
    heads = width // head
    feats = samples.shape[0]
    blocks = tokens // ROWS
    table = (blocks, expand.shape[0], ROWS)
    part, ins, outs, shapes, scratch = feed_specs(tokens, model, up_w.shape[1], 0)
    piece = shaped((model // LANE, 2 * part, LANE))

    def body(
        lengths, x, gain, shift, up_w, up_b, down_w, cot, qkv_w, qkv_b, expand, samples, dct_t,
        normed_o, cb_o, kf_o, v_o, kt_o, w_o, basis_o, cs_o, state_o, hidden_o, gpre_o, ub_o, piece_o,
        down_acc, up_acc, w_s, b_s, basis_s, cs_s, state_s,
    ):
        step = pl.program_id(0)
        ends = ends_of(lengths)
        first_pos = lax.axis_index("batch") * tokens
        start_last = seq_start(ends, first_pos + tokens - 1)

        @pl.when(step == 0)
        def _():
            clear(down_acc, up_acc, ub_o, cb_o, state_s)
            for part in (1, 2):
                to = slice((part - 1) * width, part * width)
                w_s[:, to] = take_columns(qkv_w, head, heads, part)
                b_s[:, to] = take_columns(qkv_b, head, heads, part)
            basis = lax.dot_general(
                dct_t[...], samples[...], (((1,), (1,)), ((), ())),
                preferred_element_type=f32, precision=lax.Precision.HIGHEST,
            )
            basis = basis * (1.0 / head**0.25)
            wide = below(*[beside(*[basis] * heads)] * heads)
            basis_s[...] = jnp.where(head_block(head, width, width), wide, 0.0)
            basis_o[...] = basis_s[...]
            w_o[...] = w_s[...]
            rotary_table(ends, first_pos, ROWS, tokens, cs_s)
            cs_o[...] = cs_s[...]

        xf = x[...].astype(f32)
        centered = xf - jnp.mean(xf, axis=1, keepdims=True)
        inv = lax.rsqrt(jnp.mean(centered * centered, axis=1, keepdims=True) + epsilon)
        normed = (centered * inv * gain[...] + shift[...]).astype(bf16)
        normed_o[...] = normed
        c = cot[...]
        cb_o[...] += jnp.sum(c.astype(f32).reshape(ROWS // 8, 8, model), axis=0)
        feed_step(normed, c, up_w, up_b, down_w, hidden_o, gpre_o, ub_o, down_acc, up_acc)

        projected = (nn(normed, w_s[...]) + b_s[...]).astype(bf16)
        tables = turn_tables(cs_s[step], expand[...], head, width)
        k_turn, k_feat = features(projected[:, :width], tables, two(basis_s[...]), head, feats)
        value = projected[:, width:]
        kf_o[...], v_o[...], kt_o[...] = k_feat, value, k_turn
        place = first_pos + step * ROWS + iota((ROWS, 1), 0)
        tail = jnp.where(place >= start_last, 1.0, 0.0).astype(bf16)
        state_s[...] += tn(k_feat * tail, beside(value, jnp.ones_like(value)))

        @pl.when(step == pl.num_programs(0) - 1)
        def _():
            state_o[...] = fold_state(state_s[...], head, width)
            for i in range(piece.shape[0]):
                write_down(piece_o, i, i * LANE, down_acc)
                write_up(piece_o, i, i * LANE, up_acc)

    narrow = shaped((tokens, width), bf16)
    return call(
        body,
        (lengths, x, gain, shift, up_w, up_b, down_w, cot, qkv_w, qkv_b, expand, samples, dct_t),
        [SMEM, rows_at(ROWS, model), whole(1, model), whole(1, model), *ins]
        + [whole(*a.shape) for a in (qkv_w, qkv_b, expand, samples, dct_t)],
        [rows_at(ROWS, model), whole(8, model), *[rows_at(ROWS, width)] * 3]
        + [whole(model, 2 * width), whole(width, width), whole(*table), whole(width, LANE), *outs]
        + [whole(*piece.shape)],
        [shaped((tokens, model), bf16), shaped((8, model)), *[narrow] * 3]
        + [shaped((model, 2 * width), bf16), shaped((width, width)), shaped(table, bf16)]
        + [shaped((width, LANE)), *shapes, piece],
        grid=(blocks,),
        scratch_shapes=[
            *scratch,
            pltpu.VMEM((model, 2 * width), bf16),
            pltpu.VMEM((1, 2 * width), f32),
            pltpu.VMEM((width, width), f32),
            pltpu.VMEM(table, bf16),
            pltpu.VMEM((width, 2 * width), f32),
        ],
        name="front",
    )


def project_queries_kernel(
    head, feats, normed, w_in, b_in, expand, basis, cs, cot, out_w, qf_o, qt_o, ga_o, w_o, w_s, b_s
):
    width = out_w.shape[0]
    heads = width // head

    @pl.when(pl.program_id(0) == 0)
    def _():
        w_s[...] = take_columns(w_in, head, heads, 0)
        b_s[...] = take_columns(b_in, head, heads, 0)
        w_o[...] = w_s[...]

    projected = (nn(normed[...], w_s[...]) + b_s[...]).astype(bf16)
    ga_o[...] = nt(cot[...], out_w[...])
    tables = turn_tables(cs[0], expand[...], head, width)
    qt_o[...], qf_o[...] = features(projected, tables, two(basis[...]), head, feats)


def project_queries(call, head, feats, normed, w_in, b_in, expand, basis, cs, cot, out_w):
    tokens, model = normed.shape
    width = out_w.shape[0]

    def body(*refs):
        project_queries_kernel(head, feats, *refs)

    return call(
        body,
        (normed, w_in, b_in, expand, basis, cs, cot, out_w),
        [
            rows_at(ROWS, model),
            whole(*w_in.shape),
            whole(*b_in.shape),
            whole(*expand.shape),
            whole(*basis.shape),
            pl.BlockSpec((1,) + cs.shape[1:], lambda i: (i, 0, 0)),
            rows_at(ROWS, model),
            whole(*out_w.shape),
        ],
        [rows_at(ROWS, width)] * 3 + [whole(model, width)],
        [
            shaped((tokens, width), bf16),
            shaped((tokens, width), bf16),
            shaped((tokens, width)),
            shaped((model, width), bf16),
        ],
        grid=(tokens // ROWS,),
        scratch_shapes=[pltpu.VMEM((model, width), bf16), pltpu.VMEM((1, width), f32)],
        name="project_queries",
    )


def swapped(value, axis, distance):
    size = lax.axis_size(axis)
    return lax.ppermute(value, axis, [(i, i ^ distance) for i in range(size)])


def joined(forward, lengths, tokens, base, entered, own, came):
    ends = ends_of(lengths)
    here = lax.axis_index("batch")
    count, size = 1, 2
    group = (here >> (base + count)) << (base + count)
    mine = (here >> base) & (size - 1)
    group_end = (group + (size << base)) * tokens
    total = jnp.zeros_like(own)
    entered = total if entered is None else entered
    for m in range(size):
        part = came if m else own
        other = mine ^ m
        if forward:
            edge = (group + ((other + 1) << base)) * tokens
            enters = (other < mine) & (seq_start(ends, here * tokens - 1) < edge)
            counts = seq_start(ends, group_end - 1) < edge
        else:
            start = seq_start(ends, (group + (other << base)) * tokens - 1)
            enters = (other > mine) & (start < (here + 1) * tokens)
            counts = start < group * tokens
        if m:
            entered = entered + jnp.where(enters, part, 0.0)
        total = total + jnp.where(counts, part, 0.0)
    return entered, total


def join_states(call, forward, tokens, base, lengths, entered, own, came, **rest):
    given = [own, came] if entered is None else [entered, own, came]

    def body(lengths, *refs):
        *ins, entered_o, total_o = refs
        values = [r[...] for r in ins]
        if entered is None:
            values = [None, *values]
        entered_o[...], total_o[...] = joined(
            forward, lengths, tokens, base, *values
        )

    spec = whole(*own.shape)
    return call(
        body,
        (lengths, *given),
        [SMEM] + [spec] * len(given),
        [spec, spec],
        [shaped(own.shape)] * 2,
        **rest,
        grid=(1,),
        name="join_states",
    )


def turned_grad(grad_feat, feat, turned, basis, tables, head, width):
    weighted = two(grad_feat * feat.astype(f32))
    ones = jnp.where(head_block(head, width, width), 1.0 / math.sqrt(head), 0.0).astype(bf16)
    total = nn(weighted[0], ones) + nn(weighted[1], ones)
    grad = exact3(nt, weighted, basis) - total * turned.astype(f32)
    return turn(grad, tables, -1).astype(bf16)


def attend_kernel(
    head, order, low, tokens, per_step, base, lengths, qf, kf, v, qt, ga, cs, expand, basis_i,
    normed, cot, hidden0, hidden1, down_w, out_w, entered_i, own_i, came_i,
    gq_o, gk_o, gv_o, back_o, total_o, qb_o, send_o, keep_o, *refs,
):
    *piece, state_s, q_acc, o_acc, total_s = refs
    step = pl.program_id(0)
    width = qf.shape[1]
    heads = width // head
    ends = ends_of(lengths)
    first_pos = lax.axis_index("batch") * tokens

    @pl.when(step == 0)
    def _():
        entered, _ = joined(
            True, lengths, tokens, base, entered_i[...], own_i[...], came_i[...]
        )
        state_s[...] = unfold_state(entered, head, width)
        q_acc[...] = jnp.zeros_like(q_acc)
        o_acc[...] = jnp.zeros_like(o_acc)
        total_s[...] = jnp.zeros_like(total_s)
        qb_o[...] = jnp.zeros_like(qb_o)

    basis = two(basis_i[...])
    block = head_block(head, width, width)
    both = beside(block, block)
    ones = jnp.where(block, 1.0, 0.0).astype(bf16)
    lanes = [jnp.where(iota((1, width), 1) // head == h, 1.0, 0.0).astype(bf16) for h in range(heads)]
    state = state_s[...]
    total = total_s[...]
    part = hidden0.shape[1]
    outward = nn(hidden1[...], down_w[:-part]) + nn(hidden0[...], down_w[-part:])
    mixes = []
    for sub in range(per_step):
        at = slice(sub * CHUNK, (sub + 1) * CHUNK)
        begin = first_pos + (step * per_step + sub) * CHUNK
        last = seq_start(ends, begin + CHUNK - 1)
        row = iota((CHUNK, 1), 0)
        start = seq_start(ends, begin + row)
        col = iota((CHUNK, CHUNK), 1)
        window = (col <= iota((CHUNK, CHUNK), 0)) & (col + begin >= start)
        carried = jnp.where(start < begin, 1.0, 0.0)
        q, k, value = qf[at, :], kf[at, :], v[at, :]
        q_carried = q * carried.astype(bf16)
        state_two = two(state)
        scores = [jnp.where(window, nt(q * lanes[h], k), 0.0).astype(bf16) for h in range(heads)]
        right = [beside(value * lane, jnp.broadcast_to(lane, value.shape)) for lane in lanes]
        sums = nn(beside(*scores, q_carried, q_carried), below(*right, *state_two))
        over = 1.0 / sums[:, width:]
        attended = sums[:, :width] * over
        mixed = attended.astype(bf16)
        mixes.append(mixed)
        grad_att = ga[at, :]
        g_num = grad_att * over
        product = two(grad_att * attended)
        g_den = -nn(beside(*product), below(ones, ones)) * over
        g_low = g_num.astype(bf16)
        g_both = two(beside(g_num, g_den * (1.0 / head)))
        from_state = nt(
            beside(g_both[0], g_both[0], g_both[1]), beside(state_two[0], state_two[1], state_two[0])
        )
        g_heads = [g_low * lane for lane in lanes]
        mixing = [
            jnp.where(window, nt(g_heads[h], value) + g_den[:, h * head : h * head + 1], 0.0).astype(bf16)
            for h in range(heads)
        ]
        grad_fq = carried * from_state + nn(beside(*mixing), below(*[k * lane for lane in lanes]))
        gk_o[at, :] = tn(below(*mixing), below(*[q * lane for lane in lanes]))
        gv_o[at, :] = tn(below(*scores), below(*g_heads))
        back = tn(q_carried, beside(g_num, g_den).astype(bf16))
        back_o[sub] = fold_state(back, head, width)
        live = jnp.where(seq_start(ends, begin - 1) < first_pos, 1.0, 0.0)
        total = total + live * back
        tail = jnp.where(begin + row >= last, 1.0, 0.0).astype(bf16)
        retain = jnp.where(last < begin, 1.0, 0.0)
        added = tn(k * tail, beside(value, jnp.ones_like(value)))
        state = retain * state + jnp.where(both, added, 0.0)
        tables = turn_tables(cs[0, :, at], expand[...], head, width)
        gq = turned_grad(grad_fq, q, qt[at, :], basis, tables, head, width)
        gq_o[at, :] = gq
        qb_o[...] += jnp.sum(gq.astype(f32).reshape(CHUNK // 8, 8, width), axis=0)
        q_acc[...] += tn(normed[at, :], gq)
        o_acc[...] += tn(mixed, cot[at, :])
    state_s[...] = state
    total_s[...] = total
    outward = outward + nn(below(*mixes), out_w[...])
    by_core(step & 1, send_o, keep_o, outward)

    @pl.when(step == pl.num_programs(0) - 1)
    def _():
        total_o[...] = fold_state(total, head, width)

        def write(out, i, spot):
            out[i, :width, :] = o_acc[:, pl.ds(spot, LANE)]
            for j in range(width // LANE):
                out[i, width + j * LANE : width + (j + 1) * LANE, :] = q_acc[
                    pl.ds(spot, LANE), j * LANE : (j + 1) * LANE
                ]

        deal(piece, order, low, write)


def by_core(core, send, keep, value):
    mine = lax.axis_index("branch") & 1

    @pl.when(core != mine)
    def _():
        send[0] = value

    @pl.when(core == mine)
    def _():
        keep[0] = value


def attend(
    call, head, order, low, base, lengths, qf, kf, v, qt, ga, cs, expand, basis, normed, cot,
    hidden0, hidden1, down_w, out_w, entered, own, came, **rest,
):
    tokens, width = qf.shape
    model = cot.shape[1]
    per_step = ROWS // CHUNK
    chunks = tokens // CHUNK
    part = hidden0.shape[1]
    firsts, piece = shaped((4, 2 * width, LANE)), shaped((2, 2 * width, LANE))
    chip = pl.BlockSpec((1, ROWS, model), lambda i: (i >> 1, 0, 0))
    row = rows_at(ROWS, width)
    packed = whole(width, LANE)

    def body(*refs):
        attend_kernel(head, order, low, tokens, per_step, base, *refs)

    return call(
        body,
        (lengths, qf, kf, v, qt, ga, cs, expand, basis, normed, cot, hidden0, hidden1, down_w, out_w)
        + (entered, own, came),
        [
            SMEM,
            *[row] * 5,
            pl.BlockSpec((1,) + cs.shape[1:], lambda i: (i, 0, 0)),
            whole(*expand.shape),
            whole(width, width),
            rows_at(ROWS, model),
            rows_at(ROWS, model),
            rows_at(ROWS, part),
            rows_at(ROWS, hidden1.shape[1]),
            whole(*down_w.shape),
            whole(*out_w.shape),
            *[packed] * 3,
        ],
        [
            *[row] * 3,
            pl.BlockSpec((per_step, width, LANE), lambda i: (i, 0, 0)),
            packed,
            whole(8, width),
            chip,
            chip,
            *[whole(*a.shape) for a in (firsts, piece, piece)],
        ],
        [
            shaped((tokens, width), bf16),
            shaped((tokens, width)),
            shaped((tokens, width)),
            shaped((chunks, width, LANE)),
            shaped((width, LANE)),
            shaped((8, width)),
            *[shaped((tokens // ROWS // 2, ROWS, model))] * 2,
            firsts,
            piece,
            piece,
        ],
        **rest,
        grid=(tokens // ROWS,),
        scratch_shapes=[
            pltpu.VMEM((width, 2 * width), f32),
            pltpu.VMEM((model, width), f32),
            pltpu.VMEM((width, model), f32),
            pltpu.VMEM((width, 2 * width), f32),
        ],
        name="attend",
        flops=LONG,
    )


def branch_place():
    here = lax.axis_index("branch")
    return here & 1, here >> 1


def share_at(i):
    core, chip = branch_place()
    return 2 * jnp.where(i < 2, 1 - chip, chip) + jnp.where(i & 1, core, 1 - core)


def backward(
    call, head, order, low, base, lengths, kf, v, kt, gk, gv, back, cs, expand, basis, normed, x,
    gpre0, gpre1, gq, up_w, q_w, kv_w, entered, own, came, **rest,
):
    tokens, width = kf.shape
    model = normed.shape[1]
    part = gpre0.shape[1]
    chunks, per_step = tokens // CHUNK, ROWS // CHUNK
    row = lambda n: pl.BlockSpec((ROWS, n), lambda i: (share_at(i), 0))
    packed = whole(width, LANE)
    firsts, piece = shaped((4, 2 * width, LANE)), shaped((2, 2 * width, LANE))
    acc_shape = (model, 2 * width)

    def body(
        lengths, kf, v, kt, gk, gv, back, cs, expand, basis_i, normed, x, gpre0, gpre1, gq, up_w,
        q_w, kv_w, entered_i, own_i, came_i, keep_o, far0_o, far1_o, near_o, kvb_o, gain_o, shift_o,
        *refs,
    ):
        *pieces, acc, state_s = refs
        step = pl.program_id(0)
        ends = ends_of(lengths)
        first_pos = lax.axis_index("batch") * tokens

        @pl.when(step == 0)
        def _():
            clear(kvb_o, gain_o, shift_o, acc)
            state, _ = joined(
                False, lengths, tokens, base, entered_i[...], own_i[...], came_i[...]
            )
            for chunk in reversed(range(chunks)):
                state_s[chunk] = state
                begin = first_pos + chunk * CHUNK
                last = seq_start(ends, begin + CHUNK - 1)
                state = back[chunk] + jnp.where(last < begin, state, 0.0)

        grad = nt(gpre1[...], up_w[:, :-part]) + nt(gpre0[...], up_w[:, -part:])
        basis = two(basis_i[...])
        tables = turn_tables(cs[0], expand[...], head, width)
        grads = []
        for sub in range(per_step):
            here = slice(sub * CHUNK, (sub + 1) * CHUNK)
            chunk = share_at(step) * per_step + sub
            begin = first_pos + chunk * CHUNK
            last = seq_start(ends, begin + CHUNK - 1)
            tail = jnp.where(begin + iota((CHUNK, 1), 0) >= last, 1.0, 0.0)
            k, value = kf[here, :], v[here, :]
            state = two(unfold_state(state_s[chunk], head, width))
            right = beside(value, jnp.full(value.shape, 1.0 / head, bf16))
            grad_fk = gk[here, :] + tail * nt(beside(right, right), beside(*state))
            grad_v = gv[here, :] + tail * nn(
                beside(k, k), below(state[0][:, :width], state[1][:, :width])
            )
            turned = tuple(t[here, :] for t in tables)
            grad_k = turned_grad(grad_fk, k, kt[here, :], basis, turned, head, width)
            grads.append(beside(grad_k, grad_v.astype(bf16)))
        both = below(*grads)
        kvb_o[...] += jnp.sum(both.astype(f32).reshape(ROWS // 8, 8, 2 * width), axis=0)
        grad = grad + nt(beside(gq[...], both), beside(q_w[...], kv_w[...]))
        acc[...] += tn(normed[...], both)

        @pl.when(step == 0)
        def _():
            far0_o[...] = grad[: ROWS // 2]
            far1_o[...] = grad[ROWS // 2 :]

        @pl.when(step == 2)
        def _():
            near_o[...] = grad

        @pl.when(step & 1 == 1)
        def _():
            keep_o[0] = grad

        xf = x[...].astype(f32)
        centered = xf - jnp.mean(xf, axis=1, keepdims=True)
        unit = centered * lax.rsqrt(jnp.mean(centered * centered, axis=1, keepdims=True) + epsilon)
        gain_o[...] += jnp.sum((grad * unit).reshape(ROWS // 8, 8, model), axis=0)
        shift_o[...] += jnp.sum(grad.reshape(ROWS // 8, 8, model), axis=0)

        @pl.when(step == pl.num_programs(0) - 1)
        def _():
            deal(pieces, order, low, lambda *spot: write_up(*spot, acc))

    chip = pl.BlockSpec((1, ROWS, model), lambda i: (i >> 1, 0, 0))
    sums = [shaped((8, 2 * width)), shaped((8, model)), shaped((8, model))]
    pieces = [firsts, piece, piece]
    sent = [shaped((ROWS // 2, model)), shaped((ROWS // 2, model)), shaped((ROWS, model))]
    return call(
        body,
        (lengths, kf, v, kt, gk, gv, back, cs, expand, basis, normed, x, gpre0, gpre1, gq, up_w)
        + (q_w, kv_w, entered, own, came),
        [SMEM, *[row(width)] * 5, whole(*back.shape)]
        + [pl.BlockSpec((1,) + cs.shape[1:], lambda i: (share_at(i), 0, 0)), whole(*expand.shape)]
        + [whole(width, width), row(model), row(model), row(part), row(gpre1.shape[1]), row(width)]
        + [whole(*up_w.shape), whole(*q_w.shape), whole(*kv_w.shape), *[packed] * 3],
        [chip] + [whole(*a.shape) for a in (*sent, *sums, *pieces)],
        [shaped((tokens // ROWS // 2, ROWS, model)), *sent, *sums, *pieces],
        **rest,
        grid=(tokens // ROWS,),
        scratch_shapes=[pltpu.VMEM(acc_shape, f32), pltpu.VMEM((chunks, width, LANE), f32)],
        flops=LONG,
        name="backward",
    )


def finish_small(call, one, other, sizes):
    shapes = [shaped((size // LANE, LANE)) for size in sizes]

    def body(one, other, *outs):
        row = 0
        for out in outs:
            out[...] = one[row : row + out.shape[0], :] + other[row : row + out.shape[0], :]
            row += out.shape[0]

    parts = call(
        body,
        (one, other),
        [whole(*one.shape)] * 2,
        [whole(*a.shape) for a in shapes],
        shapes,
        grid=(1,),
        name="finish_small",
    )
    return [part.reshape(-1) for part in parts]


def block_of(array, count, at):
    shape = (count,) + array.shape[1:]
    return pl.BlockSpec(shape, lambda i: (at() if callable(at) else at,) + (0,) * (len(shape) - 1))


def sums_of(call, *jobs, **rest):
    arrays, specs, outs, shapes = [], [], [], []
    for job in jobs:
        for array, count, at in job:
            arrays.append(array)
            specs.append(block_of(array, count, at))
        shapes.append(shaped((count,) + array.shape[1:]))
        outs.append(whole(*shapes[-1].shape))

    def body(*refs):
        ins, results = refs[: len(arrays)], refs[len(arrays) :]
        for job, out in zip(jobs, results):
            mine, ins = ins[: len(job)], ins[len(job) :]
            out[...] = sum(r[...] for r in mine[1:]) + mine[0][...]

    return call(body, arrays, specs, outs, shapes, grid=(1,), name="sums", **rest)


def whole_of(array):
    return array, array.shape[0], 0


def finish_feed(call, one, down, up, **rest):
    args, specs = [one], [block_of(one, 1, 0)]
    for piece, first, two_came, three_came in (down, up):
        args += [piece[2], first, two_came, three_came]
        specs += [block_of(a, 1, at) for a, at in zip(args[-4:], (0, 2, 0, 0))]
    widths = [down[0][2].shape[1], one.shape[1] // 2]

    def body(one, *refs):
        down_o, up_o = refs[-2:]
        values = []
        for a, b, c, d in (refs[:4], refs[4:8]):
            values.append((a[0] + b[0]) + (c[0] + d[0]))
        downs = (values[0], one[0, : widths[1]])
        ups = (values[1], one[0, widths[1] :])
        for down, up, start, width in zip(downs, ups, (0, widths[0]), widths):
            down_o[start : start + width, :] = down
            for j in range(0, width, LANE):
                up_o[:, start + j : start + j + LANE] = up[j : j + LANE, :]

    shapes = [shaped((sum(widths), LANE)), shaped((LANE, sum(widths)))]
    return call(
        body, args, specs, [whole(*a.shape) for a in shapes], shapes, grid=(1,), name="finish_feed", **rest
    )


def finish_heads(call, head, out_q, key_val, **rest):
    args, specs = [], []
    for piece, first, two_came, three_came in (out_q, key_val):
        args += [piece[2], first, two_came, three_came]
        specs += [block_of(a, 1, at) for a, at in zip(args[-4:], (0, 2, 0, 0))]
    width = key_val[0][2].shape[1] // 2
    heads = width // head

    def body(*refs):
        out_o, qkv_o = refs[-2:]
        values = []
        for n in range(2):
            a, b, c, d = refs[4 * n : 4 * n + 4]
            values.append((a[0] + b[0]) + (c[0] + d[0]))
        out_o[...] = values[0][:width]
        columns = []
        for rows in (values[0][width:], values[1][:width], values[1][width:]):
            columns.append(beside(*[rows[j * LANE : (j + 1) * LANE] for j in range(width // LANE)]))
        qkv_o[...] = beside(*[p[:, h * head : (h + 1) * head] for h in range(heads) for p in columns])

    shapes = [shaped((width, LANE)), shaped((LANE, 3 * width))]
    return call(
        body, args, specs, [whole(*a.shape) for a in shapes], shapes, grid=(1,), name="finish_heads", **rest
    )


def far_sums(call, keep, came, far, **rest):
    rows, model = CHUNK, keep.shape[2]
    steps = keep.shape[1] // rows
    spec = pl.BlockSpec((1, rows, model), lambda i: (far(), i, 0))
    parts = isinstance(came, tuple)

    def body(keep, *refs):
        *came, out = refs
        if parts:
            step = pl.program_id(0)
            out[...] = keep[0] + jnp.where(step == 0, came[0][...], came[1][...])
        else:
            out[...] = keep[0] + came[0][0]

    return call(
        body,
        (keep, *came) if parts else (keep, came),
        [spec, *([whole(rows, model)] * 2 if parts else [spec])],
        [rows_at(rows, model)],
        [shaped(keep.shape[1:])],
        grid=(steps,),
        name="far_sums",
        **rest,
    )


def finish_specs(keep, near):
    share, model = keep.shape[1:]
    steps = share // CHUNK
    own = pl.BlockSpec((CHUNK, model), lambda i: (lax.axis_index("branch") * steps + i, 0))
    return own, pl.BlockSpec((1, CHUNK, model), lambda i: (near(), i, 0)), rows_at(CHUNK, model), steps


def finish_output(call, x, keep, came_core, came_chip, bias, near):
    share, model = came_chip.shape
    own, part, row, steps = finish_specs(keep, near)

    def body(x, keep, core, chip, bias, out):
        total = (keep[0] + core[0]) + chip[...]
        out[...] = (x[...].astype(f32) + total + bias[...]).astype(bf16)

    return call(
        body,
        (x, keep, came_core, came_chip, bias),
        [own, part, part, row, whole(1, model)],
        [row],
        [shaped((share, model), bf16)],
        grid=(steps,),
        name="finish_output",
    )[0]


def finish_input(call, x, cot, gain, keep, came_core, came_chip, near):
    share, model = came_chip.shape
    own, part, row, steps = finish_specs(keep, near)


    def body(x, cot, gain, keep, core, chip, out):
        xf = x[...].astype(f32)
        centered = xf - jnp.mean(xf, axis=1, keepdims=True)
        inv = lax.rsqrt(jnp.mean(centered * centered, axis=1, keepdims=True) + epsilon)
        unit = centered * inv
        g = ((keep[0] + core[...]) + chip[...]) * gain[...]
        inner = g - jnp.mean(g, axis=1, keepdims=True) - unit * jnp.mean(g * unit, axis=1, keepdims=True)
        out[...] = inv * inner + cot[...].astype(f32)

    return call(
        body,
        (x, cot, gain, keep, came_core, came_chip),
        [own, own, whole(1, model), part, row, row],
        [row],
        [shaped((share, model))],
        grid=(steps,),
        name="finish_input",
    )[0]


def pack_small(call, head, branch, gain, shift, cot, qb, kvb, ubs, **rest):
    model = cot.shape[1]
    width = qb.shape[1]
    heads = width // head
    up_width = sum(u.shape[1] for u in ubs)
    qkv_rows, up_rows = 3 * width // LANE, up_width // LANE
    starts = [0, model // LANE, 2 * model // LANE, 3 * model // LANE]
    starts.append(starts[3] + qkv_rows * branch)
    total = starts[4] + up_rows * branch

    def body(gain, shift, cot, qb, kvb, ub0, ub1, out):
        out[...] = jnp.zeros_like(out)
        here = lax.axis_index("branch")

        def summed(value):
            return jnp.sum(value, axis=0, keepdims=True)

        def place(row, value):
            for j in range(value.shape[1] // LANE):
                out[pl.ds(row + j, 1), :] = value[:, j * LANE : (j + 1) * LANE]

        place(starts[0], summed(gain[...]))
        place(starts[1], summed(shift[...]))
        place(starts[2], summed(cot[...]) * jnp.where(here == 0, 1.0, 0.0))
        q, kv = summed(qb[...]), summed(kvb[...])
        parts = (q, kv[:, :width], kv[:, width:])
        place(
            starts[3] + here * qkv_rows,
            beside(*[p[:, h * head : (h + 1) * head] for h in range(heads) for p in parts]),
        )
        place(starts[4] + here * up_rows, beside(summed(ub1[...]), summed(ub0[...])))

    args = (gain, shift, cot, qb, kvb, *ubs)
    return call(
        body,
        args,
        [whole(*a.shape) for a in args],
        [whole(total, LANE)],
        [shaped((total, LANE))],
        grid=(1,),
        name="pack_small",
        **rest,
    )


def finish(part, dim, low):
    if low == 1:
        return part
    size = lax.axis_size("batch")
    groups = [[j * low + i for i in range(low)] for j in range(size // low)]
    return lax.psum_scatter(
        part, "batch", scatter_dimension=dim, axis_index_groups=groups, tiled=True
    )


def per_device(
    inputs, ln_gain, ln_shift, qkv_weight, qkv_bias, out_weight, up_weight, up_bias, down_weight,
    out_bias, feature_samples, lengths, cotangent,
):
    tokens, model = inputs.shape
    feats, head = feature_samples.shape
    width = out_weight.shape[0]
    batch = lax.axis_size("batch")
    branch = lax.axis_size("branch")
    low = batch // (model // LANE)
    y_first, z_first = (0, 1, 2), (1, 0, 2)
    bits = [1 << b for b in range(batch.bit_length() - 1)]
    expand = jnp.asarray(expand_table(head), bf16)
    dct_t = jnp.asarray(dct_table(head).T)
    gain = ln_gain.reshape(1, model)
    shift = ln_shift.reshape(1, model)
    up_b = up_bias.reshape(1, -1)
    qkv_b = qkv_bias.reshape(1, -1)
    call = Order()

    def send(value, order, step):
        return swapped(value, "batch", low << order[step])

    def enter(forward, own, came):
        entered = None
        for i, bit in enumerate(bits[1:]):
            entered, own = join_states(call, forward, tokens, i, lengths, entered, own, came)
            came = swapped(own, "batch", bit)
        return entered, own, came

    normed, cb, kf, value, kt, kv_w, basis, cs, state, hidden0, gpre0, ub0, piece0 = front(
        call, head, lengths, inputs, gain, shift, up_weight, up_b, down_weight, cotangent, qkv_weight,
        qkv_b, expand, feature_samples, dct_t,
    )
    groups = [[j * low + i for j in range(batch // low)] for i in range(low)] if low > 1 else None
    sum0 = lax.psum_scatter(
        piece0, "batch", scatter_dimension=0, axis_index_groups=groups, tiled=True
    )
    came = swapped(state, "batch", 1)
    qf, qt, ga, q_w = project_queries(
        call, head, feats, normed, qkv_weight, qkv_b, expand, basis, cs, cotangent, out_weight
    )
    states = enter(True, state, came)
    hidden1, gpre1, ub1, *pieces = feed(
        call, (y_first, z_first), low, normed, up_weight, up_b, down_weight, cotangent
    )
    down, up = pieces[:3], pieces[3:]
    down_first, up_first = send(down[0], y_first, 0), send(up[0], z_first, 0)
    gq, gk, gv, back, state, qb, out_send, out_keep, *oq = attend(
        call, head, y_first, low, len(bits) - 1, lengths, qf, kf, value, qt, ga, cs, expand, basis,
        normed, cotangent, hidden0, hidden1, down_weight, out_weight, *states,
    )
    came = swapped(state, "batch", 1)
    out_core = swapped(out_send, "branch", 1)
    far_chip = lambda: 1 - branch_place()[1]
    near_chip = lambda: branch_place()[1]
    down_2, up_2 = sums_of(
        call, [whole_of(down[1]), (down_first, 2, 0)], [whole_of(up[1]), (up_first, 2, 0)]
    )
    entered, state, oq_first = join_states(
        call, False, tokens, 0, lengths, None, state, came, through=(oq[0],), flops=LONG
    )
    came = swapped(state, "batch", bits[1])
    oq_first = send(oq_first, y_first, 0)
    (out_far,) = far_sums(call, out_keep, out_core, far_chip)
    out_chip = swapped(out_far, "branch", 2)
    for i in range(1, len(bits) - 1):
        entered, state = join_states(call, False, tokens, i, lengths, entered, state, came)
        came = swapped(state, "batch", bits[i + 1])
    down_2, up_2 = hold(call, (down_2, up_2))
    down_2, up_2 = send(down_2, y_first, 1), send(up_2, z_first, 1)
    grad_keep, far0, far1, near, kvb, gain_part, shift_part, *kv = backward(
        call, head, y_first, low, len(bits) - 1, lengths, kf, value, kt, gk, gv, back, cs,
        expand, basis, normed, inputs, gpre0, gpre1, gq, up_weight, q_w, kv_w, entered, state, came,
    )
    far_core = (swapped(far0, "branch", 1), swapped(far1, "branch", 1))
    down_3, up_3, oq_2, near, kv_first = sums_of(
        call, [(down[2], 1, 1), (down_first, 1, 3), (down_2, 1, 1)],
        [(up[2], 1, 1), (up_first, 1, 3), (up_2, 1, 1)], [whole_of(oq[1]), (oq_first, 2, 0)],
        through=(near, kv[0]),
    )
    grad_core = swapped(near, "branch", 1)
    kv_first = send(kv_first, y_first, 0)
    down_3, up_3 = send(down_3, y_first, 2), send(up_3, z_first, 2)
    oq_2 = send(oq_2, y_first, 1)
    (small,) = pack_small(
        call, head, branch, gain_part, shift_part, cb, qb, kvb, (ub0, ub1), flops=SHORT
    )
    came = swapped(small, "branch", 1)
    (grad_far,) = far_sums(call, grad_keep, far_core, lambda: 0)
    grad_chip = swapped(grad_far, "branch", 2)
    output = finish_output(
        call, inputs, out_keep, out_core, out_chip, out_bias.reshape(1, model), near_chip
    )
    (small,) = sums_of(call, [whole_of(small), whole_of(came)], after=(grad_core,))
    came = swapped(small, "batch", 1)
    (kv_2,) = sums_of(call, [whole_of(kv[1]), (kv_first, 2, 0)])
    kv_2 = send(kv_2, y_first, 1)
    (small,) = sums_of(call, [whole_of(small), whole_of(came)])
    came = swapped(small, "batch", bits[1])
    (oq_3,) = sums_of(call, [(oq[2], 1, 1), (oq_first, 1, 3), (oq_2, 1, 1)])
    oq_3 = send(oq_3, y_first, 2)
    for bit in bits[2:]:
        (small,) = sums_of(call, [whole_of(small), whole_of(came)])
        came = swapped(small, "batch", bit)
    (kv_3,) = sums_of(call, [(kv[2], 1, 1), (kv_first, 1, 3), (kv_2, 1, 1)])
    kv_3 = send(kv_3, y_first, 2)
    (small,) = sums_of(call, [whole_of(small), whole_of(came)])
    came = swapped(small, "branch", 2)
    down_sum, up_sum = finish_feed(
        call, sum0, (down, down_first, down_2, down_3), (up, up_first, up_2, up_3)
    )
    out_sum, qkv_sum = finish_heads(
        call, head, (oq, oq_first, oq_2, oq_3), (kv, kv_first, kv_2, kv_3)
    )
    small = finish_small(call, small, came, [model, model, model, 3 * width * branch, up_bias.size * branch])
    input_grad = finish_input(
        call, inputs, cotangent, gain, grad_keep, grad_core, grad_chip, lambda: 1
    )
    down_sum, out_sum = finish(down_sum, 1, low), finish(out_sum, 1, low)
    up_sum, qkv_sum = finish(up_sum, 0, low), finish(qkv_sum, 0, low)

    gain_grad, shift_grad, out_bias_grad, qkv_bias_grad, up_bias_grad = small
    return (
        output,
        input_grad,
        gain_grad,
        shift_grad,
        qkv_sum,
        qkv_bias_grad,
        out_sum,
        up_sum,
        up_bias_grad,
        down_sum,
        out_bias_grad,
    )


def solution(mesh):
    placed = (
        P("batch", None),
        P(),
        P(),
        P(None, "branch"),
        P("branch"),
        P("branch", None),
        P(None, "branch"),
        P("branch"),
        P("branch", None),
        P(),
        P(),
        P(),
        P("batch", None),
    )
    return jax.shard_map(
        per_device,
        mesh=mesh,
        in_specs=placed,
        out_specs=(
            P(("batch", "branch"), None),
            P(("batch", "branch"), None),
            P(),
            P(),
            P("batch", "branch"),
            P(),
            P("branch", "batch"),
            P("batch", "branch"),
            P(),
            P("branch", "batch"),
            P(),
        ),
        check_vma=False,
    )
```

```python
import math

import numpy as np

import jax
import jax.numpy as jnp
from jax import lax
from jax.experimental import pallas as pl
from jax.experimental.pallas import tpu as pltpu
from jax.sharding import PartitionSpec as P

ROT = 16
CHUNK = 256
ROWS = 512
LANE = 128
epsilon = 1e-05
f32 = jnp.float32
bf16 = jnp.bfloat16
HALF_ROOT = math.sqrt(0.5)
GAUSS = 1.0 / math.sqrt(2.0 * math.pi)
VMEM_BYTES = 64 * 2**20
STEP = 2**30
COST_FAR = 13 * STEP
COST_NEAR = 0
COST_END = 10 * STEP
COST_ATTEND = 16 * STEP
COST_KEYS = 50 * STEP
PARTS = ((3, 1), (0, 3))


def nn(a, b):
    return lax.dot_general(a, b, (((1,), (0,)), ((), ())), preferred_element_type=f32)


def nt(a, b):
    return lax.dot_general(a, b, (((1,), (1,)), ((), ())), preferred_element_type=f32)


def tn(a, b):
    return lax.dot_general(a, b, (((0,), (0,)), ((), ())), preferred_element_type=f32)


def two(value):
    high = value.astype(bf16)
    return high, (value - high.astype(f32)).astype(bf16)


def exact3(dot, a, b):
    return dot(a[0], b[0]) + (dot(a[1], b[0]) + dot(a[0], b[1]))


def beside(*parts):
    return jnp.concatenate(parts, axis=1)


def below(*parts):
    return jnp.concatenate(parts, axis=0)


class Order:
    def __init__(self):
        self.last = ()

    def __call__(
        self, body, args, in_specs, out_specs, out_shape, after=(), through=(), flops=0, **rest
    ):
        given, results = len(args), len(out_shape)
        skipped = [*self.last, *after, *through]

        def without(*refs):
            outs = refs[given + len(skipped) :]
            body(*refs[:given], *outs[:results], *outs[results + len(through) :])

        place = pl.BlockSpec(memory_space=pl.ANY)
        first = given + len(skipped) - len(through)
        outs = pl.pallas_call(
            without,
            in_specs=[*in_specs, *[place] * len(skipped)],
            out_specs=[*out_specs, *[place] * len(through)],
            out_shape=[*out_shape, *[shaped(t.shape, t.dtype) for t in through]],
            input_output_aliases={first + i: results + i for i in range(len(through))},
            compiler_params=pltpu.CompilerParams(vmem_limit_bytes=VMEM_BYTES),
            cost_estimate=pl.CostEstimate(flops=flops, bytes_accessed=0, transcendentals=0),
            **rest,
        )(*args, *skipped)
        self.last = (outs[0],)
        return outs


def hold(call, arrays, after=()):
    def body(out):
        out[...] = jnp.zeros_like(out)

    return call(body, (), [], [whole(8, LANE)], [shaped((8, LANE))], after, arrays, grid=(1,), name="hold")[1:]


def shaped(shape, dtype=f32):
    return jax.ShapeDtypeStruct(tuple(shape), dtype)


def whole(*shape):
    return pl.BlockSpec(shape, lambda *ids: (0,) * len(shape))


def rows_at(rows, width):
    return pl.BlockSpec((rows, width), lambda i: (i, 0))


SMEM = pl.BlockSpec(memory_space=pltpu.SMEM)


def dct_table(size):
    row = np.arange(size)[:, None]
    col = np.arange(size)[None, :]
    table = np.cos(math.pi * (col + 0.5) * row / size) * math.sqrt(2.0 / size)
    table[0] *= math.sqrt(0.5)
    return table.astype(np.float32)


def expand_table(head):
    half = ROT // 2
    table = np.zeros((ROT, 3 * LANE), np.float32)
    for lane in range(LANE):
        place = lane % head
        if place < half:
            table[place, lane] = 1.0
            table[half + place, LANE + lane] = -1.0
        elif place < ROT:
            table[place - half, lane] = 1.0
            table[place, 2 * LANE + lane] = 1.0
    return np.concatenate([table] * 3, axis=0)


def ends_of(lengths):
    ends, total = [], jnp.int32(0)
    for j in range(lengths.shape[0]):
        total = total + lengths[j]
        ends.append(total)
    return ends


def seq_start(ends, place):
    start = jnp.zeros_like(place)
    for end in ends:
        start = jnp.where(place >= end, end, start)
    return start


def iota(shape, dim):
    return lax.broadcasted_iota(jnp.int32, shape, dim)


def head_block(head, rows, cols):
    return iota((rows, cols), 0) // head == iota((rows, cols), 1) // head


def turn_tables(cs, expand, head, width):
    wide = tn(cs, expand)
    lane = iota((1, LANE), 1) % head
    cosine = wide[:, :LANE] + jnp.where(lane < ROT, 0.0, 1.0)
    times = width // LANE
    return tuple(
        beside(*[part] * times) for part in (cosine, wide[:, LANE : 2 * LANE], wide[:, 2 * LANE :])
    )


def turn(value, tables, sign):
    cosine, up, down = tables
    width = value.shape[1]
    half = ROT // 2
    moved = pltpu.roll(value, width - half, 1) * up + pltpu.roll(value, half, 1) * down
    return value * cosine + moved if sign > 0 else value * cosine - moved


def own_half(head, rows):
    return iota((rows, LANE), 1) // head == iota((rows, LANE), 0) // head % 2


def pairs_of(width):
    return [slice(p, p + LANE) for p in range(0, width, LANE)]


def outer_pairs(left, right, other):
    return below(
        *[tn(left[:, p], beside(right[:, p], other[:, p])) for p in pairs_of(left.shape[1])]
    )


def masked_state(full, head):
    half = own_half(head, full.shape[0])
    return jnp.where(beside(half, half), full, 0.0)


def fold_state(full, head):
    full = masked_state(full, head)
    return full[:, :LANE] + pltpu.roll(full[:, LANE:], LANE // 2, 1)


def unfold_state(packed, head):
    return masked_state(beside(packed, pltpu.roll(packed, LANE // 2, 1)), head)


def deal(outs, order, low, write):
    mine = lax.axis_index("batch") // low
    first, second, third = (1 << bit for bit in order)
    wanted = [base + i * third for base in (first + second, first, second, 0) for i in range(2)]
    slots = [(out, i) for out in outs for i in range(out.shape[0])]
    for (out, i), block in zip(slots, wanted):
        write(out, i, pl.multiple_of((mine ^ block) * LANE, LANE))


def feed_step(normed, c, up_w, up_b, down_w, hidden_o, gpre_o, ub_o, down_acc, up_acc):
    rows, width = hidden_o.shape
    pre = nn(normed, up_w[...]) + up_b[...]
    grad_hidden = nt(c, down_w[...])
    phi = 0.5 + 0.5 * lax.erf(pre * HALF_ROOT)
    hidden = (pre * phi).astype(bf16)
    hidden_o[...] = hidden
    down_acc[...] += tn(hidden, c)
    slope = phi + pre * jnp.exp(-0.5 * pre * pre) * GAUSS
    gpre = (grad_hidden * slope).astype(bf16)
    gpre_o[...] = gpre
    up_acc[...] += tn(normed, gpre)
    ub_o[...] += jnp.sum(gpre.astype(f32).reshape(rows // 8, 8, width), axis=0)


def clear(*refs):
    for ref in refs:
        ref[...] = jnp.zeros_like(ref)


def write_down(out, i, at, down_acc):
    out[i, : down_acc.shape[0], :] = down_acc[:, pl.ds(at, LANE)]


def write_up(out, i, at, up_acc):
    width = up_acc.shape[1]
    first = out.shape[1] - width
    for j in range(0, width, LANE):
        out[i, first + j : first + j + LANE, :] = up_acc[pl.ds(at, LANE), j : j + LANE]


def feed_specs(tokens, model, units, part):
    first, quarters = PARTS[part]
    width = units // 4 * quarters
    part = first // quarters
    ins = [
        pl.BlockSpec((model, width), lambda i: (0, part)),
        pl.BlockSpec((1, width), lambda i: (0, part)),
        pl.BlockSpec((width, model), lambda i: (part, 0)),
        rows_at(ROWS, model),
    ]
    outs = [rows_at(ROWS, width)] * 2 + [whole(8, width)]
    shapes = [shaped((tokens, width), bf16)] * 2 + [shaped((8, width))]
    scratch = [pltpu.VMEM((width, model), f32), pltpu.VMEM((model, width), f32)]
    return width, ins, outs, shapes, scratch


def feed(call, orders, low, normed, up_w, up_b, down_w, cot, **rest):
    tokens, model = cot.shape
    width, ins, outs, shapes, scratch = feed_specs(tokens, model, up_w.shape[1], 1)
    firsts, piece = shaped((4, width, LANE)), shaped((2, width, LANE))
    pieces_out = [firsts, piece, piece] * 2

    def body(normed, up_w, up_b, down_w, cot, hidden_o, gpre_o, ub_o, *refs):
        *pieces, down_acc, up_acc = refs
        step = pl.program_id(0)

        @pl.when(step == 0)
        def _():
            clear(down_acc, up_acc, ub_o)

        feed_step(
            normed[...], cot[...], up_w, up_b, down_w, hidden_o, gpre_o, ub_o, down_acc, up_acc
        )

        @pl.when(step == pl.num_programs(0) - 1)
        def _():
            deal(pieces[:3], orders[0], low, lambda *at: write_down(*at, down_acc))
            deal(pieces[3:], orders[1], low, lambda *at: write_up(*at, up_acc))

    return call(
        body,
        (normed, up_w, up_b, down_w, cot),
        [rows_at(ROWS, model), *ins],
        outs + [whole(*a.shape) for a in pieces_out],
        shapes + pieces_out,
        **rest,
        grid=(tokens // ROWS,),
        scratch_shapes=scratch,
        name="feed_forward",
    )


def take_columns(w_in, head, heads, part):
    return beside(*[w_in[:, (3 * h + part) * head : (3 * h + part + 1) * head] for h in range(heads)])


def features(part, tables, basis, head, feats):
    width = part.shape[1]
    turned = turn(part.astype(f32), tables, 1)
    square = (turned * turned).astype(bf16)
    ones = jnp.where(head_block(head, width, width), 1.0 / (2.0 * math.sqrt(head)), 0.0).astype(bf16)
    argument = exact3(nn, two(turned), basis) - nn(square, ones)
    return turned.astype(bf16), (jnp.exp(argument) * (1.0 / math.sqrt(feats))).astype(bf16)


def rotary_table(ends, first_pos, rows, tokens, out):
    half = ROT // 2
    order = iota((half, rows), 0)
    frequency = jnp.zeros((half, rows), f32)
    for j in range(half):
        value = float(np.float32(10000.0) ** np.float32(-2.0 * j / ROT))
        frequency = jnp.where(order == j, value, frequency)
    for i in range(tokens // rows):
        place = first_pos + i * rows + iota((half, rows), 1)
        angle = (place - seq_start(ends, place)).astype(f32) * frequency
        circle = below(jnp.cos(angle), jnp.sin(angle))
        high, rest = two(circle)
        middle, lowest = two(circle - high.astype(f32))
        out[i] = below(high, middle, lowest)


def front(
    call, head, lengths, x, gain, shift, up_w, up_b, down_w, cot, qkv_w, qkv_b, expand,
    samples, dct_t,
):
    tokens, model = x.shape
    width = qkv_w.shape[1] // 3
    heads = width // head
    feats = samples.shape[0]
    blocks = tokens // ROWS
    table = (blocks, expand.shape[0], ROWS)
    part, ins, outs, shapes, scratch = feed_specs(tokens, model, up_w.shape[1], 0)
    piece = shaped((model // LANE, 2 * part, LANE))

    def body(
        lengths, x, gain, shift, up_w, up_b, down_w, cot, qkv_w, qkv_b, expand, samples, dct_t,
        normed_o, cb_o, kf_o, v_o, kt_o, w_o, b_o, basis_o, cs_o, state_o, hidden_o, gpre_o, ub_o, piece_o,
        down_acc, up_acc, w_s, b_s, basis_s, cs_s, state_s,
    ):
        step = pl.program_id(0)
        ends = ends_of(lengths)
        first_pos = lax.axis_index("batch") * tokens
        start_last = seq_start(ends, first_pos + tokens - 1)

        @pl.when(step == 0)
        def _():
            clear(down_acc, up_acc, ub_o, cb_o, state_s)
            for part in range(3):
                to = slice(part * width, (part + 1) * width)
                w_s[:, to] = take_columns(qkv_w, head, heads, part)
                b_s[:, to] = take_columns(qkv_b, head, heads, part)
            basis = lax.dot_general(
                dct_t[...], samples[...], (((1,), (1,)), ((), ())),
                preferred_element_type=f32, precision=lax.Precision.HIGHEST,
            )
            basis = basis * (1.0 / head**0.25)
            wide = below(*[beside(*[basis] * heads)] * heads)
            basis_s[...] = jnp.where(head_block(head, width, width), wide, 0.0)
            basis_o[...] = basis_s[...]
            w_o[...] = w_s[...]
            b_o[...] = b_s[...]
            rotary_table(ends, first_pos, ROWS, tokens, cs_s)
            cs_o[...] = cs_s[...]

        xf = x[...].astype(f32)
        centered = xf - jnp.mean(xf, axis=1, keepdims=True)
        inv = lax.rsqrt(jnp.mean(centered * centered, axis=1, keepdims=True) + epsilon)
        normed = (centered * inv * gain[...] + shift[...]).astype(bf16)
        normed_o[...] = normed
        c = cot[...]
        cb_o[...] += jnp.sum(c.astype(f32).reshape(ROWS // 8, 8, model), axis=0)
        feed_step(normed, c, up_w, up_b, down_w, hidden_o, gpre_o, ub_o, down_acc, up_acc)

        projected = (nn(normed, w_s[:, width:]) + b_s[:, width:]).astype(bf16)
        tables = turn_tables(cs_s[step], expand[...], head, width)
        k_turn, k_feat = features(projected[:, :width], tables, two(basis_s[...]), head, feats)
        value = projected[:, width:]
        kf_o[...], v_o[...], kt_o[...] = k_feat, value, k_turn
        place = first_pos + step * ROWS + iota((ROWS, 1), 0)
        tail = jnp.where(place >= start_last, 1.0, 0.0).astype(bf16)
        state_s[...] += outer_pairs(k_feat * tail, value, jnp.ones_like(value))

        @pl.when(step == pl.num_programs(0) - 1)
        def _():
            state_o[...] = fold_state(state_s[...], head)
            for i in range(piece.shape[0]):
                write_down(piece_o, i, i * LANE, down_acc)
                write_up(piece_o, i, i * LANE, up_acc)

    narrow = shaped((tokens, width), bf16)
    return call(
        body,
        (lengths, x, gain, shift, up_w, up_b, down_w, cot, qkv_w, qkv_b, expand, samples, dct_t),
        [SMEM, rows_at(ROWS, model), whole(1, model), whole(1, model), *ins]
        + [whole(*a.shape) for a in (qkv_w, qkv_b, expand, samples, dct_t)],
        [rows_at(ROWS, model), whole(8, model), *[rows_at(ROWS, width)] * 3]
        + [whole(model, 3 * width), whole(1, 3 * width), whole(width, width), whole(*table)]
        + [whole(width, LANE), *outs]
        + [whole(*piece.shape)],
        [shaped((tokens, model), bf16), shaped((8, model)), *[narrow] * 3]
        + [shaped((model, 3 * width), bf16), shaped((1, 3 * width)), shaped((width, width))]
        + [shaped(table, bf16)]
        + [shaped((width, LANE)), *shapes, piece],
        grid=(blocks,),
        scratch_shapes=[
            *scratch,
            pltpu.VMEM((model, 3 * width), bf16),
            pltpu.VMEM((1, 3 * width), f32),
            pltpu.VMEM((width, width), f32),
            pltpu.VMEM(table, bf16),
            pltpu.VMEM((width, 2 * LANE), f32),
        ],
        name="front",
    )


def project_queries(call, head, feats, normed, w, b, expand, basis, cs, cot, out_w):
    tokens, model = normed.shape
    width = out_w.shape[0]

    def body(normed, w, b, expand, basis, cs, cot, out_w, qf_o, qt_o, ga_o):
        projected = (nn(normed[...], w[...]) + b[...]).astype(bf16)
        ga_o[...] = nt(cot[...], out_w[...])
        tables = turn_tables(cs[0], expand[...], head, width)
        qt_o[...], qf_o[...] = features(projected, tables, two(basis[...]), head, feats)

    return call(
        body,
        (normed, w, b, expand, basis, cs, cot, out_w),
        [
            rows_at(ROWS, model),
            whole(model, width),
            whole(1, width),
            whole(*expand.shape),
            whole(*basis.shape),
            pl.BlockSpec((1,) + cs.shape[1:], lambda i: (i, 0, 0)),
            rows_at(ROWS, model),
            whole(*out_w.shape),
        ],
        [rows_at(ROWS, width)] * 3,
        [shaped((tokens, width), bf16), shaped((tokens, width), bf16), shaped((tokens, width))],
        grid=(tokens // ROWS,),
        name="project_queries",
    )


def swapped(value, axis, distance):
    size = lax.axis_size(axis)
    return lax.ppermute(value, axis, [(i, i ^ distance) for i in range(size)])


def joined(forward, lengths, tokens, base, entered, own, came):
    ends = ends_of(lengths)
    here = lax.axis_index("batch")
    count, size = 1, 2
    group = (here >> (base + count)) << (base + count)
    mine = (here >> base) & (size - 1)
    group_end = (group + (size << base)) * tokens
    total = jnp.zeros_like(own)
    entered = total if entered is None else entered
    for m in range(size):
        part = came if m else own
        other = mine ^ m
        if forward:
            edge = (group + ((other + 1) << base)) * tokens
            enters = (other < mine) & (seq_start(ends, here * tokens - 1) < edge)
            counts = seq_start(ends, group_end - 1) < edge
        else:
            start = seq_start(ends, (group + (other << base)) * tokens - 1)
            enters = (other > mine) & (start < (here + 1) * tokens)
            counts = start < group * tokens
        if m:
            entered = entered + jnp.where(enters, part, 0.0)
        total = total + jnp.where(counts, part, 0.0)
    return entered, total


def join_states(call, forward, tokens, base, lengths, entered, own, came, **rest):
    given = [own, came] if entered is None else [entered, own, came]

    def body(lengths, *refs):
        *ins, entered_o, total_o = refs
        values = [r[...] for r in ins]
        if entered is None:
            values = [None, *values]
        entered_o[...], total_o[...] = joined(
            forward, lengths, tokens, base, *values
        )

    spec = whole(*own.shape)
    return call(
        body,
        (lengths, *given),
        [SMEM] + [spec] * len(given),
        [spec, spec],
        [shaped(own.shape)] * 2,
        **rest,
        grid=(1,),
        name="join_states",
    )


def turned_grad(grad_feat, feat, turned, basis, tables, head, width):
    weighted = (grad_feat * feat.astype(f32)).astype(bf16)
    ones = jnp.where(head_block(head, width, width), 1.0 / math.sqrt(head), 0.0).astype(bf16)
    grad = nt(beside(weighted, weighted), beside(*basis)) - nn(weighted, ones) * turned.astype(f32)
    return turn(grad, tables, -1).astype(bf16)


def attend_kernel(
    head, tokens, per_step, base, lengths, qf, kf, v, qt, ga, cs, expand, basis_i,
    normed, cot, hidden0, hidden1, down_w, out_w, entered_i, own_i, came_i,
    gq_o, gk_o, gv_o, back_o, total_o, qb_o, send_o, keep_o, *refs,
):
    piece_o, state_s, q_acc, o_acc, total_s = refs
    step = pl.program_id(0)
    width = qf.shape[1]
    heads = width // head
    ends = ends_of(lengths)
    first_pos = lax.axis_index("batch") * tokens

    @pl.when(step == 0)
    def _():
        entered, _ = joined(
            True, lengths, tokens, base, entered_i[...], own_i[...], came_i[...]
        )
        state_s[...] = unfold_state(entered, head)
        q_acc[...] = jnp.zeros_like(q_acc)
        o_acc[...] = jnp.zeros_like(o_acc)
        total_s[...] = jnp.zeros_like(total_s)
        qb_o[...] = jnp.zeros_like(qb_o)

    basis = two(basis_i[...])
    block = head_block(head, width, width)
    ones = jnp.where(block, 1.0, 0.0).astype(bf16)
    lanes = [jnp.where(iota((1, width), 1) // head == h, 1.0, 0.0).astype(bf16) for h in range(heads)]
    state = state_s[...]
    total = total_s[...]
    part = hidden0.shape[1]
    subs = range(per_step)
    ats = [slice(sub * CHUNK, (sub + 1) * CHUNK) for sub in subs]
    row = iota((CHUNK, 1), 0)
    col = iota((CHUNK, CHUNK), 1)
    causal = col <= iota((CHUNK, CHUNK), 0)
    windows, carries, states, live = [], [], [], []
    for sub, at in zip(subs, ats):
        begin = first_pos + (step * per_step + sub) * CHUNK
        last = seq_start(ends, begin + CHUNK - 1)
        start = seq_start(ends, begin + row)
        windows.append(causal & (col + begin >= start))
        carries.append(jnp.where(start < begin, 1.0, 0.0))
        live.append(jnp.where(seq_start(ends, begin - 1) < first_pos, 1.0, 0.0))
        states.append(two(state))
        tail = jnp.where(begin + row >= last, 1.0, 0.0).astype(bf16)
        retain = jnp.where(last < begin, 1.0, 0.0)
        value = v[at, :]
        added = outer_pairs(kf[at, :] * tail, value, jnp.ones_like(value))
        state = retain * state + masked_state(added, head)
    scores = [
        [jnp.where(window, nt(qf[at, :] * lane, kf[at, :]), 0.0).astype(bf16) for lane in lanes]
        for at, window in zip(ats, windows)
    ]
    outward = nn(hidden1[...], down_w[:-part]) + nn(hidden0[...], down_w[-part:])
    q_carries = [qf[at, :] * c.astype(bf16) for at, c in zip(ats, carries)]
    attends, overs, mixes = [], [], []
    for sub, at in zip(subs, ats):
        nums, dens = [], []
        for p, pair in enumerate(pairs_of(width)):
            mine = range(p * LANE // head, (p + 1) * LANE // head)
            right = [
                beside(v[at, pair] * lanes[h][:, pair], jnp.broadcast_to(lanes[h][:, pair], (CHUNK, LANE)))
                for h in mine
            ]
            carry = q_carries[sub][:, pair]
            sums = nn(
                beside(*[scores[sub][h] for h in mine], carry, carry),
                below(*right, states[sub][0][pair, :], states[sub][1][pair, :]),
            )
            nums.append(sums[:, :LANE])
            dens.append(sums[:, LANE:])
        overs.append(1.0 / beside(*dens))
        attends.append(beside(*nums) * overs[sub])
        mixes.append(attends[sub].astype(bf16))
    g_nums = [(ga[at, :] * over).astype(bf16) for at, over in zip(ats, overs)]
    g_dens = []
    for g_num, attended in zip(g_nums, attends):
        product = two(g_num.astype(f32) * attended)
        g_dens.append(-nn(beside(*product), below(ones, ones)))
    g_heads = [[g_num * lane for lane in lanes] for g_num in g_nums]
    mixing = [
        [
            jnp.where(
                windows[sub], nt(g_heads[sub][h], v[at, :]) + g_dens[sub][:, h * head : h * head + 1], 0.0
            ).astype(bf16)
            for h in range(heads)
        ]
        for sub, at in zip(subs, ats)
    ]
    grad_fqs = []
    for sub, at in zip(subs, ats):
        den_two = two(g_dens[sub] * (2.0 / head))
        den_both = jnp.where(iota((1, width), 1) % head < head // 2, den_two[0], den_two[1])
        from_state = []
        for pair in pairs_of(width):
            left = beside(g_nums[sub][:, pair], den_both[:, pair])
            from_state.append(
                nt(beside(left, left), beside(states[sub][0][pair, :], states[sub][1][pair, :]))
            )
        grad_fqs.append(
            carries[sub] * beside(*from_state)
            + nn(beside(*mixing[sub]), below(*[kf[at, :] * lane for lane in lanes]))
        )
    gqs = []
    for sub, at in zip(subs, ats):
        tables = turn_tables(cs[0, :, at], expand[...], head, width)
        gqs.append(turned_grad(grad_fqs[sub], qf[at, :], qt[at, :], basis, tables, head, width))
    for sub, at in zip(subs, ats):
        gk_o[at, :] = tn(below(*mixing[sub]), below(*[qf[at, :] * lane for lane in lanes]))
        gv_o[at, :] = tn(below(*scores[sub]), below(*g_heads[sub]))
        back = fold_state(outer_pairs(q_carries[sub], g_nums[sub], g_dens[sub].astype(bf16)), head)
        back_o[sub] = back
        total = total + live[sub] * back
    gq = below(*gqs)
    gq_o[...] = gq
    qb_o[...] += jnp.sum(gq.astype(f32).reshape(per_step * CHUNK // 8, 8, width), axis=0)
    q_acc[...] += tn(normed[...], gq)
    o_acc[...] += tn(below(*mixes), cot[...])
    state_s[...] = state
    total_s[...] = total
    outward = outward + nn(below(*mixes), out_w[...])
    by_core(step & 1, send_o, keep_o, outward)

    @pl.when(step == pl.num_programs(0) - 1)
    def _():
        total_o[...] = total

        for i in range(piece_o.shape[0]):
            write_down(piece_o, i, i * LANE, o_acc)
            write_up(piece_o, i, i * LANE, q_acc)


def by_core(core, send, keep, value):
    mine = lax.axis_index("branch") & 1

    @pl.when(core != mine)
    def _():
        send[0] = value

    @pl.when(core == mine)
    def _():
        keep[0] = value


def attend(
    call, head, base, lengths, qf, kf, v, qt, ga, cs, expand, basis, normed, cot,
    hidden0, hidden1, down_w, out_w, entered, own, came, **rest,
):
    tokens, width = qf.shape
    model = cot.shape[1]
    per_step = ROWS // CHUNK
    chunks = tokens // CHUNK
    part = hidden0.shape[1]
    piece = shaped((model // LANE, 2 * width, LANE))
    chip = pl.BlockSpec((1, ROWS, model), lambda i: (i >> 1, 0, 0))
    row = rows_at(ROWS, width)
    packed = whole(width, LANE)

    def body(*refs):
        attend_kernel(head, tokens, per_step, base, *refs)

    return call(
        body,
        (lengths, qf, kf, v, qt, ga, cs, expand, basis, normed, cot, hidden0, hidden1, down_w, out_w)
        + (entered, own, came),
        [
            SMEM,
            *[row] * 5,
            pl.BlockSpec((1,) + cs.shape[1:], lambda i: (i, 0, 0)),
            whole(*expand.shape),
            whole(width, width),
            rows_at(ROWS, model),
            rows_at(ROWS, model),
            rows_at(ROWS, part),
            rows_at(ROWS, hidden1.shape[1]),
            whole(*down_w.shape),
            whole(*out_w.shape),
            *[packed] * 3,
        ],
        [
            *[row] * 3,
            pl.BlockSpec((per_step, width, LANE), lambda i: (i, 0, 0)),
            packed,
            whole(8, width),
            chip,
            chip,
            whole(*piece.shape),
        ],
        [
            shaped((tokens, width), bf16),
            shaped((tokens, width)),
            shaped((tokens, width)),
            shaped((chunks, width, LANE)),
            shaped((width, LANE)),
            shaped((8, width)),
            *[shaped((tokens // ROWS // 2, ROWS, model))] * 2,
            piece,
        ],
        **rest,
        grid=(tokens // ROWS,),
        scratch_shapes=[
            pltpu.VMEM((width, 2 * LANE), f32),
            pltpu.VMEM((model, width), f32),
            pltpu.VMEM((width, model), f32),
            pltpu.VMEM((width, LANE), f32),
        ],
        name="attend",
        flops=COST_ATTEND,
    )


def branch_place():
    here = lax.axis_index("branch")
    return here & 1, here >> 1


def keys(
    call, head, order, low, base, lengths, kf, v, kt, gk, gv, back, cs, expand, basis, normed,
    entered, own, came, **rest,
):
    tokens, width = kf.shape
    model = normed.shape[1]
    chunks, per_step = tokens // CHUNK, ROWS // CHUNK
    row = lambda n: rows_at(ROWS, n)
    packed = whole(width, LANE)
    firsts, piece = shaped((4, 2 * width, LANE)), shaped((2, 2 * width, LANE))
    acc_shape = (model, 2 * width)

    def body(
        lengths, kf, v, kt, gk, gv, back, cs, expand, basis_i, normed, entered_i, own_i, came_i,
        gkv_o, kvb_o, *refs,
    ):
        *pieces, acc, state_s = refs
        step = pl.program_id(0)
        ends = ends_of(lengths)
        first_pos = lax.axis_index("batch") * tokens

        @pl.when(step == 0)
        def _():
            clear(kvb_o, acc)
            state, _ = joined(
                False, lengths, tokens, base, entered_i[...], own_i[...], came_i[...]
            )
            for chunk in reversed(range(chunks)):
                state_s[chunk] = state
                begin = first_pos + chunk * CHUNK
                last = seq_start(ends, begin + CHUNK - 1)
                state = back[chunk] + jnp.where(last < begin, state, 0.0)

        basis = two(basis_i[...])
        tables = turn_tables(cs[0], expand[...], head, width)
        share = jnp.full((CHUNK, LANE), 1.0 / head, bf16)
        heres = [slice(sub * CHUNK, (sub + 1) * CHUNK) for sub in range(per_step)]
        tails, states = [], []
        for sub in range(per_step):
            begin = first_pos + (step * per_step + sub) * CHUNK
            last = seq_start(ends, begin + CHUNK - 1)
            tails.append(jnp.where(begin + iota((CHUNK, 1), 0) >= last, 1.0, 0.0))
            states.append(two(unfold_state(state_s[step * per_step + sub], head)))
        grad_fks, grad_vs = [], []
        for here, tail, state in zip(heres, tails, states):
            to_k, to_v = [], []
            for pair in pairs_of(width):
                high, low_ = state[0][pair, :], state[1][pair, :]
                left = beside(v[here, pair], share)
                to_k.append(nt(beside(left, left), beside(high, low_)))
                to_v.append(
                    nn(beside(kf[here, pair], kf[here, pair]), below(high[:, :LANE], low_[:, :LANE]))
                )
            grad_fks.append(gk[here, :] + tail * beside(*to_k))
            grad_vs.append((gv[here, :] + tail * beside(*to_v)).astype(bf16))
        grad_k = turned_grad(below(*grad_fks), kf[...], kt[...], basis, tables, head, width)
        grads = [beside(grad_k, below(*grad_vs))]
        both = below(*grads)
        gkv_o[...] = both
        kvb_o[...] += jnp.sum(both.astype(f32).reshape(ROWS // 8, 8, 2 * width), axis=0)
        acc[...] += tn(normed[...], both)

        @pl.when(step == pl.num_programs(0) - 1)
        def _():
            deal(pieces, order, low, lambda *spot: write_up(*spot, acc))

    pieces = [firsts, piece, piece]
    return call(
        body,
        (lengths, kf, v, kt, gk, gv, back, cs, expand, basis, normed, entered, own, came),
        [SMEM, *[row(width)] * 5]
        + [whole(*back.shape)]
        + [pl.BlockSpec((1,) + cs.shape[1:], lambda i: (i, 0, 0)), whole(*expand.shape)]
        + [whole(width, width), row(model), *[packed] * 3],
        [row(2 * width), whole(8, 2 * width), *[whole(*a.shape) for a in pieces]],
        [shaped((tokens, 2 * width), bf16), shaped((8, 2 * width)), *pieces],
        **rest,
        grid=(tokens // ROWS,),
        scratch_shapes=[pltpu.VMEM(acc_shape, f32), pltpu.VMEM((chunks, width, LANE), f32)],
        name="keys",
    )


def inward(call, far, x, gpre0, gpre1, gq, gkv, up_w, qkv_w, **rest):
    tokens, model = x.shape
    part = gpre0.shape[1]

    def at(i):
        core, chip = branch_place()
        return 2 * (1 - chip) + i if far else 2 * chip + (i ^ (1 - core))

    row = lambda a: pl.BlockSpec((ROWS, a.shape[1]), lambda i: (at(i), 0))

    def body(x, gpre0, gpre1, gq, gkv, up_w, qkv_w, *refs):
        *outs, gain_o, shift_o = refs
        step = pl.program_id(0)

        @pl.when(step == 0)
        def _():
            clear(gain_o, shift_o)

        grad = nt(gpre1[...], up_w[:, :-part]) + nt(gpre0[...], up_w[:, -part:])
        grad = grad + nt(beside(gq[...], gkv[...]), qkv_w[...])
        if far:
            outs[0][0] = grad
        else:

            @pl.when(step == 0)
            def _():
                outs[0][...] = grad[: ROWS // 2]
                outs[1][...] = grad[ROWS // 2 :]

            @pl.when(step == 1)
            def _():
                outs[2][...] = grad

        xf = x[...].astype(f32)
        centered = xf - jnp.mean(xf, axis=1, keepdims=True)
        unit = centered * lax.rsqrt(jnp.mean(centered * centered, axis=1, keepdims=True) + epsilon)
        gain_o[...] += jnp.sum((grad * unit).reshape(ROWS // 8, 8, model), axis=0)
        shift_o[...] += jnp.sum(grad.reshape(ROWS // 8, 8, model), axis=0)

    if far:
        specs = [pl.BlockSpec((1, ROWS, model), lambda i: (i, 0, 0))]
        shapes = [shaped((2, ROWS, model))]
    else:
        shapes = [shaped((rows, model)) for rows in (ROWS // 2, ROWS // 2, ROWS)]
        specs = [whole(*a.shape) for a in shapes]
    return call(
        body,
        (x, gpre0, gpre1, gq, gkv, up_w, qkv_w),
        [row(a) for a in (x, gpre0, gpre1, gq, gkv)] + [whole(*up_w.shape), whole(*qkv_w.shape)],
        specs + [whole(8, model)] * 2,
        shapes + [shaped((8, model))] * 2,
        **rest,
        grid=(2,),
        name="inward",
    )


def finish_small(call, one, other, sizes):
    shapes = [shaped((size // LANE, LANE)) for size in sizes]

    def body(one, other, *outs):
        row = 0
        for out in outs:
            out[...] = one[row : row + out.shape[0], :] + other[row : row + out.shape[0], :]
            row += out.shape[0]

    parts = call(
        body,
        (one, other),
        [whole(*one.shape)] * 2,
        [whole(*a.shape) for a in shapes],
        shapes,
        grid=(1,),
        name="finish_small",
    )
    return [part.reshape(-1) for part in parts]


def block_of(array, count, at):
    shape = (count,) + array.shape[1:]
    return pl.BlockSpec(shape, lambda i: (at() if callable(at) else at,) + (0,) * (len(shape) - 1))


def sums_of(call, *jobs, stack=False, **rest):
    arrays, specs, shapes = [], [], []
    for job in jobs:
        for array, count, at in job:
            arrays.append(array)
            specs.append(block_of(array, count, at))
        shapes.append(shaped((count,) + array.shape[1:]))
    counts = [a.shape[0] for a in shapes]
    if stack:
        shapes = [shaped((sum(counts),) + shapes[0].shape[1:])]
    outs = [whole(*a.shape) for a in shapes]

    def body(*refs):
        ins, results = refs[: len(arrays)], refs[len(arrays) :]
        start = 0
        for i, job in enumerate(jobs):
            mine, ins = ins[: len(job)], ins[len(job) :]
            value = sum(r[...] for r in mine[1:]) + mine[0][...]
            if stack:
                results[0][start : start + counts[i]] = value
                start += counts[i]
            else:
                results[i][...] = value

    return call(body, arrays, specs, outs, shapes, grid=(1,), name="sums", **rest)


def whole_of(array):
    return array, array.shape[0], 0


def finish_feed(call, one, down, up, **rest):
    args, specs = [one], [block_of(one, 1, 0)]
    for piece, first, two_came, (three_came, which) in (down, up):
        args += [piece[2], first, two_came, three_came]
        specs += [block_of(a, 1, at) for a, at in zip(args[-4:], (0, 2, 0, which))]
    widths = [down[0][2].shape[1], one.shape[1] // 2]

    def body(one, *refs):
        down_o, up_o = refs[-2:]
        values = []
        for a, b, c, d in (refs[:4], refs[4:8]):
            values.append((a[0] + b[0]) + (c[0] + d[0]))
        downs = (values[0], one[0, : widths[1]])
        ups = (values[1], one[0, widths[1] :])
        for down, up, start, width in zip(downs, ups, (0, widths[0]), widths):
            down_o[start : start + width, :] = down
            for j in range(0, width, LANE):
                up_o[:, start + j : start + j + LANE] = up[j : j + LANE, :]

    shapes = [shaped((sum(widths), LANE)), shaped((LANE, sum(widths)))]
    return call(
        body, args, specs, [whole(*a.shape) for a in shapes], shapes, grid=(1,), name="finish_feed", **rest
    )


def finish_heads(call, head, one, key_val, **rest):
    piece, first, two_came, three_came = key_val
    args = [one, piece[2], first, two_came, three_came]
    specs = [block_of(a, 1, at) for a, at in zip(args, (0, 0, 2, 0, 0))]
    width = one.shape[1] // 2
    heads = width // head

    def body(one, a, b, c, d, out_o, qkv_o):
        value = (a[0] + b[0]) + (c[0] + d[0])
        out_o[...] = one[0, :width]
        columns = []
        for rows in (one[0, width:], value[:width], value[width:]):
            columns.append(beside(*[rows[j * LANE : (j + 1) * LANE] for j in range(width // LANE)]))
        qkv_o[...] = beside(*[p[:, h * head : (h + 1) * head] for h in range(heads) for p in columns])

    shapes = [shaped((width, LANE)), shaped((LANE, 3 * width))]
    return call(
        body, args, specs, [whole(*a.shape) for a in shapes], shapes, grid=(1,), name="finish_heads", **rest
    )


def far_sums(call, one, other, far=(lambda: 0, lambda: 0), **rest):
    rows, model = CHUNK, one.shape[2]
    specs = [pl.BlockSpec((1, rows, model), lambda i, at=at: (at(), i, 0)) for at in far]

    def body(one, other, out):
        out[...] = one[0] + other[0]

    return call(
        body,
        (one, other),
        specs,
        [rows_at(rows, model)],
        [shaped(one.shape[1:])],
        grid=(one.shape[1] // rows,),
        name="far_sums",
        **rest,
    )


def finish_specs(share, model):
    steps = share // CHUNK
    own = pl.BlockSpec((CHUNK, model), lambda i: (lax.axis_index("branch") * steps + i, 0))
    return own, rows_at(CHUNK, model), steps


def finish_output(call, x, keep, came_core, came_chip, bias, near):
    share, model = came_chip.shape
    own, row, steps = finish_specs(share, model)
    part = pl.BlockSpec((1, CHUNK, model), lambda i: (near(), i, 0))

    def body(x, keep, core, chip, bias, out):
        total = (keep[0] + core[0]) + chip[...]
        out[...] = (x[...].astype(f32) + total + bias[...]).astype(bf16)

    return call(
        body,
        (x, keep, came_core, came_chip, bias),
        [own, part, part, row, whole(1, model)],
        [row],
        [shaped((share, model), bf16)],
        grid=(steps,),
        name="finish_output",
    )[0]


def finish_input(call, x, cot, gain, keep, came_core, came_chip, **rest):
    share, model = came_chip.shape
    own, row, steps = finish_specs(share, model)


    def body(x, cot, gain, keep, core0, core1, chip, out):
        core = jnp.where(pl.program_id(0) == 0, core0[...], core1[...])
        xf = x[...].astype(f32)
        centered = xf - jnp.mean(xf, axis=1, keepdims=True)
        inv = lax.rsqrt(jnp.mean(centered * centered, axis=1, keepdims=True) + epsilon)
        unit = centered * inv
        g = ((keep[...] + core) + chip[...]) * gain[...]
        inner = g - jnp.mean(g, axis=1, keepdims=True) - unit * jnp.mean(g * unit, axis=1, keepdims=True)
        out[...] = inv * inner + cot[...].astype(f32)

    return call(
        body,
        (x, cot, gain, keep, *came_core, came_chip),
        [own, own, whole(1, model), row, *[whole(CHUNK, model)] * 2, row],
        [row],
        [shaped((share, model))],
        **rest,
        grid=(steps,),
        name="finish_input",
    )[0]


def pack_small(call, head, branch, gains, shifts, cot, qb, kvb, ubs, **rest):
    model = cot.shape[1]
    width = qb.shape[1]
    heads = width // head
    up_width = sum(u.shape[1] for u in ubs)
    qkv_rows, up_rows = 3 * width // LANE, up_width // LANE
    starts = [0, model // LANE, 2 * model // LANE, 3 * model // LANE]
    starts.append(starts[3] + qkv_rows * branch)
    total = starts[4] + up_rows * branch

    def body(gain0, gain1, shift0, shift1, cot, qb, kvb, ub0, ub1, out):
        out[...] = jnp.zeros_like(out)
        here = lax.axis_index("branch")

        def summed(value):
            return jnp.sum(value, axis=0, keepdims=True)

        def place(row, value):
            for j in range(value.shape[1] // LANE):
                out[pl.ds(row + j, 1), :] = value[:, j * LANE : (j + 1) * LANE]

        place(starts[0], summed(gain0[...] + gain1[...]))
        place(starts[1], summed(shift0[...] + shift1[...]))
        place(starts[2], summed(cot[...]) * jnp.where(here == 0, 1.0, 0.0))
        q, kv = summed(qb[...]), summed(kvb[...])
        parts = (q, kv[:, :width], kv[:, width:])
        place(
            starts[3] + here * qkv_rows,
            beside(*[p[:, h * head : (h + 1) * head] for h in range(heads) for p in parts]),
        )
        place(starts[4] + here * up_rows, beside(summed(ub1[...]), summed(ub0[...])))

    args = (*gains, *shifts, cot, qb, kvb, *ubs)
    return call(
        body,
        args,
        [whole(*a.shape) for a in args],
        [whole(total, LANE)],
        [shaped((total, LANE))],
        grid=(1,),
        name="pack_small",
        **rest,
    )


def finish(part, dim, low):
    if low == 1:
        return part
    size = lax.axis_size("batch")
    groups = [[j * low + i for i in range(low)] for j in range(size // low)]
    return lax.psum_scatter(
        part, "batch", scatter_dimension=dim, axis_index_groups=groups, tiled=True
    )


def per_device(
    inputs, ln_gain, ln_shift, qkv_weight, qkv_bias, out_weight, up_weight, up_bias, down_weight,
    out_bias, feature_samples, lengths, cotangent,
):
    tokens, model = inputs.shape
    feats, head = feature_samples.shape
    width = out_weight.shape[0]
    batch = lax.axis_size("batch")
    branch = lax.axis_size("branch")
    low = batch // (model // LANE)
    y_first, z_first = (0, 1, 2), (1, 2, 0)
    bits = [1 << b for b in range(batch.bit_length() - 1)]
    expand = jnp.asarray(expand_table(head), bf16)
    dct_t = jnp.asarray(dct_table(head).T)
    gain = ln_gain.reshape(1, model)
    shift = ln_shift.reshape(1, model)
    up_b = up_bias.reshape(1, -1)
    qkv_b = qkv_bias.reshape(1, -1)
    call = Order()

    def send(value, order, step):
        return swapped(value, "batch", low << order[step])

    def enter(forward, own, came):
        entered = None
        for i, bit in enumerate(bits[1:]):
            entered, own = join_states(call, forward, tokens, i, lengths, entered, own, came)
            came = swapped(own, "batch", bit)
        return entered, own, came

    normed, cb, kf, value, kt, w_perm, b_perm, basis, cs, state, hidden0, gpre0, ub0, piece0 = front(
        call, head, lengths, inputs, gain, shift, up_weight, up_b, down_weight, cotangent, qkv_weight,
        qkv_b, expand, feature_samples, dct_t,
    )
    groups = [[j * low + i for j in range(batch // low)] for i in range(low)] if low > 1 else None

    def scattered(piece):
        return lax.psum_scatter(
            piece, "batch", scatter_dimension=0, axis_index_groups=groups, tiled=True
        )

    sum0 = scattered(piece0)
    came = swapped(state, "batch", 1)
    qf, qt, ga = project_queries(
        call, head, feats, normed, w_perm, b_perm, expand, basis, cs, cotangent, out_weight
    )
    states = enter(True, state, came)
    hidden1, gpre1, ub1, *pieces = feed(
        call, (y_first, z_first), low, normed, up_weight, up_b, down_weight, cotangent
    )
    down, up = pieces[:3], pieces[3:]
    down_first, up_first = send(down[0], y_first, 0), send(up[0], z_first, 0)
    gq, gk, gv, back, state, qb, out_send, out_keep, oq = attend(
        call, head, len(bits) - 1, lengths, qf, kf, value, qt, ga, cs, expand, basis,
        normed, cotangent, hidden0, hidden1, down_weight, out_weight, *states,
    )
    came = swapped(state, "batch", 1)
    out_core = swapped(out_send, "branch", 1)
    far_chip = lambda: 1 - branch_place()[1]
    near_chip = lambda: branch_place()[1]
    down_2, up_2 = sums_of(
        call, [whole_of(down[1]), (down_first, 2, 0)], [whole_of(up[1]), (up_first, 2, 0)],
        after=(sum0,),
    )
    entered, state = join_states(
        call, False, tokens, 0, lengths, None, state, came, flops=50 * STEP
    )
    came = swapped(state, "batch", bits[1])
    (out_far,) = far_sums(call, out_keep, out_core, (far_chip, far_chip))
    out_chip = swapped(out_far, "branch", 2)
    for i in range(1, len(bits) - 1):
        entered, state = join_states(call, False, tokens, i, lengths, entered, state, came)
        came = swapped(state, "batch", bits[i + 1])
    down_2, up_2, oq = hold(call, (down_2, up_2, oq))
    sum_oq = scattered(oq)
    down_2, up_2 = send(down_2, y_first, 1), send(up_2, z_first, 1)
    gkv, kvb, *kv = keys(
        call, head, y_first, low, len(bits) - 1, lengths, kf, value, kt, gk, gv, back, cs, expand,
        basis, normed, entered, state, came, flops=COST_KEYS,
    )
    kv_first = send(kv[0], y_first, 0)
    in_args = (inputs, gpre0, gpre1, gq, gkv, up_weight, w_perm)
    far, gain0, shift0 = inward(call, True, *in_args, flops=COST_FAR)
    cores = [[i, i + 1] for i in range(0, branch, 2)]
    far = lax.all_to_all(far, "branch", 0, 0, axis_index_groups=cores, tiled=True)
    (grad_far,) = far_sums(call, far, far, (lambda: 0, lambda: 1))
    grad_chip = swapped(grad_far, "branch", 2)
    kv_2, down_3, up_3 = sums_of(
        call, [whole_of(kv[1]), (kv_first, 2, 0)],
        [(down[2], 1, 1), (down_first, 1, 3), (down_2, 1, 1)],
        [(up[2], 1, 1), (up_first, 1, 3), (up_2, 1, 1)],
    )
    kv_2, down_3, up_3 = send(kv_2, y_first, 1), send(down_3, y_first, 2), send(up_3, z_first, 2)
    near0, near1, grad_keep, gain1, shift1 = inward(call, False, *in_args, flops=COST_NEAR)
    (small,) = pack_small(
        call, head, branch, (gain0, gain1), (shift0, shift1), cb, qb, kvb, (ub0, ub1),
        after=(out_chip,),
    )
    came = swapped(small, "batch", 1)
    grad_core = swapped(near0, "branch", 1), swapped(near1, "branch", 1)
    output = finish_output(
        call, inputs, out_keep, out_core, out_chip, out_bias.reshape(1, model), near_chip
    )
    (small,) = sums_of(call, [whole_of(small), whole_of(came)])
    came = swapped(small, "batch", bits[1])
    down_sum, up_sum = finish_feed(
        call, sum0, (down, down_first, down_2, (down_3, 0)), (up, up_first, up_2, (up_3, 0))
    )
    for bit in bits[2:]:
        (small,) = sums_of(call, [whole_of(small), whole_of(came)])
        came = swapped(small, "batch", bit)
    (small,) = sums_of(call, [whole_of(small), whole_of(came)])
    came = swapped(small, "branch", 1)
    (kv_3,) = sums_of(call, [(kv[2], 1, 1), (kv_first, 1, 3), (kv_2, 1, 1)])
    kv_3 = send(kv_3, y_first, 2)
    (small,) = sums_of(call, [whole_of(small), whole_of(came)], flops=COST_END)
    came = swapped(small, "branch", 2)
    small = finish_small(call, small, came, [model, model, model, 3 * width * branch, up_bias.size * branch])
    input_grad = finish_input(
        call, inputs, cotangent, gain, grad_keep, grad_core, grad_chip, after=(sum_oq,)
    )
    out_sum, qkv_sum = finish_heads(call, head, sum_oq, (kv, kv_first, kv_2, kv_3))
    down_sum, out_sum = finish(down_sum, 1, low), finish(out_sum, 1, low)
    up_sum, qkv_sum = finish(up_sum, 0, low), finish(qkv_sum, 0, low)

    gain_grad, shift_grad, out_bias_grad, qkv_bias_grad, up_bias_grad = small
    return (
        output,
        input_grad,
        gain_grad,
        shift_grad,
        qkv_sum,
        qkv_bias_grad,
        out_sum,
        up_sum,
        up_bias_grad,
        down_sum,
        out_bias_grad,
    )


def solution(mesh):
    placed = (
        P("batch", None),
        P(),
        P(),
        P(None, "branch"),
        P("branch"),
        P("branch", None),
        P(None, "branch"),
        P("branch"),
        P("branch", None),
        P(),
        P(),
        P(),
        P("batch", None),
    )
    return jax.shard_map(
        per_device,
        mesh=mesh,
        in_specs=placed,
        out_specs=(
            P(("batch", "branch"), None),
            P(("batch", "branch"), None),
            P(),
            P(),
            P("batch", "branch"),
            P(),
            P("branch", "batch"),
            P("batch", "branch"),
            P(),
            P("branch", "batch"),
            P(),
        ),
        check_vma=False,
    )
```

```python
import math

import numpy as np

import jax
import jax.numpy as jnp
from jax import lax
from jax.experimental import pallas as pl
from jax.experimental.pallas import tpu as pltpu
from jax.sharding import PartitionSpec as P

ROT = 16
CHUNK = 256
ROWS = 512
LANE = 128
epsilon = 1e-05
f32 = jnp.float32
bf16 = jnp.bfloat16
HALF_ROOT = math.sqrt(0.5)
GAUSS = 1.0 / math.sqrt(2.0 * math.pi)
VMEM_BYTES = 64 * 2**20
STEP = 2**30
COST_FAR = 13 * STEP
COST_NEAR = 0
COST_END = 10 * STEP
COST_ATTEND = 6 * STEP
COST_KEYS = 50 * STEP
PARTS = ((3, 1), (0, 3))


def nn(a, b):
    return lax.dot_general(a, b, (((1,), (0,)), ((), ())), preferred_element_type=f32)


def nt(a, b):
    return lax.dot_general(a, b, (((1,), (1,)), ((), ())), preferred_element_type=f32)


def tn(a, b):
    return lax.dot_general(a, b, (((0,), (0,)), ((), ())), preferred_element_type=f32)


def two(value):
    high = value.astype(bf16)
    return high, (value - high.astype(f32)).astype(bf16)


def exact3(dot, a, b):
    return dot(a[0], b[0]) + (dot(a[1], b[0]) + dot(a[0], b[1]))


def beside(*parts):
    return jnp.concatenate(parts, axis=1)


def below(*parts):
    return jnp.concatenate(parts, axis=0)


class Order:
    def __init__(self):
        self.last = ()

    def __call__(
        self, body, args, in_specs, out_specs, out_shape, after=(), through=(), flops=0, **rest
    ):
        given, results = len(args), len(out_shape)
        skipped = [*self.last, *after, *through]

        def without(*refs):
            outs = refs[given + len(skipped) :]
            body(*refs[:given], *outs[:results], *outs[results + len(through) :])

        place = pl.BlockSpec(memory_space=pl.ANY)
        first = given + len(skipped) - len(through)
        outs = pl.pallas_call(
            without,
            in_specs=[*in_specs, *[place] * len(skipped)],
            out_specs=[*out_specs, *[place] * len(through)],
            out_shape=[*out_shape, *[shaped(t.shape, t.dtype) for t in through]],
            input_output_aliases={first + i: results + i for i in range(len(through))},
            compiler_params=pltpu.CompilerParams(vmem_limit_bytes=VMEM_BYTES),
            cost_estimate=pl.CostEstimate(flops=flops, bytes_accessed=0, transcendentals=0),
            **rest,
        )(*args, *skipped)
        self.last = (outs[0],)
        return outs


def hold(call, arrays, after=()):
    def body(out):
        out[...] = jnp.zeros_like(out)

    return call(body, (), [], [whole(8, LANE)], [shaped((8, LANE))], after, arrays, grid=(1,), name="hold")[1:]


def shaped(shape, dtype=f32):
    return jax.ShapeDtypeStruct(tuple(shape), dtype)


def whole(*shape):
    return pl.BlockSpec(shape, lambda *ids: (0,) * len(shape))


def rows_at(rows, width):
    return pl.BlockSpec((rows, width), lambda i: (i, 0))


SMEM = pl.BlockSpec(memory_space=pltpu.SMEM)


def dct_table(size):
    row = np.arange(size)[:, None]
    col = np.arange(size)[None, :]
    table = np.cos(math.pi * (col + 0.5) * row / size) * math.sqrt(2.0 / size)
    table[0] *= math.sqrt(0.5)
    return table.astype(np.float32)


def expand_table(head):
    half = ROT // 2
    table = np.zeros((ROT, 3 * LANE), np.float32)
    for lane in range(LANE):
        place = lane % head
        if place < half:
            table[place, lane] = 1.0
            table[half + place, LANE + lane] = -1.0
        elif place < ROT:
            table[place - half, lane] = 1.0
            table[place, 2 * LANE + lane] = 1.0
    return np.concatenate([table] * 3, axis=0)


def ends_of(lengths):
    ends, total = [], jnp.int32(0)
    for j in range(lengths.shape[0]):
        total = total + lengths[j]
        ends.append(total)
    return ends


def seq_start(ends, place):
    start = jnp.zeros_like(place)
    for end in ends:
        start = jnp.where(place >= end, end, start)
    return start


def iota(shape, dim):
    return lax.broadcasted_iota(jnp.int32, shape, dim)


def head_block(head, rows, cols):
    return iota((rows, cols), 0) // head == iota((rows, cols), 1) // head


def turn_tables(cs, expand, head, width):
    wide = tn(cs, expand)
    lane = iota((1, LANE), 1) % head
    cosine = wide[:, :LANE] + jnp.where(lane < ROT, 0.0, 1.0)
    times = width // LANE
    return tuple(
        beside(*[part] * times) for part in (cosine, wide[:, LANE : 2 * LANE], wide[:, 2 * LANE :])
    )


def turn(value, tables, sign):
    cosine, up, down = tables
    width = value.shape[1]
    half = ROT // 2
    moved = pltpu.roll(value, width - half, 1) * up + pltpu.roll(value, half, 1) * down
    return value * cosine + moved if sign > 0 else value * cosine - moved


def own_half(head, rows):
    return iota((rows, LANE), 1) // head == iota((rows, LANE), 0) // head % 2


def pairs_of(width):
    return [slice(p, p + LANE) for p in range(0, width, LANE)]


def outer_pairs(left, right, other):
    return below(
        *[tn(left[:, p], beside(right[:, p], other[:, p])) for p in pairs_of(left.shape[1])]
    )


def masked_state(full, head):
    half = own_half(head, full.shape[0])
    return jnp.where(beside(half, half), full, 0.0)


def fold_state(full, head):
    full = masked_state(full, head)
    return full[:, :LANE] + pltpu.roll(full[:, LANE:], LANE // 2, 1)


def unfold_state(packed, head):
    return masked_state(beside(packed, pltpu.roll(packed, LANE // 2, 1)), head)


def deal(outs, order, low, write):
    mine = lax.axis_index("batch") // low
    first, second, third = (1 << bit for bit in order)
    wanted = [base + i * third for base in (first + second, first, second, 0) for i in range(2)]
    slots = [(out, i) for out in outs for i in range(out.shape[0])]
    for (out, i), block in zip(slots, wanted):
        write(out, i, pl.multiple_of((mine ^ block) * LANE, LANE))


def feed_step(normed, c, up_w, up_b, down_w, hidden_o, gpre_o, ub_o, down_acc, up_acc):
    rows, width = hidden_o.shape
    pre = nn(normed, up_w[...]) + up_b[...]
    grad_hidden = nt(c, down_w[...])
    phi = 0.5 + 0.5 * lax.erf(pre * HALF_ROOT)
    hidden = (pre * phi).astype(bf16)
    hidden_o[...] = hidden
    down_acc[...] += tn(hidden, c)
    slope = phi + pre * jnp.exp(-0.5 * pre * pre) * GAUSS
    gpre = (grad_hidden * slope).astype(bf16)
    gpre_o[...] = gpre
    up_acc[...] += tn(normed, gpre)
    ub_o[...] += jnp.sum(gpre.astype(f32).reshape(rows // 8, 8, width), axis=0)


def clear(*refs):
    for ref in refs:
        ref[...] = jnp.zeros_like(ref)


def write_down(out, i, at, down_acc):
    out[i, : down_acc.shape[0], :] = down_acc[:, pl.ds(at, LANE)]


def write_up(out, i, at, up_acc):
    width = up_acc.shape[1]
    first = out.shape[1] - width
    for j in range(0, width, LANE):
        out[i, first + j : first + j + LANE, :] = up_acc[pl.ds(at, LANE), j : j + LANE]


def feed_specs(tokens, model, units, part):
    first, quarters = PARTS[part]
    width = units // 4 * quarters
    part = first // quarters
    ins = [
        pl.BlockSpec((model, width), lambda i: (0, part)),
        pl.BlockSpec((1, width), lambda i: (0, part)),
        pl.BlockSpec((width, model), lambda i: (part, 0)),
        rows_at(ROWS, model),
    ]
    outs = [rows_at(ROWS, width)] * 2 + [whole(8, width)]
    shapes = [shaped((tokens, width), bf16)] * 2 + [shaped((8, width))]
    scratch = [pltpu.VMEM((width, model), f32), pltpu.VMEM((model, width), f32)]
    return width, ins, outs, shapes, scratch


def feed(call, orders, low, normed, up_w, up_b, down_w, cot, **rest):
    tokens, model = cot.shape
    width, ins, outs, shapes, scratch = feed_specs(tokens, model, up_w.shape[1], 1)
    firsts, piece = shaped((4, width, LANE)), shaped((2, width, LANE))
    pieces_out = [firsts, piece, piece] * 2

    def body(normed, up_w, up_b, down_w, cot, hidden_o, gpre_o, ub_o, *refs):
        *pieces, down_acc, up_acc = refs
        step = pl.program_id(0)

        @pl.when(step == 0)
        def _():
            clear(down_acc, up_acc, ub_o)

        feed_step(
            normed[...], cot[...], up_w, up_b, down_w, hidden_o, gpre_o, ub_o, down_acc, up_acc
        )

        @pl.when(step == pl.num_programs(0) - 1)
        def _():
            deal(pieces[:3], orders[0], low, lambda *at: write_down(*at, down_acc))
            deal(pieces[3:], orders[1], low, lambda *at: write_up(*at, up_acc))

    return call(
        body,
        (normed, up_w, up_b, down_w, cot),
        [rows_at(ROWS, model), *ins],
        outs + [whole(*a.shape) for a in pieces_out],
        shapes + pieces_out,
        **rest,
        grid=(tokens // ROWS,),
        scratch_shapes=scratch,
        name="feed_forward",
    )


def take_columns(w_in, head, heads, part):
    return beside(*[w_in[:, (3 * h + part) * head : (3 * h + part + 1) * head] for h in range(heads)])


def features(part, tables, basis, head, feats):
    width = part.shape[1]
    turned = turn(part.astype(f32), tables, 1)
    square = (turned * turned).astype(bf16)
    ones = jnp.where(head_block(head, width, width), 1.0 / (2.0 * math.sqrt(head)), 0.0).astype(bf16)
    argument = exact3(nn, two(turned), basis) - nn(square, ones)
    return turned.astype(bf16), (jnp.exp(argument) * (1.0 / math.sqrt(feats))).astype(bf16)


def rotary_table(ends, first_pos, rows, tokens, out):
    half = ROT // 2
    order = iota((half, rows), 0)
    frequency = jnp.zeros((half, rows), f32)
    for j in range(half):
        value = float(np.float32(10000.0) ** np.float32(-2.0 * j / ROT))
        frequency = jnp.where(order == j, value, frequency)
    for i in range(tokens // rows):
        place = first_pos + i * rows + iota((half, rows), 1)
        angle = (place - seq_start(ends, place)).astype(f32) * frequency
        circle = below(jnp.cos(angle), jnp.sin(angle))
        high, rest = two(circle)
        middle, lowest = two(circle - high.astype(f32))
        out[i] = below(high, middle, lowest)


def front(
    call, head, lengths, x, gain, shift, up_w, up_b, down_w, cot, qkv_w, qkv_b, expand,
    samples, dct_t,
):
    tokens, model = x.shape
    width = qkv_w.shape[1] // 3
    heads = width // head
    feats = samples.shape[0]
    blocks = tokens // ROWS
    table = (blocks, expand.shape[0], ROWS)
    part, ins, outs, shapes, scratch = feed_specs(tokens, model, up_w.shape[1], 0)
    piece = shaped((model // LANE, 2 * part, LANE))

    def body(
        lengths, x, gain, shift, up_w, up_b, down_w, cot, qkv_w, qkv_b, expand, samples, dct_t,
        normed_o, cb_o, kf_o, v_o, kt_o, w_o, b_o, basis_o, cs_o, state_o, hidden_o, gpre_o, ub_o, piece_o,
        down_acc, up_acc, w_s, b_s, basis_s, cs_s, state_s,
    ):
        step = pl.program_id(0)
        ends = ends_of(lengths)
        first_pos = lax.axis_index("batch") * tokens
        start_last = seq_start(ends, first_pos + tokens - 1)

        @pl.when(step == 0)
        def _():
            clear(down_acc, up_acc, ub_o, cb_o, state_s)
            for part in range(3):
                to = slice(part * width, (part + 1) * width)
                w_s[:, to] = take_columns(qkv_w, head, heads, part)
                b_s[:, to] = take_columns(qkv_b, head, heads, part)
            basis = lax.dot_general(
                dct_t[...], samples[...], (((1,), (1,)), ((), ())),
                preferred_element_type=f32, precision=lax.Precision.HIGHEST,
            )
            basis = basis * (1.0 / head**0.25)
            wide = below(*[beside(*[basis] * heads)] * heads)
            basis_s[...] = jnp.where(head_block(head, width, width), wide, 0.0)
            basis_o[...] = basis_s[...]
            w_o[...] = w_s[...]
            b_o[...] = b_s[...]
            rotary_table(ends, first_pos, ROWS, tokens, cs_s)
            cs_o[...] = cs_s[...]

        xf = x[...].astype(f32)
        centered = xf - jnp.mean(xf, axis=1, keepdims=True)
        inv = lax.rsqrt(jnp.mean(centered * centered, axis=1, keepdims=True) + epsilon)
        normed = (centered * inv * gain[...] + shift[...]).astype(bf16)
        normed_o[...] = normed
        c = cot[...]
        cb_o[...] += jnp.sum(c.astype(f32).reshape(ROWS // 8, 8, model), axis=0)
        feed_step(normed, c, up_w, up_b, down_w, hidden_o, gpre_o, ub_o, down_acc, up_acc)

        projected = (nn(normed, w_s[:, width:]) + b_s[:, width:]).astype(bf16)
        tables = turn_tables(cs_s[step], expand[...], head, width)
        k_turn, k_feat = features(projected[:, :width], tables, two(basis_s[...]), head, feats)
        value = projected[:, width:]
        kf_o[...], v_o[...], kt_o[...] = k_feat, value, k_turn
        place = first_pos + step * ROWS + iota((ROWS, 1), 0)
        tail = jnp.where(place >= start_last, 1.0, 0.0).astype(bf16)
        state_s[...] += outer_pairs(k_feat * tail, value, jnp.ones_like(value))

        @pl.when(step == pl.num_programs(0) - 1)
        def _():
            state_o[...] = fold_state(state_s[...], head)
            for i in range(piece.shape[0]):
                write_down(piece_o, i, i * LANE, down_acc)
                write_up(piece_o, i, i * LANE, up_acc)

    narrow = shaped((tokens, width), bf16)
    return call(
        body,
        (lengths, x, gain, shift, up_w, up_b, down_w, cot, qkv_w, qkv_b, expand, samples, dct_t),
        [SMEM, rows_at(ROWS, model), whole(1, model), whole(1, model), *ins]
        + [whole(*a.shape) for a in (qkv_w, qkv_b, expand, samples, dct_t)],
        [rows_at(ROWS, model), whole(8, model), *[rows_at(ROWS, width)] * 3]
        + [whole(model, 3 * width), whole(1, 3 * width), whole(width, width), whole(*table)]
        + [whole(width, LANE), *outs]
        + [whole(*piece.shape)],
        [shaped((tokens, model), bf16), shaped((8, model)), *[narrow] * 3]
        + [shaped((model, 3 * width), bf16), shaped((1, 3 * width)), shaped((width, width))]
        + [shaped(table, bf16)]
        + [shaped((width, LANE)), *shapes, piece],
        grid=(blocks,),
        scratch_shapes=[
            *scratch,
            pltpu.VMEM((model, 3 * width), bf16),
            pltpu.VMEM((1, 3 * width), f32),
            pltpu.VMEM((width, width), f32),
            pltpu.VMEM(table, bf16),
            pltpu.VMEM((width, 2 * LANE), f32),
        ],
        name="front",
    )


def project_queries(call, head, feats, normed, w, b, expand, basis, cs, cot, out_w):
    tokens, model = normed.shape
    width = out_w.shape[0]

    def body(normed, w, b, expand, basis, cs, cot, out_w, qf_o, qt_o, ga_o):
        projected = (nn(normed[...], w[...]) + b[...]).astype(bf16)
        ga_o[...] = nt(cot[...], out_w[...])
        tables = turn_tables(cs[0], expand[...], head, width)
        qt_o[...], qf_o[...] = features(projected, tables, two(basis[...]), head, feats)

    return call(
        body,
        (normed, w, b, expand, basis, cs, cot, out_w),
        [
            rows_at(ROWS, model),
            whole(model, width),
            whole(1, width),
            whole(*expand.shape),
            whole(*basis.shape),
            pl.BlockSpec((1,) + cs.shape[1:], lambda i: (i, 0, 0)),
            rows_at(ROWS, model),
            whole(*out_w.shape),
        ],
        [rows_at(ROWS, width)] * 3,
        [shaped((tokens, width), bf16), shaped((tokens, width), bf16), shaped((tokens, width))],
        grid=(tokens // ROWS,),
        name="project_queries",
    )


def swapped(value, axis, distance):
    size = lax.axis_size(axis)
    return lax.ppermute(value, axis, [(i, i ^ distance) for i in range(size)])


def joined(forward, lengths, tokens, base, entered, own, came):
    ends = ends_of(lengths)
    here = lax.axis_index("batch")
    count, size = 1, 2
    group = (here >> (base + count)) << (base + count)
    mine = (here >> base) & (size - 1)
    group_end = (group + (size << base)) * tokens
    total = jnp.zeros_like(own)
    entered = total if entered is None else entered
    for m in range(size):
        part = came if m else own
        other = mine ^ m
        if forward:
            edge = (group + ((other + 1) << base)) * tokens
            enters = (other < mine) & (seq_start(ends, here * tokens - 1) < edge)
            counts = seq_start(ends, group_end - 1) < edge
        else:
            start = seq_start(ends, (group + (other << base)) * tokens - 1)
            enters = (other > mine) & (start < (here + 1) * tokens)
            counts = start < group * tokens
        if m:
            entered = entered + jnp.where(enters, part, 0.0)
        total = total + jnp.where(counts, part, 0.0)
    return entered, total


def join_states(call, forward, tokens, base, lengths, entered, own, came, **rest):
    given = [own, came] if entered is None else [entered, own, came]

    def body(lengths, *refs):
        *ins, entered_o, total_o = refs
        values = [r[...] for r in ins]
        if entered is None:
            values = [None, *values]
        entered_o[...], total_o[...] = joined(
            forward, lengths, tokens, base, *values
        )

    spec = whole(*own.shape)
    return call(
        body,
        (lengths, *given),
        [SMEM] + [spec] * len(given),
        [spec, spec],
        [shaped(own.shape)] * 2,
        **rest,
        grid=(1,),
        name="join_states",
    )


def turned_grad(grad_feat, feat, turned, basis, tables, head, width):
    weighted = (grad_feat * feat.astype(f32)).astype(bf16)
    ones = jnp.where(head_block(head, width, width), 1.0 / math.sqrt(head), 0.0).astype(bf16)
    grad = nt(beside(weighted, weighted), beside(*basis)) - nn(weighted, ones) * turned.astype(f32)
    return turn(grad, tables, -1).astype(bf16)


def attend_kernel(
    head, tokens, per_step, base, lengths, qf, kf, v, qt, ga, cs, expand, basis_i,
    normed, cot, hidden0, hidden1, down_w, out_w, entered_i, own_i, came_i,
    gq_o, gk_o, gv_o, back_o, total_o, qb_o, keep_o, far0_o, far1_o, near_o, *refs,
):
    piece_o, state_s, q_acc, o_acc, total_s = refs
    step = pl.program_id(0)
    width = qf.shape[1]
    heads = width // head
    ends = ends_of(lengths)
    first_pos = lax.axis_index("batch") * tokens

    @pl.when(step == 0)
    def _():
        entered, _ = joined(
            True, lengths, tokens, base, entered_i[...], own_i[...], came_i[...]
        )
        state_s[...] = unfold_state(entered, head)
        q_acc[...] = jnp.zeros_like(q_acc)
        o_acc[...] = jnp.zeros_like(o_acc)
        total_s[...] = jnp.zeros_like(total_s)
        qb_o[...] = jnp.zeros_like(qb_o)

    basis = two(basis_i[...])
    block = head_block(head, width, width)
    ones = jnp.where(block, 1.0, 0.0).astype(bf16)
    lanes = [jnp.where(iota((1, width), 1) // head == h, 1.0, 0.0).astype(bf16) for h in range(heads)]
    state = state_s[...]
    total = total_s[...]
    part = hidden0.shape[1]
    subs = range(per_step)
    ats = [slice(sub * CHUNK, (sub + 1) * CHUNK) for sub in subs]
    row = iota((CHUNK, 1), 0)
    col = iota((CHUNK, CHUNK), 1)
    causal = col <= iota((CHUNK, CHUNK), 0)
    windows, carries, states, live = [], [], [], []
    for sub, at in zip(subs, ats):
        begin = first_pos + (step * per_step + sub) * CHUNK
        last = seq_start(ends, begin + CHUNK - 1)
        start = seq_start(ends, begin + row)
        windows.append(causal & (col + begin >= start))
        carries.append(jnp.where(start < begin, 1.0, 0.0))
        live.append(jnp.where(seq_start(ends, begin - 1) < first_pos, 1.0, 0.0))
        states.append(two(state))
        tail = jnp.where(begin + row >= last, 1.0, 0.0).astype(bf16)
        retain = jnp.where(last < begin, 1.0, 0.0)
        value = v[at, :]
        added = outer_pairs(kf[at, :] * tail, value, jnp.ones_like(value))
        state = retain * state + masked_state(added, head)
    scores = [
        [jnp.where(window, nt(qf[at, :] * lane, kf[at, :]), 0.0).astype(bf16) for lane in lanes]
        for at, window in zip(ats, windows)
    ]
    outward = nn(hidden1[...], down_w[:-part]) + nn(hidden0[...], down_w[-part:])
    q_carries = [qf[at, :] * c.astype(bf16) for at, c in zip(ats, carries)]
    attends, overs, mixes = [], [], []
    for sub, at in zip(subs, ats):
        nums, dens = [], []
        for p, pair in enumerate(pairs_of(width)):
            mine = range(p * LANE // head, (p + 1) * LANE // head)
            right = [
                beside(v[at, pair] * lanes[h][:, pair], jnp.broadcast_to(lanes[h][:, pair], (CHUNK, LANE)))
                for h in mine
            ]
            carry = q_carries[sub][:, pair]
            sums = nn(
                beside(*[scores[sub][h] for h in mine], carry, carry),
                below(*right, states[sub][0][pair, :], states[sub][1][pair, :]),
            )
            nums.append(sums[:, :LANE])
            dens.append(sums[:, LANE:])
        overs.append(1.0 / beside(*dens))
        attends.append(beside(*nums) * overs[sub])
        mixes.append(attends[sub].astype(bf16))
    g_nums = [(ga[at, :] * over).astype(bf16) for at, over in zip(ats, overs)]
    g_dens = []
    for g_num, attended in zip(g_nums, attends):
        product = two(g_num.astype(f32) * attended)
        g_dens.append(-nn(beside(*product), below(ones, ones)))
    g_heads = [[g_num * lane for lane in lanes] for g_num in g_nums]
    mixing = [
        [
            jnp.where(
                windows[sub], nt(g_heads[sub][h], v[at, :]) + g_dens[sub][:, h * head : h * head + 1], 0.0
            ).astype(bf16)
            for h in range(heads)
        ]
        for sub, at in zip(subs, ats)
    ]
    grad_fqs = []
    for sub, at in zip(subs, ats):
        den_two = two(g_dens[sub] * (2.0 / head))
        den_both = jnp.where(iota((1, width), 1) % head < head // 2, den_two[0], den_two[1])
        from_state = []
        for pair in pairs_of(width):
            left = beside(g_nums[sub][:, pair], den_both[:, pair])
            from_state.append(
                nt(beside(left, left), beside(states[sub][0][pair, :], states[sub][1][pair, :]))
            )
        grad_fqs.append(
            carries[sub] * beside(*from_state)
            + nn(beside(*mixing[sub]), below(*[kf[at, :] * lane for lane in lanes]))
        )
    gqs = []
    for sub, at in zip(subs, ats):
        tables = turn_tables(cs[0, :, at], expand[...], head, width)
        gqs.append(turned_grad(grad_fqs[sub], qf[at, :], qt[at, :], basis, tables, head, width))
    for sub, at in zip(subs, ats):
        gk_o[at, :] = tn(below(*mixing[sub]), below(*[qf[at, :] * lane for lane in lanes]))
        gv_o[at, :] = tn(below(*scores[sub]), below(*g_heads[sub]))
        back = fold_state(outer_pairs(q_carries[sub], g_nums[sub], g_dens[sub].astype(bf16)), head)
        back_o[sub] = back
        total = total + live[sub] * back
    gq = below(*gqs)
    gq_o[...] = gq
    qb_o[...] += jnp.sum(gq.astype(f32).reshape(per_step * CHUNK // 8, 8, width), axis=0)
    q_acc[...] += tn(normed[...], gq)
    o_acc[...] += tn(below(*mixes), cot[...])
    state_s[...] = state
    total_s[...] = total
    outward = outward + nn(below(*mixes), out_w[...])
    by_core(step, outward, keep_o, far0_o, far1_o, near_o)

    @pl.when(step == pl.num_programs(0) - 1)
    def _():
        total_o[...] = total

        for i in range(piece_o.shape[0]):
            write_down(piece_o, i, i * LANE, o_acc)
            write_up(piece_o, i, i * LANE, q_acc)


def by_core(share, value, keep, far0, far1, near):
    core, chip = branch_place()
    other, mine = share & 1 != core, share >> 1 == chip

    @pl.when(jnp.logical_not(other))
    def _():
        keep[0] = value

    @pl.when(other & jnp.logical_not(mine))
    def _():
        far0[...] = value[: ROWS // 2]
        far1[...] = value[ROWS // 2 :]

    @pl.when(other & mine)
    def _():
        near[...] = value


def attend(
    call, head, base, lengths, qf, kf, v, qt, ga, cs, expand, basis, normed, cot,
    hidden0, hidden1, down_w, out_w, entered, own, came, **rest,
):
    tokens, width = qf.shape
    model = cot.shape[1]
    per_step = ROWS // CHUNK
    chunks = tokens // CHUNK
    part = hidden0.shape[1]
    piece = shaped((model // LANE, 2 * width, LANE))
    chip = pl.BlockSpec((1, ROWS, model), lambda i: (i >> 1 ^ (1 - branch_place()[1]), 0, 0))
    sent = [shaped((rows, model)) for rows in (ROWS // 2, ROWS // 2, ROWS)]
    row = rows_at(ROWS, width)
    packed = whole(width, LANE)

    def body(*refs):
        attend_kernel(head, tokens, per_step, base, *refs)

    return call(
        body,
        (lengths, qf, kf, v, qt, ga, cs, expand, basis, normed, cot, hidden0, hidden1, down_w, out_w)
        + (entered, own, came),
        [
            SMEM,
            *[row] * 5,
            pl.BlockSpec((1,) + cs.shape[1:], lambda i: (i, 0, 0)),
            whole(*expand.shape),
            whole(width, width),
            rows_at(ROWS, model),
            rows_at(ROWS, model),
            rows_at(ROWS, part),
            rows_at(ROWS, hidden1.shape[1]),
            whole(*down_w.shape),
            whole(*out_w.shape),
            *[packed] * 3,
        ],
        [
            *[row] * 3,
            pl.BlockSpec((per_step, width, LANE), lambda i: (i, 0, 0)),
            packed,
            whole(8, width),
            chip,
            *[whole(*a.shape) for a in sent],
            whole(*piece.shape),
        ],
        [
            shaped((tokens, width), bf16),
            shaped((tokens, width)),
            shaped((tokens, width)),
            shaped((chunks, width, LANE)),
            shaped((width, LANE)),
            shaped((8, width)),
            shaped((tokens // ROWS // 2, ROWS, model)),
            *sent,
            piece,
        ],
        **rest,
        grid=(tokens // ROWS,),
        scratch_shapes=[
            pltpu.VMEM((width, 2 * LANE), f32),
            pltpu.VMEM((model, width), f32),
            pltpu.VMEM((width, model), f32),
            pltpu.VMEM((width, LANE), f32),
        ],
        name="attend",
        flops=COST_ATTEND,
    )


def branch_place():
    here = lax.axis_index("branch")
    return here & 1, here >> 1


def keys(
    call, head, order, low, base, lengths, kf, v, kt, gk, gv, back, cs, expand, basis, normed,
    entered, own, came, **rest,
):
    tokens, width = kf.shape
    model = normed.shape[1]
    chunks, per_step = tokens // CHUNK, ROWS // CHUNK
    row = lambda n: rows_at(ROWS, n)
    packed = whole(width, LANE)
    firsts, piece = shaped((4, 2 * width, LANE)), shaped((2, 2 * width, LANE))
    acc_shape = (model, 2 * width)

    def body(
        lengths, kf, v, kt, gk, gv, back, cs, expand, basis_i, normed, entered_i, own_i, came_i,
        gkv_o, kvb_o, *refs,
    ):
        *pieces, acc, state_s = refs
        step = pl.program_id(0)
        ends = ends_of(lengths)
        first_pos = lax.axis_index("batch") * tokens

        @pl.when(step == 0)
        def _():
            clear(kvb_o, acc)
            state, _ = joined(
                False, lengths, tokens, base, entered_i[...], own_i[...], came_i[...]
            )
            for chunk in reversed(range(chunks)):
                state_s[chunk] = state
                begin = first_pos + chunk * CHUNK
                last = seq_start(ends, begin + CHUNK - 1)
                state = back[chunk] + jnp.where(last < begin, state, 0.0)

        basis = two(basis_i[...])
        tables = turn_tables(cs[0], expand[...], head, width)
        share = jnp.full((CHUNK, LANE), 1.0 / head, bf16)
        heres = [slice(sub * CHUNK, (sub + 1) * CHUNK) for sub in range(per_step)]
        tails, states = [], []
        for sub in range(per_step):
            begin = first_pos + (step * per_step + sub) * CHUNK
            last = seq_start(ends, begin + CHUNK - 1)
            tails.append(jnp.where(begin + iota((CHUNK, 1), 0) >= last, 1.0, 0.0))
            states.append(two(unfold_state(state_s[step * per_step + sub], head)))
        grad_fks, grad_vs = [], []
        for here, tail, state in zip(heres, tails, states):
            to_k, to_v = [], []
            for pair in pairs_of(width):
                high, low_ = state[0][pair, :], state[1][pair, :]
                left = beside(v[here, pair], share)
                to_k.append(nt(beside(left, left), beside(high, low_)))
                to_v.append(
                    nn(beside(kf[here, pair], kf[here, pair]), below(high[:, :LANE], low_[:, :LANE]))
                )
            grad_fks.append(gk[here, :] + tail * beside(*to_k))
            grad_vs.append((gv[here, :] + tail * beside(*to_v)).astype(bf16))
        grad_k = turned_grad(below(*grad_fks), kf[...], kt[...], basis, tables, head, width)
        grads = [beside(grad_k, below(*grad_vs))]
        both = below(*grads)
        gkv_o[...] = both
        kvb_o[...] += jnp.sum(both.astype(f32).reshape(ROWS // 8, 8, 2 * width), axis=0)
        acc[...] += tn(normed[...], both)

        @pl.when(step == pl.num_programs(0) - 1)
        def _():
            deal(pieces, order, low, lambda *spot: write_up(*spot, acc))

    pieces = [firsts, piece, piece]
    return call(
        body,
        (lengths, kf, v, kt, gk, gv, back, cs, expand, basis, normed, entered, own, came),
        [SMEM, *[row(width)] * 5]
        + [whole(*back.shape)]
        + [pl.BlockSpec((1,) + cs.shape[1:], lambda i: (i, 0, 0)), whole(*expand.shape)]
        + [whole(width, width), row(model), *[packed] * 3],
        [row(2 * width), whole(8, 2 * width), *[whole(*a.shape) for a in pieces]],
        [shaped((tokens, 2 * width), bf16), shaped((8, 2 * width)), *pieces],
        **rest,
        grid=(tokens // ROWS,),
        scratch_shapes=[pltpu.VMEM(acc_shape, f32), pltpu.VMEM((chunks, width, LANE), f32)],
        name="keys",
    )


def inward(call, far, x, gpre0, gpre1, gq, gkv, up_w, qkv_w, **rest):
    tokens, model = x.shape
    part = gpre0.shape[1]

    def at(i):
        core, chip = branch_place()
        return 2 * (1 - chip) + i if far else 2 * chip + (i ^ (1 - core))

    row = lambda a: pl.BlockSpec((ROWS, a.shape[1]), lambda i: (at(i), 0))

    def body(x, gpre0, gpre1, gq, gkv, up_w, qkv_w, *refs):
        *outs, gain_o, shift_o = refs
        step = pl.program_id(0)

        @pl.when(step == 0)
        def _():
            clear(gain_o, shift_o)

        grad = nt(gpre1[...], up_w[:, :-part]) + nt(gpre0[...], up_w[:, -part:])
        grad = grad + nt(beside(gq[...], gkv[...]), qkv_w[...])
        if far:
            outs[0][0] = grad
        else:

            @pl.when(step == 0)
            def _():
                outs[0][...] = grad[: ROWS // 2]
                outs[1][...] = grad[ROWS // 2 :]

            @pl.when(step == 1)
            def _():
                outs[2][...] = grad

        xf = x[...].astype(f32)
        centered = xf - jnp.mean(xf, axis=1, keepdims=True)
        unit = centered * lax.rsqrt(jnp.mean(centered * centered, axis=1, keepdims=True) + epsilon)
        gain_o[...] += jnp.sum((grad * unit).reshape(ROWS // 8, 8, model), axis=0)
        shift_o[...] += jnp.sum(grad.reshape(ROWS // 8, 8, model), axis=0)

    if far:
        specs = [pl.BlockSpec((1, ROWS, model), lambda i: (i, 0, 0))]
        shapes = [shaped((2, ROWS, model))]
    else:
        shapes = [shaped((rows, model)) for rows in (ROWS // 2, ROWS // 2, ROWS)]
        specs = [whole(*a.shape) for a in shapes]
    return call(
        body,
        (x, gpre0, gpre1, gq, gkv, up_w, qkv_w),
        [row(a) for a in (x, gpre0, gpre1, gq, gkv)] + [whole(*up_w.shape), whole(*qkv_w.shape)],
        specs + [whole(8, model)] * 2,
        shapes + [shaped((8, model))] * 2,
        **rest,
        grid=(2,),
        name="inward",
    )


def finish_small(call, one, other, sizes):
    shapes = [shaped((size // LANE, LANE)) for size in sizes]

    def body(one, other, *outs):
        row = 0
        for out in outs:
            out[...] = one[row : row + out.shape[0], :] + other[row : row + out.shape[0], :]
            row += out.shape[0]

    parts = call(
        body,
        (one, other),
        [whole(*one.shape)] * 2,
        [whole(*a.shape) for a in shapes],
        shapes,
        grid=(1,),
        name="finish_small",
    )
    return [part.reshape(-1) for part in parts]


def block_of(array, count, at):
    shape = (count,) + array.shape[1:]
    return pl.BlockSpec(shape, lambda i: (at() if callable(at) else at,) + (0,) * (len(shape) - 1))


def sums_of(call, *jobs, stack=False, **rest):
    arrays, specs, shapes = [], [], []
    for job in jobs:
        for array, count, at in job:
            arrays.append(array)
            specs.append(block_of(array, count, at))
        shapes.append(shaped((count,) + array.shape[1:]))
    counts = [a.shape[0] for a in shapes]
    if stack:
        shapes = [shaped((sum(counts),) + shapes[0].shape[1:])]
    outs = [whole(*a.shape) for a in shapes]

    def body(*refs):
        ins, results = refs[: len(arrays)], refs[len(arrays) :]
        start = 0
        for i, job in enumerate(jobs):
            mine, ins = ins[: len(job)], ins[len(job) :]
            value = sum(r[...] for r in mine[1:]) + mine[0][...]
            if stack:
                results[0][start : start + counts[i]] = value
                start += counts[i]
            else:
                results[i][...] = value

    return call(body, arrays, specs, outs, shapes, grid=(1,), name="sums", **rest)


def whole_of(array):
    return array, array.shape[0], 0


def finish_feed(call, one, down, up, **rest):
    args, specs = [one], [block_of(one, 1, 0)]
    for piece, first, two_came, (three_came, which) in (down, up):
        args += [piece[2], first, two_came, three_came]
        specs += [block_of(a, 1, at) for a, at in zip(args[-4:], (0, 2, 0, which))]
    widths = [down[0][2].shape[1], one.shape[1] // 2]

    def body(one, *refs):
        down_o, up_o = refs[-2:]
        values = []
        for a, b, c, d in (refs[:4], refs[4:8]):
            values.append((a[0] + b[0]) + (c[0] + d[0]))
        downs = (values[0], one[0, : widths[1]])
        ups = (values[1], one[0, widths[1] :])
        for down, up, start, width in zip(downs, ups, (0, widths[0]), widths):
            down_o[start : start + width, :] = down
            for j in range(0, width, LANE):
                up_o[:, start + j : start + j + LANE] = up[j : j + LANE, :]

    shapes = [shaped((sum(widths), LANE)), shaped((LANE, sum(widths)))]
    return call(
        body, args, specs, [whole(*a.shape) for a in shapes], shapes, grid=(1,), name="finish_feed", **rest
    )


def finish_heads(call, head, one, key_val, **rest):
    piece, first, two_came, three_came = key_val
    args = [one, piece[2], first, two_came, three_came]
    specs = [block_of(a, 1, at) for a, at in zip(args, (0, 0, 2, 0, 0))]
    width = one.shape[1] // 2
    heads = width // head

    def body(one, a, b, c, d, out_o, qkv_o):
        value = (a[0] + b[0]) + (c[0] + d[0])
        out_o[...] = one[0, :width]
        columns = []
        for rows in (one[0, width:], value[:width], value[width:]):
            columns.append(beside(*[rows[j * LANE : (j + 1) * LANE] for j in range(width // LANE)]))
        qkv_o[...] = beside(*[p[:, h * head : (h + 1) * head] for h in range(heads) for p in columns])

    shapes = [shaped((width, LANE)), shaped((LANE, 3 * width))]
    return call(
        body, args, specs, [whole(*a.shape) for a in shapes], shapes, grid=(1,), name="finish_heads", **rest
    )


def far_sums(call, keep, came, **rest):
    rows, model = CHUNK, keep.shape[2]
    steps = keep.shape[1] // rows
    halves = isinstance(came, tuple)
    spec = lambda at: pl.BlockSpec((1, rows, model), lambda i: (at, i, 0))

    def body(keep, *refs):
        *came, out = refs
        if halves:
            out[...] = keep[0] + jnp.where(pl.program_id(0) == 0, came[0][...], came[1][...])
        else:
            out[...] = keep[0] + came[0][0]

    return call(
        body,
        (keep, *came) if halves else (keep, came),
        [spec(0), *([whole(rows, model)] * 2 if halves else [spec(1)])],
        [rows_at(rows, model)],
        [shaped(keep.shape[1:])],
        grid=(steps,),
        name="far_sums",
        **rest,
    )


def finish_specs(share, model):
    steps = share // CHUNK
    own = pl.BlockSpec((CHUNK, model), lambda i: (lax.axis_index("branch") * steps + i, 0))
    return own, rows_at(CHUNK, model), steps


def finish_output(call, x, keep, came_core, came_chip, bias):
    share, model = came_chip.shape
    own, row, steps = finish_specs(share, model)

    def body(x, keep, core, chip, bias, out):
        total = (keep[0] + core[...]) + chip[...]
        out[...] = (x[...].astype(f32) + total + bias[...]).astype(bf16)

    return call(
        body,
        (x, keep, came_core, came_chip, bias),
        [own, pl.BlockSpec((1, CHUNK, model), lambda i: (1, i, 0)), row, row, whole(1, model)],
        [row],
        [shaped((share, model), bf16)],
        grid=(steps,),
        name="finish_output",
    )[0]


def finish_input(call, x, cot, gain, keep, came_core, came_chip, **rest):
    share, model = came_chip.shape
    own, row, steps = finish_specs(share, model)


    def body(x, cot, gain, keep, core0, core1, chip, out):
        core = jnp.where(pl.program_id(0) == 0, core0[...], core1[...])
        xf = x[...].astype(f32)
        centered = xf - jnp.mean(xf, axis=1, keepdims=True)
        inv = lax.rsqrt(jnp.mean(centered * centered, axis=1, keepdims=True) + epsilon)
        unit = centered * inv
        g = ((keep[...] + core) + chip[...]) * gain[...]
        inner = g - jnp.mean(g, axis=1, keepdims=True) - unit * jnp.mean(g * unit, axis=1, keepdims=True)
        out[...] = inv * inner + cot[...].astype(f32)

    return call(
        body,
        (x, cot, gain, keep, *came_core, came_chip),
        [own, own, whole(1, model), row, *[whole(CHUNK, model)] * 2, row],
        [row],
        [shaped((share, model))],
        **rest,
        grid=(steps,),
        name="finish_input",
    )[0]


def pack_small(call, head, branch, gains, shifts, cot, qb, kvb, ubs, **rest):
    model = cot.shape[1]
    width = qb.shape[1]
    heads = width // head
    up_width = sum(u.shape[1] for u in ubs)
    qkv_rows, up_rows = 3 * width // LANE, up_width // LANE
    starts = [0, model // LANE, 2 * model // LANE, 3 * model // LANE]
    starts.append(starts[3] + qkv_rows * branch)
    total = starts[4] + up_rows * branch

    def body(gain0, gain1, shift0, shift1, cot, qb, kvb, ub0, ub1, out):
        out[...] = jnp.zeros_like(out)
        here = lax.axis_index("branch")

        def summed(value):
            return jnp.sum(value, axis=0, keepdims=True)

        def place(row, value):
            for j in range(value.shape[1] // LANE):
                out[pl.ds(row + j, 1), :] = value[:, j * LANE : (j + 1) * LANE]

        place(starts[0], summed(gain0[...] + gain1[...]))
        place(starts[1], summed(shift0[...] + shift1[...]))
        place(starts[2], summed(cot[...]) * jnp.where(here == 0, 1.0, 0.0))
        q, kv = summed(qb[...]), summed(kvb[...])
        parts = (q, kv[:, :width], kv[:, width:])
        place(
            starts[3] + here * qkv_rows,
            beside(*[p[:, h * head : (h + 1) * head] for h in range(heads) for p in parts]),
        )
        place(starts[4] + here * up_rows, beside(summed(ub1[...]), summed(ub0[...])))

    args = (*gains, *shifts, cot, qb, kvb, *ubs)
    return call(
        body,
        args,
        [whole(*a.shape) for a in args],
        [whole(total, LANE)],
        [shaped((total, LANE))],
        grid=(1,),
        name="pack_small",
        **rest,
    )


def finish(part, dim, low):
    if low == 1:
        return part
    size = lax.axis_size("batch")
    groups = [[j * low + i for i in range(low)] for j in range(size // low)]
    return lax.psum_scatter(
        part, "batch", scatter_dimension=dim, axis_index_groups=groups, tiled=True
    )


def per_device(
    inputs, ln_gain, ln_shift, qkv_weight, qkv_bias, out_weight, up_weight, up_bias, down_weight,
    out_bias, feature_samples, lengths, cotangent,
):
    tokens, model = inputs.shape
    feats, head = feature_samples.shape
    width = out_weight.shape[0]
    batch = lax.axis_size("batch")
    branch = lax.axis_size("branch")
    low = batch // (model // LANE)
    y_first, z_first = (0, 1, 2), (1, 2, 0)
    bits = [1 << b for b in range(batch.bit_length() - 1)]
    expand = jnp.asarray(expand_table(head), bf16)
    dct_t = jnp.asarray(dct_table(head).T)
    gain = ln_gain.reshape(1, model)
    shift = ln_shift.reshape(1, model)
    up_b = up_bias.reshape(1, -1)
    qkv_b = qkv_bias.reshape(1, -1)
    call = Order()

    def send(value, order, step):
        return swapped(value, "batch", low << order[step])

    def enter(forward, own, came):
        entered = None
        for i, bit in enumerate(bits[1:]):
            entered, own = join_states(call, forward, tokens, i, lengths, entered, own, came)
            came = swapped(own, "batch", bit)
        return entered, own, came

    normed, cb, kf, value, kt, w_perm, b_perm, basis, cs, state, hidden0, gpre0, ub0, piece0 = front(
        call, head, lengths, inputs, gain, shift, up_weight, up_b, down_weight, cotangent, qkv_weight,
        qkv_b, expand, feature_samples, dct_t,
    )
    groups = [[j * low + i for j in range(batch // low)] for i in range(low)] if low > 1 else None

    def scattered(piece):
        return lax.psum_scatter(
            piece, "batch", scatter_dimension=0, axis_index_groups=groups, tiled=True
        )

    sum0 = scattered(piece0)
    came = swapped(state, "batch", 1)
    qf, qt, ga = project_queries(
        call, head, feats, normed, w_perm, b_perm, expand, basis, cs, cotangent, out_weight
    )
    states = enter(True, state, came)
    hidden1, gpre1, ub1, *pieces = feed(
        call, (y_first, z_first), low, normed, up_weight, up_b, down_weight, cotangent
    )
    down, up = pieces[:3], pieces[3:]
    down_first, up_first = send(down[0], y_first, 0), send(up[0], z_first, 0)
    gq, gk, gv, back, state, qb, out_keep, far0, far1, out_near, oq = attend(
        call, head, len(bits) - 1, lengths, qf, kf, value, qt, ga, cs, expand, basis, normed, cotangent,
        hidden0, hidden1, down_weight, out_weight, *states,
    )
    came = swapped(state, "batch", 1)
    far_core = swapped(far0, "branch", 1), swapped(far1, "branch", 1)
    (out_far,) = far_sums(call, out_keep, far_core)
    out_chip = swapped(out_far, "branch", 2)
    entered, state = join_states(call, False, tokens, 0, lengths, None, state, came)
    came = swapped(state, "batch", bits[1])
    down_2, up_2, out_near = sums_of(
        call, [whole_of(down[1]), (down_first, 2, 0)], [whole_of(up[1]), (up_first, 2, 0)],
        after=(sum0,), through=(out_near,),
    )
    out_core = swapped(out_near, "branch", 1)
    for i in range(1, len(bits) - 1):
        entered, state = join_states(call, False, tokens, i, lengths, entered, state, came)
        came = swapped(state, "batch", bits[i + 1])
    down_2, up_2, oq = hold(call, (down_2, up_2, oq))
    sum_oq = scattered(oq)
    down_2, up_2 = send(down_2, y_first, 1), send(up_2, z_first, 1)
    gkv, kvb, *kv = keys(
        call, head, y_first, low, len(bits) - 1, lengths, kf, value, kt, gk, gv, back, cs, expand,
        basis, normed, entered, state, came, flops=COST_KEYS,
    )
    kv_first = send(kv[0], y_first, 0)
    in_args = (inputs, gpre0, gpre1, gq, gkv, up_weight, w_perm)
    far, gain0, shift0 = inward(call, True, *in_args, flops=COST_FAR)
    cores = [[i, i + 1] for i in range(0, branch, 2)]
    far = lax.all_to_all(far, "branch", 0, 0, axis_index_groups=cores, tiled=True)
    (grad_far,) = far_sums(call, far, far)
    grad_chip = swapped(grad_far, "branch", 2)
    kv_2, down_3, up_3 = sums_of(
        call, [whole_of(kv[1]), (kv_first, 2, 0)],
        [(down[2], 1, 1), (down_first, 1, 3), (down_2, 1, 1)],
        [(up[2], 1, 1), (up_first, 1, 3), (up_2, 1, 1)],
    )
    kv_2, down_3, up_3 = send(kv_2, y_first, 1), send(down_3, y_first, 2), send(up_3, z_first, 2)
    near0, near1, grad_keep, gain1, shift1 = inward(call, False, *in_args, flops=COST_NEAR)
    (small,) = pack_small(
        call, head, branch, (gain0, gain1), (shift0, shift1), cb, qb, kvb, (ub0, ub1),
        after=(out_chip,),
    )
    came = swapped(small, "batch", 1)
    grad_core = swapped(near0, "branch", 1), swapped(near1, "branch", 1)
    output = finish_output(
        call, inputs, out_keep, out_core, out_chip, out_bias.reshape(1, model)
    )
    (small,) = sums_of(call, [whole_of(small), whole_of(came)])
    came = swapped(small, "batch", bits[1])
    down_sum, up_sum = finish_feed(
        call, sum0, (down, down_first, down_2, (down_3, 0)), (up, up_first, up_2, (up_3, 0))
    )
    for bit in bits[2:]:
        (small,) = sums_of(call, [whole_of(small), whole_of(came)])
        came = swapped(small, "batch", bit)
    (small,) = sums_of(call, [whole_of(small), whole_of(came)])
    came = swapped(small, "branch", 1)
    (kv_3,) = sums_of(call, [(kv[2], 1, 1), (kv_first, 1, 3), (kv_2, 1, 1)])
    kv_3 = send(kv_3, y_first, 2)
    (small,) = sums_of(call, [whole_of(small), whole_of(came)], flops=COST_END)
    came = swapped(small, "branch", 2)
    small = finish_small(call, small, came, [model, model, model, 3 * width * branch, up_bias.size * branch])
    input_grad = finish_input(
        call, inputs, cotangent, gain, grad_keep, grad_core, grad_chip, after=(sum_oq,)
    )
    out_sum, qkv_sum = finish_heads(call, head, sum_oq, (kv, kv_first, kv_2, kv_3))
    down_sum, out_sum = finish(down_sum, 1, low), finish(out_sum, 1, low)
    up_sum, qkv_sum = finish(up_sum, 0, low), finish(qkv_sum, 0, low)

    gain_grad, shift_grad, out_bias_grad, qkv_bias_grad, up_bias_grad = small
    return (
        output,
        input_grad,
        gain_grad,
        shift_grad,
        qkv_sum,
        qkv_bias_grad,
        out_sum,
        up_sum,
        up_bias_grad,
        down_sum,
        out_bias_grad,
    )


def solution(mesh):
    placed = (
        P("batch", None),
        P(),
        P(),
        P(None, "branch"),
        P("branch"),
        P("branch", None),
        P(None, "branch"),
        P("branch"),
        P("branch", None),
        P(),
        P(),
        P(),
        P("batch", None),
    )
    return jax.shard_map(
        per_device,
        mesh=mesh,
        in_specs=placed,
        out_specs=(
            P(("batch", "branch"), None),
            P(("batch", "branch"), None),
            P(),
            P(),
            P("batch", "branch"),
            P(),
            P("branch", "batch"),
            P("batch", "branch"),
            P(),
            P("branch", "batch"),
            P(),
        ),
        check_vma=False,
    )
```

```python
import math

import numpy as np

import jax
import jax.numpy as jnp
from jax import lax
from jax.experimental import pallas as pl
from jax.experimental.pallas import tpu as pltpu
from jax.sharding import PartitionSpec as P

ROT = 16
CHUNK = 256
ROWS = 512
LANE = 128
epsilon = 1e-05
f32 = jnp.float32
bf16 = jnp.bfloat16
HALF_ROOT = math.sqrt(0.5)
GAUSS = 1.0 / math.sqrt(2.0 * math.pi)
VMEM_BYTES = 64 * 2**20
STEP = 2**30
COST_FAR = 13 * STEP
COST_NEAR = 0
COST_END = 12 * STEP
COST_ATTEND = 6 * STEP
COST_KEYS = 50 * STEP
PARTS = ((3, 1), (0, 3))


def nn(a, b):
    return lax.dot_general(a, b, (((1,), (0,)), ((), ())), preferred_element_type=f32)


def nt(a, b):
    return lax.dot_general(a, b, (((1,), (1,)), ((), ())), preferred_element_type=f32)


def tn(a, b):
    return lax.dot_general(a, b, (((0,), (0,)), ((), ())), preferred_element_type=f32)


def two(value):
    high = value.astype(bf16)
    return high, (value - high.astype(f32)).astype(bf16)


def exact3(dot, a, b):
    return dot(a[0], b[0]) + (dot(a[1], b[0]) + dot(a[0], b[1]))


def beside(*parts):
    return jnp.concatenate(parts, axis=1)


def below(*parts):
    return jnp.concatenate(parts, axis=0)


class Order:
    def __init__(self):
        self.last = ()

    def __call__(
        self, body, args, in_specs, out_specs, out_shape, after=(), through=(), flops=0, **rest
    ):
        given, results = len(args), len(out_shape)
        skipped = [*self.last, *after, *through]

        def without(*refs):
            outs = refs[given + len(skipped) :]
            body(*refs[:given], *outs[:results], *outs[results + len(through) :])

        place = pl.BlockSpec(memory_space=pl.ANY)
        first = given + len(skipped) - len(through)
        outs = pl.pallas_call(
            without,
            in_specs=[*in_specs, *[place] * len(skipped)],
            out_specs=[*out_specs, *[place] * len(through)],
            out_shape=[*out_shape, *[shaped(t.shape, t.dtype) for t in through]],
            input_output_aliases={first + i: results + i for i in range(len(through))},
            compiler_params=pltpu.CompilerParams(vmem_limit_bytes=VMEM_BYTES),
            cost_estimate=pl.CostEstimate(flops=flops, bytes_accessed=0, transcendentals=0),
            **rest,
        )(*args, *skipped)
        self.last = (outs[0],)
        return outs


def hold(call, arrays, after=()):
    def body(out):
        out[...] = jnp.zeros_like(out)

    return call(body, (), [], [whole(8, LANE)], [shaped((8, LANE))], after, arrays, grid=(1,), name="hold")[1:]


def shaped(shape, dtype=f32):
    return jax.ShapeDtypeStruct(tuple(shape), dtype)


def whole(*shape):
    return pl.BlockSpec(shape, lambda *ids: (0,) * len(shape))


def rows_at(rows, width):
    return pl.BlockSpec((rows, width), lambda i: (i, 0))


SMEM = pl.BlockSpec(memory_space=pltpu.SMEM)


def dct_table(size):
    row = np.arange(size)[:, None]
    col = np.arange(size)[None, :]
    table = np.cos(math.pi * (col + 0.5) * row / size) * math.sqrt(2.0 / size)
    table[0] *= math.sqrt(0.5)
    return table.astype(np.float32)


def expand_table(head):
    half = ROT // 2
    table = np.zeros((ROT, 3 * LANE), np.float32)
    for lane in range(LANE):
        place = lane % head
        if place < half:
            table[place, lane] = 1.0
            table[half + place, LANE + lane] = -1.0
        elif place < ROT:
            table[place - half, lane] = 1.0
            table[place, 2 * LANE + lane] = 1.0
    return np.concatenate([table] * 3, axis=0)


def ends_of(lengths):
    ends, total = [], jnp.int32(0)
    for j in range(lengths.shape[0]):
        total = total + lengths[j]
        ends.append(total)
    return ends


def seq_start(ends, place):
    start = jnp.zeros_like(place)
    for end in ends:
        start = jnp.where(place >= end, end, start)
    return start


def iota(shape, dim):
    return lax.broadcasted_iota(jnp.int32, shape, dim)


def head_block(head, rows, cols):
    return iota((rows, cols), 0) // head == iota((rows, cols), 1) // head


def turn_tables(cs, expand, head, width):
    wide = tn(cs, expand)
    lane = iota((1, LANE), 1) % head
    cosine = wide[:, :LANE] + jnp.where(lane < ROT, 0.0, 1.0)
    times = width // LANE
    return tuple(
        beside(*[part] * times) for part in (cosine, wide[:, LANE : 2 * LANE], wide[:, 2 * LANE :])
    )


def turn(value, tables, sign):
    cosine, up, down = tables
    width = value.shape[1]
    half = ROT // 2
    moved = pltpu.roll(value, width - half, 1) * up + pltpu.roll(value, half, 1) * down
    return value * cosine + moved if sign > 0 else value * cosine - moved


def own_half(head, rows):
    return iota((rows, LANE), 1) // head == iota((rows, LANE), 0) // head % 2


def pairs_of(width):
    return [slice(p, p + LANE) for p in range(0, width, LANE)]


def outer_pairs(left, right, other):
    return below(
        *[tn(left[:, p], beside(right[:, p], other[:, p])) for p in pairs_of(left.shape[1])]
    )


def masked_state(full, head):
    half = own_half(head, full.shape[0])
    return jnp.where(beside(half, half), full, 0.0)


def fold_state(full, head):
    full = masked_state(full, head)
    return full[:, :LANE] + pltpu.roll(full[:, LANE:], LANE // 2, 1)


def unfold_state(packed, head):
    return masked_state(beside(packed, pltpu.roll(packed, LANE // 2, 1)), head)


def deal(outs, order, low, write):
    mine = lax.axis_index("batch") // low
    first, second, third = (1 << bit for bit in order)
    wanted = [base + i * third for base in (first + second, first, second, 0) for i in range(2)]
    slots = [(out, i) for out in outs for i in range(out.shape[0])]
    for (out, i), block in zip(slots, wanted):
        write(out, i, pl.multiple_of((mine ^ block) * LANE, LANE))


def feed_step(normed, c, up_w, up_b, down_w, hidden_o, gpre_o, ub_o, down_acc, up_acc):
    rows, width = hidden_o.shape
    pre = nn(normed, up_w[...]) + up_b[...]
    grad_hidden = nt(c, down_w[...])
    phi = 0.5 + 0.5 * lax.erf(pre * HALF_ROOT)
    hidden = (pre * phi).astype(bf16)
    hidden_o[...] = hidden
    down_acc[...] += tn(hidden, c)
    slope = phi + pre * jnp.exp(-0.5 * pre * pre) * GAUSS
    gpre = (grad_hidden * slope).astype(bf16)
    gpre_o[...] = gpre
    up_acc[...] += tn(normed, gpre)
    ub_o[...] += jnp.sum(gpre.astype(f32).reshape(rows // 8, 8, width), axis=0)


def clear(*refs):
    for ref in refs:
        ref[...] = jnp.zeros_like(ref)


def write_down(out, i, at, down_acc):
    out[i, : down_acc.shape[0], :] = down_acc[:, pl.ds(at, LANE)]


def write_up(out, i, at, up_acc):
    width = up_acc.shape[1]
    first = out.shape[1] - width
    for j in range(0, width, LANE):
        out[i, first + j : first + j + LANE, :] = up_acc[pl.ds(at, LANE), j : j + LANE]


def feed_specs(tokens, model, units, part):
    first, quarters = PARTS[part]
    width = units // 4 * quarters
    part = first // quarters
    ins = [
        pl.BlockSpec((model, width), lambda i: (0, part)),
        pl.BlockSpec((1, width), lambda i: (0, part)),
        pl.BlockSpec((width, model), lambda i: (part, 0)),
        rows_at(ROWS, model),
    ]
    outs = [rows_at(ROWS, width)] * 2 + [whole(8, width)]
    shapes = [shaped((tokens, width), bf16)] * 2 + [shaped((8, width))]
    scratch = [pltpu.VMEM((width, model), f32), pltpu.VMEM((model, width), f32)]
    return width, ins, outs, shapes, scratch


def feed(call, orders, low, normed, up_w, up_b, down_w, cot, **rest):
    tokens, model = cot.shape
    width, ins, outs, shapes, scratch = feed_specs(tokens, model, up_w.shape[1], 1)
    firsts, piece = shaped((4, width, LANE)), shaped((2, width, LANE))
    pieces_out = [firsts, piece, piece] * 2

    def body(normed, up_w, up_b, down_w, cot, hidden_o, gpre_o, ub_o, *refs):
        *pieces, down_acc, up_acc = refs
        step = pl.program_id(0)

        @pl.when(step == 0)
        def _():
            clear(down_acc, up_acc, ub_o)

        feed_step(
            normed[...], cot[...], up_w, up_b, down_w, hidden_o, gpre_o, ub_o, down_acc, up_acc
        )

        @pl.when(step == pl.num_programs(0) - 1)
        def _():
            deal(pieces[:3], orders[0], low, lambda *at: write_down(*at, down_acc))
            deal(pieces[3:], orders[1], low, lambda *at: write_up(*at, up_acc))

    return call(
        body,
        (normed, up_w, up_b, down_w, cot),
        [rows_at(ROWS, model), *ins],
        outs + [whole(*a.shape) for a in pieces_out],
        shapes + pieces_out,
        **rest,
        grid=(tokens // ROWS,),
        scratch_shapes=scratch,
        name="feed_forward",
    )


def take_columns(w_in, head, heads, part):
    return beside(*[w_in[:, (3 * h + part) * head : (3 * h + part + 1) * head] for h in range(heads)])


def features(part, tables, basis, head, feats):
    width = part.shape[1]
    turned = turn(part.astype(f32), tables, 1)
    square = (turned * turned).astype(bf16)
    ones = jnp.where(head_block(head, width, width), 1.0 / (2.0 * math.sqrt(head)), 0.0).astype(bf16)
    argument = exact3(nn, two(turned), basis) - nn(square, ones)
    return turned.astype(bf16), (jnp.exp(argument) * (1.0 / math.sqrt(feats))).astype(bf16)


def rotary_table(ends, first_pos, rows, tokens, out):
    half = ROT // 2
    order = iota((half, rows), 0)
    frequency = jnp.zeros((half, rows), f32)
    for j in range(half):
        value = float(np.float32(10000.0) ** np.float32(-2.0 * j / ROT))
        frequency = jnp.where(order == j, value, frequency)
    for i in range(tokens // rows):
        place = first_pos + i * rows + iota((half, rows), 1)
        angle = (place - seq_start(ends, place)).astype(f32) * frequency
        circle = below(jnp.cos(angle), jnp.sin(angle))
        high, rest = two(circle)
        middle, lowest = two(circle - high.astype(f32))
        out[i] = below(high, middle, lowest)


def front(
    call, head, lengths, x, gain, shift, up_w, up_b, down_w, cot, qkv_w, qkv_b, expand,
    samples, dct_t,
):
    tokens, model = x.shape
    width = qkv_w.shape[1] // 3
    heads = width // head
    feats = samples.shape[0]
    blocks = tokens // ROWS
    table = (blocks, expand.shape[0], ROWS)
    part, ins, outs, shapes, scratch = feed_specs(tokens, model, up_w.shape[1], 0)
    piece = shaped((model // LANE, 2 * part, LANE))

    def body(
        lengths, x, gain, shift, up_w, up_b, down_w, cot, qkv_w, qkv_b, expand, samples, dct_t,
        normed_o, cb_o, kf_o, v_o, kt_o, w_o, b_o, basis_o, cs_o, state_o, hidden_o, gpre_o, ub_o, piece_o,
        down_acc, up_acc, w_s, b_s, basis_s, cs_s, state_s,
    ):
        step = pl.program_id(0)
        ends = ends_of(lengths)
        first_pos = lax.axis_index("batch") * tokens
        start_last = seq_start(ends, first_pos + tokens - 1)

        @pl.when(step == 0)
        def _():
            clear(down_acc, up_acc, ub_o, cb_o, state_s)
            for part in range(3):
                to = slice(part * width, (part + 1) * width)
                w_s[:, to] = take_columns(qkv_w, head, heads, part)
                b_s[:, to] = take_columns(qkv_b, head, heads, part)
            basis = lax.dot_general(
                dct_t[...], samples[...], (((1,), (1,)), ((), ())),
                preferred_element_type=f32, precision=lax.Precision.HIGHEST,
            )
            basis = basis * (1.0 / head**0.25)
            wide = below(*[beside(*[basis] * heads)] * heads)
            basis_s[...] = jnp.where(head_block(head, width, width), wide, 0.0)
            basis_o[...] = basis_s[...]
            w_o[...] = w_s[...]
            b_o[...] = b_s[...]
            rotary_table(ends, first_pos, ROWS, tokens, cs_s)
            cs_o[...] = cs_s[...]

        xf = x[...].astype(f32)
        centered = xf - jnp.mean(xf, axis=1, keepdims=True)
        inv = lax.rsqrt(jnp.mean(centered * centered, axis=1, keepdims=True) + epsilon)
        normed = (centered * inv * gain[...] + shift[...]).astype(bf16)
        normed_o[...] = normed
        c = cot[...]
        cb_o[...] += jnp.sum(c.astype(f32).reshape(ROWS // 8, 8, model), axis=0)
        feed_step(normed, c, up_w, up_b, down_w, hidden_o, gpre_o, ub_o, down_acc, up_acc)

        projected = (nn(normed, w_s[:, width:]) + b_s[:, width:]).astype(bf16)
        tables = turn_tables(cs_s[step], expand[...], head, width)
        k_turn, k_feat = features(projected[:, :width], tables, two(basis_s[...]), head, feats)
        value = projected[:, width:]
        kf_o[...], v_o[...], kt_o[...] = k_feat, value, k_turn
        place = first_pos + step * ROWS + iota((ROWS, 1), 0)
        tail = jnp.where(place >= start_last, 1.0, 0.0).astype(bf16)
        state_s[...] += outer_pairs(k_feat * tail, value, jnp.ones_like(value))

        @pl.when(step == pl.num_programs(0) - 1)
        def _():
            state_o[...] = fold_state(state_s[...], head)
            for i in range(piece.shape[0]):
                write_down(piece_o, i, i * LANE, down_acc)
                write_up(piece_o, i, i * LANE, up_acc)

    narrow = shaped((tokens, width), bf16)
    return call(
        body,
        (lengths, x, gain, shift, up_w, up_b, down_w, cot, qkv_w, qkv_b, expand, samples, dct_t),
        [SMEM, rows_at(ROWS, model), whole(1, model), whole(1, model), *ins]
        + [whole(*a.shape) for a in (qkv_w, qkv_b, expand, samples, dct_t)],
        [rows_at(ROWS, model), whole(8, model), *[rows_at(ROWS, width)] * 3]
        + [whole(model, 3 * width), whole(1, 3 * width), whole(width, width), whole(*table)]
        + [whole(width, LANE), *outs]
        + [whole(*piece.shape)],
        [shaped((tokens, model), bf16), shaped((8, model)), *[narrow] * 3]
        + [shaped((model, 3 * width), bf16), shaped((1, 3 * width)), shaped((width, width))]
        + [shaped(table, bf16)]
        + [shaped((width, LANE)), *shapes, piece],
        grid=(blocks,),
        scratch_shapes=[
            *scratch,
            pltpu.VMEM((model, 3 * width), bf16),
            pltpu.VMEM((1, 3 * width), f32),
            pltpu.VMEM((width, width), f32),
            pltpu.VMEM(table, bf16),
            pltpu.VMEM((width, 2 * LANE), f32),
        ],
        name="front",
    )


def project_queries(call, head, feats, normed, w, b, expand, basis, cs, cot, out_w):
    tokens, model = normed.shape
    width = out_w.shape[0]

    def body(normed, w, b, expand, basis, cs, cot, out_w, qf_o, qt_o, ga_o):
        projected = (nn(normed[...], w[...]) + b[...]).astype(bf16)
        ga_o[...] = nt(cot[...], out_w[...])
        tables = turn_tables(cs[0], expand[...], head, width)
        qt_o[...], qf_o[...] = features(projected, tables, two(basis[...]), head, feats)

    return call(
        body,
        (normed, w, b, expand, basis, cs, cot, out_w),
        [
            rows_at(ROWS, model),
            whole(model, width),
            whole(1, width),
            whole(*expand.shape),
            whole(*basis.shape),
            pl.BlockSpec((1,) + cs.shape[1:], lambda i: (i, 0, 0)),
            rows_at(ROWS, model),
            whole(*out_w.shape),
        ],
        [rows_at(ROWS, width)] * 3,
        [shaped((tokens, width), bf16), shaped((tokens, width), bf16), shaped((tokens, width))],
        grid=(tokens // ROWS,),
        name="project_queries",
    )


def swapped(value, axis, distance):
    size = lax.axis_size(axis)
    return lax.ppermute(value, axis, [(i, i ^ distance) for i in range(size)])


def joined(forward, lengths, tokens, base, entered, own, came):
    ends = ends_of(lengths)
    here = lax.axis_index("batch")
    count, size = 1, 2
    group = (here >> (base + count)) << (base + count)
    mine = (here >> base) & (size - 1)
    group_end = (group + (size << base)) * tokens
    total = jnp.zeros_like(own)
    entered = total if entered is None else entered
    for m in range(size):
        part = came if m else own
        other = mine ^ m
        if forward:
            edge = (group + ((other + 1) << base)) * tokens
            enters = (other < mine) & (seq_start(ends, here * tokens - 1) < edge)
            counts = seq_start(ends, group_end - 1) < edge
        else:
            start = seq_start(ends, (group + (other << base)) * tokens - 1)
            enters = (other > mine) & (start < (here + 1) * tokens)
            counts = start < group * tokens
        if m:
            entered = entered + jnp.where(enters, part, 0.0)
        total = total + jnp.where(counts, part, 0.0)
    return entered, total


def join_states(call, forward, tokens, base, lengths, entered, own, came, **rest):
    given = [own, came] if entered is None else [entered, own, came]

    def body(lengths, *refs):
        *ins, entered_o, total_o = refs
        values = [r[...] for r in ins]
        if entered is None:
            values = [None, *values]
        entered_o[...], total_o[...] = joined(
            forward, lengths, tokens, base, *values
        )

    spec = whole(*own.shape)
    return call(
        body,
        (lengths, *given),
        [SMEM] + [spec] * len(given),
        [spec, spec],
        [shaped(own.shape)] * 2,
        **rest,
        grid=(1,),
        name="join_states",
    )


def turned_grad(grad_feat, feat, turned, basis, tables, head, width):
    weighted = (grad_feat * feat.astype(f32)).astype(bf16)
    ones = jnp.where(head_block(head, width, width), 1.0 / math.sqrt(head), 0.0).astype(bf16)
    grad = nt(beside(weighted, weighted), beside(*basis)) - nn(weighted, ones) * turned.astype(f32)
    return turn(grad, tables, -1).astype(bf16)


def attend_kernel(
    head, tokens, per_step, base, lengths, qf, kf, v, qt, ga, cs, expand, basis_i,
    normed, cot, hidden0, hidden1, down_w, out_w, entered_i, own_i, came_i,
    gq_o, gk_o, gv_o, back_o, total_o, qb_o, keep_o, far0_o, far1_o, near_o, *refs,
):
    piece_o, state_s, q_acc, o_acc, total_s = refs
    step = pl.program_id(0)
    width = qf.shape[1]
    heads = width // head
    ends = ends_of(lengths)
    first_pos = lax.axis_index("batch") * tokens

    @pl.when(step == 0)
    def _():
        entered, _ = joined(
            True, lengths, tokens, base, entered_i[...], own_i[...], came_i[...]
        )
        state_s[...] = unfold_state(entered, head)
        q_acc[...] = jnp.zeros_like(q_acc)
        o_acc[...] = jnp.zeros_like(o_acc)
        total_s[...] = jnp.zeros_like(total_s)
        qb_o[...] = jnp.zeros_like(qb_o)

    basis = two(basis_i[...])
    block = head_block(head, width, width)
    ones = jnp.where(block, 1.0, 0.0).astype(bf16)
    lanes = [jnp.where(iota((1, width), 1) // head == h, 1.0, 0.0).astype(bf16) for h in range(heads)]
    state = state_s[...]
    total = total_s[...]
    part = hidden0.shape[1]
    subs = range(per_step)
    ats = [slice(sub * CHUNK, (sub + 1) * CHUNK) for sub in subs]
    row = iota((CHUNK, 1), 0)
    col = iota((CHUNK, CHUNK), 1)
    causal = col <= iota((CHUNK, CHUNK), 0)
    windows, carries, states, live = [], [], [], []
    for sub, at in zip(subs, ats):
        begin = first_pos + (step * per_step + sub) * CHUNK
        last = seq_start(ends, begin + CHUNK - 1)
        start = seq_start(ends, begin + row)
        windows.append(causal & (col + begin >= start))
        carries.append(jnp.where(start < begin, 1.0, 0.0))
        live.append(jnp.where(seq_start(ends, begin - 1) < first_pos, 1.0, 0.0))
        states.append(two(state))
        tail = jnp.where(begin + row >= last, 1.0, 0.0).astype(bf16)
        retain = jnp.where(last < begin, 1.0, 0.0)
        value = v[at, :]
        added = outer_pairs(kf[at, :] * tail, value, jnp.ones_like(value))
        state = retain * state + masked_state(added, head)
    scores = [
        [jnp.where(window, nt(qf[at, :] * lane, kf[at, :]), 0.0).astype(bf16) for lane in lanes]
        for at, window in zip(ats, windows)
    ]
    outward = nn(hidden1[...], down_w[:-part]) + nn(hidden0[...], down_w[-part:])
    q_carries = [qf[at, :] * c.astype(bf16) for at, c in zip(ats, carries)]
    attends, overs, mixes = [], [], []
    for sub, at in zip(subs, ats):
        nums, dens = [], []
        for p, pair in enumerate(pairs_of(width)):
            mine = range(p * LANE // head, (p + 1) * LANE // head)
            right = [
                beside(v[at, pair] * lanes[h][:, pair], jnp.broadcast_to(lanes[h][:, pair], (CHUNK, LANE)))
                for h in mine
            ]
            carry = q_carries[sub][:, pair]
            sums = nn(
                beside(*[scores[sub][h] for h in mine], carry, carry),
                below(*right, states[sub][0][pair, :], states[sub][1][pair, :]),
            )
            nums.append(sums[:, :LANE])
            dens.append(sums[:, LANE:])
        overs.append(1.0 / beside(*dens))
        attends.append(beside(*nums) * overs[sub])
        mixes.append(attends[sub].astype(bf16))
    g_nums = [(ga[at, :] * over).astype(bf16) for at, over in zip(ats, overs)]
    g_dens = []
    for g_num, attended in zip(g_nums, attends):
        product = two(g_num.astype(f32) * attended)
        g_dens.append(-nn(beside(*product), below(ones, ones)))
    g_heads = [[g_num * lane for lane in lanes] for g_num in g_nums]
    mixing = [
        [
            jnp.where(
                windows[sub], nt(g_heads[sub][h], v[at, :]) + g_dens[sub][:, h * head : h * head + 1], 0.0
            ).astype(bf16)
            for h in range(heads)
        ]
        for sub, at in zip(subs, ats)
    ]
    grad_fqs = []
    for sub, at in zip(subs, ats):
        den_two = two(g_dens[sub] * (2.0 / head))
        den_both = jnp.where(iota((1, width), 1) % head < head // 2, den_two[0], den_two[1])
        from_state = []
        for pair in pairs_of(width):
            left = beside(g_nums[sub][:, pair], den_both[:, pair])
            from_state.append(
                nt(beside(left, left), beside(states[sub][0][pair, :], states[sub][1][pair, :]))
            )
        grad_fqs.append(
            carries[sub] * beside(*from_state)
            + nn(beside(*mixing[sub]), below(*[kf[at, :] * lane for lane in lanes]))
        )
    gqs = []
    for sub, at in zip(subs, ats):
        tables = turn_tables(cs[0, :, at], expand[...], head, width)
        gqs.append(turned_grad(grad_fqs[sub], qf[at, :], qt[at, :], basis, tables, head, width))
    for sub, at in zip(subs, ats):
        gk_o[at, :] = tn(below(*mixing[sub]), below(*[qf[at, :] * lane for lane in lanes]))
        gv_o[at, :] = tn(below(*scores[sub]), below(*g_heads[sub]))
        back = fold_state(outer_pairs(q_carries[sub], g_nums[sub], g_dens[sub].astype(bf16)), head)
        back_o[sub] = back
        total = total + live[sub] * back
    gq = below(*gqs)
    gq_o[...] = gq
    qb_o[...] += jnp.sum(gq.astype(f32).reshape(per_step * CHUNK // 8, 8, width), axis=0)
    q_acc[...] += tn(normed[...], gq)
    o_acc[...] += tn(below(*mixes), cot[...])
    state_s[...] = state
    total_s[...] = total
    outward = outward + nn(below(*mixes), out_w[...])
    by_core(step, outward, keep_o, far0_o, far1_o, near_o)

    @pl.when(step == pl.num_programs(0) - 1)
    def _():
        total_o[...] = total

        for i in range(piece_o.shape[0]):
            write_down(piece_o, i, i * LANE, o_acc)
            write_up(piece_o, i, i * LANE, q_acc)


def by_core(share, value, keep, far0, far1, near):
    core, chip = branch_place()
    other, mine = share & 1 != core, share >> 1 == chip

    @pl.when(jnp.logical_not(other))
    def _():
        keep[0] = value

    @pl.when(other & jnp.logical_not(mine))
    def _():
        far0[...] = value[: ROWS // 2]
        far1[...] = value[ROWS // 2 :]

    @pl.when(other & mine)
    def _():
        near[...] = value


def attend(
    call, head, base, lengths, qf, kf, v, qt, ga, cs, expand, basis, normed, cot,
    hidden0, hidden1, down_w, out_w, entered, own, came, **rest,
):
    tokens, width = qf.shape
    model = cot.shape[1]
    per_step = ROWS // CHUNK
    chunks = tokens // CHUNK
    part = hidden0.shape[1]
    piece = shaped((model // LANE, 2 * width, LANE))
    chip = pl.BlockSpec((1, ROWS, model), lambda i: (i >> 1 ^ (1 - branch_place()[1]), 0, 0))
    sent = [shaped((rows, model)) for rows in (ROWS // 2, ROWS // 2, ROWS)]
    row = rows_at(ROWS, width)
    packed = whole(width, LANE)

    def body(*refs):
        attend_kernel(head, tokens, per_step, base, *refs)

    return call(
        body,
        (lengths, qf, kf, v, qt, ga, cs, expand, basis, normed, cot, hidden0, hidden1, down_w, out_w)
        + (entered, own, came),
        [
            SMEM,
            *[row] * 5,
            pl.BlockSpec((1,) + cs.shape[1:], lambda i: (i, 0, 0)),
            whole(*expand.shape),
            whole(width, width),
            rows_at(ROWS, model),
            rows_at(ROWS, model),
            rows_at(ROWS, part),
            rows_at(ROWS, hidden1.shape[1]),
            whole(*down_w.shape),
            whole(*out_w.shape),
            *[packed] * 3,
        ],
        [
            *[row] * 3,
            pl.BlockSpec((per_step, width, LANE), lambda i: (i, 0, 0)),
            packed,
            whole(8, width),
            chip,
            *[whole(*a.shape) for a in sent],
            whole(*piece.shape),
        ],
        [
            shaped((tokens, width), bf16),
            shaped((tokens, width)),
            shaped((tokens, width)),
            shaped((chunks, width, LANE)),
            shaped((width, LANE)),
            shaped((8, width)),
            shaped((tokens // ROWS // 2, ROWS, model)),
            *sent,
            piece,
        ],
        **rest,
        grid=(tokens // ROWS,),
        scratch_shapes=[
            pltpu.VMEM((width, 2 * LANE), f32),
            pltpu.VMEM((model, width), f32),
            pltpu.VMEM((width, model), f32),
            pltpu.VMEM((width, LANE), f32),
        ],
        name="attend",
        flops=COST_ATTEND,
    )


def branch_place():
    here = lax.axis_index("branch")
    return here & 1, here >> 1


def keys(
    call, head, order, low, base, lengths, kf, v, kt, gk, gv, back, cs, expand, basis, normed,
    entered, own, came, **rest,
):
    tokens, width = kf.shape
    model = normed.shape[1]
    chunks, per_step = tokens // CHUNK, ROWS // CHUNK
    row = lambda n: rows_at(ROWS, n)
    packed = whole(width, LANE)
    firsts, piece = shaped((4, 2 * width, LANE)), shaped((2, 2 * width, LANE))
    acc_shape = (model, 2 * width)

    def body(
        lengths, kf, v, kt, gk, gv, back, cs, expand, basis_i, normed, entered_i, own_i, came_i,
        gkv_o, kvb_o, *refs,
    ):
        *pieces, acc, state_s = refs
        step = pl.program_id(0)
        ends = ends_of(lengths)
        first_pos = lax.axis_index("batch") * tokens

        @pl.when(step == 0)
        def _():
            clear(kvb_o, acc)
            state, _ = joined(
                False, lengths, tokens, base, entered_i[...], own_i[...], came_i[...]
            )
            for chunk in reversed(range(chunks)):
                state_s[chunk] = state
                begin = first_pos + chunk * CHUNK
                last = seq_start(ends, begin + CHUNK - 1)
                state = back[chunk] + jnp.where(last < begin, state, 0.0)

        basis = two(basis_i[...])
        tables = turn_tables(cs[0], expand[...], head, width)
        share = jnp.full((CHUNK, LANE), 1.0 / head, bf16)
        heres = [slice(sub * CHUNK, (sub + 1) * CHUNK) for sub in range(per_step)]
        tails, states = [], []
        for sub in range(per_step):
            begin = first_pos + (step * per_step + sub) * CHUNK
            last = seq_start(ends, begin + CHUNK - 1)
            tails.append(jnp.where(begin + iota((CHUNK, 1), 0) >= last, 1.0, 0.0))
            states.append(two(unfold_state(state_s[step * per_step + sub], head)))
        grad_fks, grad_vs = [], []
        for here, tail, state in zip(heres, tails, states):
            to_k, to_v = [], []
            for pair in pairs_of(width):
                high, low_ = state[0][pair, :], state[1][pair, :]
                left = beside(v[here, pair], share)
                to_k.append(nt(beside(left, left), beside(high, low_)))
                to_v.append(
                    nn(beside(kf[here, pair], kf[here, pair]), below(high[:, :LANE], low_[:, :LANE]))
                )
            grad_fks.append(gk[here, :] + tail * beside(*to_k))
            grad_vs.append((gv[here, :] + tail * beside(*to_v)).astype(bf16))
        grad_k = turned_grad(below(*grad_fks), kf[...], kt[...], basis, tables, head, width)
        grads = [beside(grad_k, below(*grad_vs))]
        both = below(*grads)
        gkv_o[...] = both
        kvb_o[...] += jnp.sum(both.astype(f32).reshape(ROWS // 8, 8, 2 * width), axis=0)
        acc[...] += tn(normed[...], both)

        @pl.when(step == pl.num_programs(0) - 1)
        def _():
            deal(pieces, order, low, lambda *spot: write_up(*spot, acc))

    pieces = [firsts, piece, piece]
    return call(
        body,
        (lengths, kf, v, kt, gk, gv, back, cs, expand, basis, normed, entered, own, came),
        [SMEM, *[row(width)] * 5]
        + [whole(*back.shape)]
        + [pl.BlockSpec((1,) + cs.shape[1:], lambda i: (i, 0, 0)), whole(*expand.shape)]
        + [whole(width, width), row(model), *[packed] * 3],
        [row(2 * width), whole(8, 2 * width), *[whole(*a.shape) for a in pieces]],
        [shaped((tokens, 2 * width), bf16), shaped((8, 2 * width)), *pieces],
        **rest,
        grid=(tokens // ROWS,),
        scratch_shapes=[pltpu.VMEM(acc_shape, f32), pltpu.VMEM((chunks, width, LANE), f32)],
        name="keys",
    )


def inward(call, far, x, gpre0, gpre1, gq, gkv, up_w, qkv_w, **rest):
    tokens, model = x.shape
    part = gpre0.shape[1]

    def at(i):
        core, chip = branch_place()
        return 2 * (1 - chip) + i if far else 2 * chip + (i ^ (1 - core))

    row = lambda a: pl.BlockSpec((ROWS, a.shape[1]), lambda i: (at(i), 0))

    def body(x, gpre0, gpre1, gq, gkv, up_w, qkv_w, *refs):
        *outs, gain_o, shift_o = refs
        step = pl.program_id(0)

        @pl.when(step == 0)
        def _():
            clear(gain_o, shift_o)

        grad = nt(gpre1[...], up_w[:, :-part]) + nt(gpre0[...], up_w[:, -part:])
        grad = grad + nt(beside(gq[...], gkv[...]), qkv_w[...])
        if far:
            outs[0][0] = grad
        else:

            @pl.when(step == 0)
            def _():
                outs[0][...] = grad[: ROWS // 2]
                outs[1][...] = grad[ROWS // 2 :]

            @pl.when(step == 1)
            def _():
                outs[2][...] = grad

        xf = x[...].astype(f32)
        centered = xf - jnp.mean(xf, axis=1, keepdims=True)
        unit = centered * lax.rsqrt(jnp.mean(centered * centered, axis=1, keepdims=True) + epsilon)
        gain_o[...] += jnp.sum((grad * unit).reshape(ROWS // 8, 8, model), axis=0)
        shift_o[...] += jnp.sum(grad.reshape(ROWS // 8, 8, model), axis=0)

    if far:
        specs = [pl.BlockSpec((1, ROWS, model), lambda i: (i, 0, 0))]
        shapes = [shaped((2, ROWS, model))]
    else:
        shapes = [shaped((rows, model)) for rows in (ROWS // 2, ROWS // 2, ROWS)]
        specs = [whole(*a.shape) for a in shapes]
    return call(
        body,
        (x, gpre0, gpre1, gq, gkv, up_w, qkv_w),
        [row(a) for a in (x, gpre0, gpre1, gq, gkv)] + [whole(*up_w.shape), whole(*qkv_w.shape)],
        specs + [whole(8, model)] * 2,
        shapes + [shaped((8, model))] * 2,
        **rest,
        grid=(2,),
        name="inward",
    )


def finish_small(call, one, other, sizes):
    shapes = [shaped((size // LANE, LANE)) for size in sizes]

    def body(one, other, *outs):
        row = 0
        for out in outs:
            out[...] = one[row : row + out.shape[0], :] + other[row : row + out.shape[0], :]
            row += out.shape[0]

    parts = call(
        body,
        (one, other),
        [whole(*one.shape)] * 2,
        [whole(*a.shape) for a in shapes],
        shapes,
        grid=(1,),
        name="finish_small",
    )
    return [part.reshape(-1) for part in parts]


def block_of(array, count, at):
    shape = (count,) + array.shape[1:]
    return pl.BlockSpec(shape, lambda i: (at() if callable(at) else at,) + (0,) * (len(shape) - 1))


def sums_of(call, *jobs, stack=False, **rest):
    arrays, specs, shapes = [], [], []
    for job in jobs:
        for array, count, at in job:
            arrays.append(array)
            specs.append(block_of(array, count, at))
        shapes.append(shaped((count,) + array.shape[1:]))
    counts = [a.shape[0] for a in shapes]
    if stack:
        shapes = [shaped((sum(counts),) + shapes[0].shape[1:])]
    outs = [whole(*a.shape) for a in shapes]

    def body(*refs):
        ins, results = refs[: len(arrays)], refs[len(arrays) :]
        start = 0
        for i, job in enumerate(jobs):
            mine, ins = ins[: len(job)], ins[len(job) :]
            value = sum(r[...] for r in mine[1:]) + mine[0][...]
            if stack:
                results[0][start : start + counts[i]] = value
                start += counts[i]
            else:
                results[i][...] = value

    return call(body, arrays, specs, outs, shapes, grid=(1,), name="sums", **rest)


def whole_of(array):
    return array, array.shape[0], 0


def finish_feed(call, one, down, up, **rest):
    args, specs = [one], [block_of(one, 1, 0)]
    for piece, first, two_came, (three_came, which) in (down, up):
        args += [piece[2], first, two_came, three_came]
        specs += [block_of(a, 1, at) for a, at in zip(args[-4:], (0, 2, 0, which))]
    widths = [down[0][2].shape[1], one.shape[1] // 2]

    def body(one, *refs):
        down_o, up_o = refs[-2:]
        values = []
        for a, b, c, d in (refs[:4], refs[4:8]):
            values.append((a[0] + b[0]) + (c[0] + d[0]))
        downs = (values[0], one[0, : widths[1]])
        ups = (values[1], one[0, widths[1] :])
        for down, up, start, width in zip(downs, ups, (0, widths[0]), widths):
            down_o[start : start + width, :] = down
            for j in range(0, width, LANE):
                up_o[:, start + j : start + j + LANE] = up[j : j + LANE, :]

    shapes = [shaped((sum(widths), LANE)), shaped((LANE, sum(widths)))]
    return call(
        body, args, specs, [whole(*a.shape) for a in shapes], shapes, grid=(1,), name="finish_feed", **rest
    )


def finish_heads(call, head, one, key_val, **rest):
    piece, first, two_came, three_came = key_val
    args = [one, piece[2], first, two_came, three_came]
    specs = [block_of(a, 1, at) for a, at in zip(args, (0, 0, 2, 0, 0))]
    width = one.shape[1] // 2
    heads = width // head

    def body(one, a, b, c, d, out_o, qkv_o):
        value = (a[0] + b[0]) + (c[0] + d[0])
        out_o[...] = one[0, :width]
        columns = []
        for rows in (one[0, width:], value[:width], value[width:]):
            columns.append(beside(*[rows[j * LANE : (j + 1) * LANE] for j in range(width // LANE)]))
        qkv_o[...] = beside(*[p[:, h * head : (h + 1) * head] for h in range(heads) for p in columns])

    shapes = [shaped((width, LANE)), shaped((LANE, 3 * width))]
    return call(
        body, args, specs, [whole(*a.shape) for a in shapes], shapes, grid=(1,), name="finish_heads", **rest
    )


def far_sums(call, keep, came, **rest):
    rows, model = CHUNK, keep.shape[2]
    steps = keep.shape[1] // rows
    halves = isinstance(came, tuple)
    spec = lambda at: pl.BlockSpec((1, rows, model), lambda i: (at, i, 0))

    def body(keep, *refs):
        *came, out = refs
        if halves:
            out[...] = keep[0] + jnp.where(pl.program_id(0) == 0, came[0][...], came[1][...])
        else:
            out[...] = keep[0] + came[0][0]

    return call(
        body,
        (keep, *came) if halves else (keep, came),
        [spec(0), *([whole(rows, model)] * 2 if halves else [spec(1)])],
        [rows_at(rows, model)],
        [shaped(keep.shape[1:])],
        grid=(steps,),
        name="far_sums",
        **rest,
    )


def finish_specs(share, model):
    steps = share // CHUNK
    own = pl.BlockSpec((CHUNK, model), lambda i: (lax.axis_index("branch") * steps + i, 0))
    return own, rows_at(CHUNK, model), steps


def finish_output(call, x, keep, came_core, came_chip, bias):
    share, model = came_chip.shape
    own, row, steps = finish_specs(share, model)

    def body(x, keep, core, chip, bias, out):
        total = (keep[0] + core[...]) + chip[...]
        out[...] = (x[...].astype(f32) + total + bias[...]).astype(bf16)

    return call(
        body,
        (x, keep, came_core, came_chip, bias),
        [own, pl.BlockSpec((1, CHUNK, model), lambda i: (1, i, 0)), row, row, whole(1, model)],
        [row],
        [shaped((share, model), bf16)],
        grid=(steps,),
        name="finish_output",
    )[0]


def finish_input(call, x, cot, gain, keep, came_core, came_chip, **rest):
    share, model = came_chip.shape
    own, row, steps = finish_specs(share, model)


    def body(x, cot, gain, keep, core0, core1, chip, out):
        core = jnp.where(pl.program_id(0) == 0, core0[...], core1[...])
        xf = x[...].astype(f32)
        centered = xf - jnp.mean(xf, axis=1, keepdims=True)
        inv = lax.rsqrt(jnp.mean(centered * centered, axis=1, keepdims=True) + epsilon)
        unit = centered * inv
        g = ((keep[...] + core) + chip[...]) * gain[...]
        inner = g - jnp.mean(g, axis=1, keepdims=True) - unit * jnp.mean(g * unit, axis=1, keepdims=True)
        out[...] = inv * inner + cot[...].astype(f32)

    return call(
        body,
        (x, cot, gain, keep, *came_core, came_chip),
        [own, own, whole(1, model), row, *[whole(CHUNK, model)] * 2, row],
        [row],
        [shaped((share, model))],
        **rest,
        grid=(steps,),
        name="finish_input",
    )[0]


def pack_small(call, head, branch, gains, shifts, cot, qb, kvb, ubs, **rest):
    model = cot.shape[1]
    width = qb.shape[1]
    heads = width // head
    up_width = sum(u.shape[1] for u in ubs)
    qkv_rows, up_rows = 3 * width // LANE, up_width // LANE
    starts = [0, model // LANE, 2 * model // LANE, 3 * model // LANE]
    starts.append(starts[3] + qkv_rows * branch)
    total = starts[4] + up_rows * branch

    def body(gain0, gain1, shift0, shift1, cot, qb, kvb, ub0, ub1, out):
        out[...] = jnp.zeros_like(out)
        here = lax.axis_index("branch")

        def summed(value):
            return jnp.sum(value, axis=0, keepdims=True)

        def place(row, value):
            for j in range(value.shape[1] // LANE):
                out[pl.ds(row + j, 1), :] = value[:, j * LANE : (j + 1) * LANE]

        place(starts[0], summed(gain0[...] + gain1[...]))
        place(starts[1], summed(shift0[...] + shift1[...]))
        place(starts[2], summed(cot[...]) * jnp.where(here == 0, 1.0, 0.0))
        q, kv = summed(qb[...]), summed(kvb[...])
        parts = (q, kv[:, :width], kv[:, width:])
        place(
            starts[3] + here * qkv_rows,
            beside(*[p[:, h * head : (h + 1) * head] for h in range(heads) for p in parts]),
        )
        place(starts[4] + here * up_rows, beside(summed(ub1[...]), summed(ub0[...])))

    args = (*gains, *shifts, cot, qb, kvb, *ubs)
    return call(
        body,
        args,
        [whole(*a.shape) for a in args],
        [whole(total, LANE)],
        [shaped((total, LANE))],
        grid=(1,),
        name="pack_small",
        **rest,
    )


def finish(part, dim, low):
    if low == 1:
        return part
    size = lax.axis_size("batch")
    groups = [[j * low + i for i in range(low)] for j in range(size // low)]
    return lax.psum_scatter(
        part, "batch", scatter_dimension=dim, axis_index_groups=groups, tiled=True
    )


def per_device(
    inputs, ln_gain, ln_shift, qkv_weight, qkv_bias, out_weight, up_weight, up_bias, down_weight,
    out_bias, feature_samples, lengths, cotangent,
):
    tokens, model = inputs.shape
    feats, head = feature_samples.shape
    width = out_weight.shape[0]
    batch = lax.axis_size("batch")
    branch = lax.axis_size("branch")
    low = batch // (model // LANE)
    y_first, z_first = (0, 1, 2), (1, 2, 0)
    bits = [1 << b for b in range(batch.bit_length() - 1)]
    expand = jnp.asarray(expand_table(head), bf16)
    dct_t = jnp.asarray(dct_table(head).T)
    gain = ln_gain.reshape(1, model)
    shift = ln_shift.reshape(1, model)
    up_b = up_bias.reshape(1, -1)
    qkv_b = qkv_bias.reshape(1, -1)
    call = Order()

    def send(value, order, step):
        return swapped(value, "batch", low << order[step])

    def enter(forward, own, came):
        entered = None
        for i, bit in enumerate(bits[1:]):
            entered, own = join_states(call, forward, tokens, i, lengths, entered, own, came)
            came = swapped(own, "batch", bit)
        return entered, own, came

    normed, cb, kf, value, kt, w_perm, b_perm, basis, cs, state, hidden0, gpre0, ub0, piece0 = front(
        call, head, lengths, inputs, gain, shift, up_weight, up_b, down_weight, cotangent, qkv_weight,
        qkv_b, expand, feature_samples, dct_t,
    )
    groups = [[j * low + i for j in range(batch // low)] for i in range(low)] if low > 1 else None

    def scattered(piece):
        return lax.psum_scatter(
            piece, "batch", scatter_dimension=0, axis_index_groups=groups, tiled=True
        )

    sum0 = scattered(piece0)
    came = swapped(state, "batch", 1)
    qf, qt, ga = project_queries(
        call, head, feats, normed, w_perm, b_perm, expand, basis, cs, cotangent, out_weight
    )
    states = enter(True, state, came)
    hidden1, gpre1, ub1, *pieces = feed(
        call, (y_first, z_first), low, normed, up_weight, up_b, down_weight, cotangent
    )
    down, up = pieces[:3], pieces[3:]
    down_first, up_first = send(down[0], y_first, 0), send(up[0], z_first, 0)
    gq, gk, gv, back, state, qb, out_keep, far0, far1, out_near, oq = attend(
        call, head, len(bits) - 1, lengths, qf, kf, value, qt, ga, cs, expand, basis, normed, cotangent,
        hidden0, hidden1, down_weight, out_weight, *states,
    )
    came = swapped(state, "batch", 1)
    far_core = swapped(far0, "branch", 1), swapped(far1, "branch", 1)
    (out_far,) = far_sums(call, out_keep, far_core)
    out_chip = swapped(out_far, "branch", 2)
    entered, state = join_states(call, False, tokens, 0, lengths, None, state, came)
    came = swapped(state, "batch", bits[1])
    down_2, up_2, out_near = sums_of(
        call, [whole_of(down[1]), (down_first, 2, 0)], [whole_of(up[1]), (up_first, 2, 0)],
        after=(sum0,), through=(out_near,),
    )
    out_core = swapped(out_near, "branch", 1)
    for i in range(1, len(bits) - 1):
        entered, state = join_states(call, False, tokens, i, lengths, entered, state, came)
        came = swapped(state, "batch", bits[i + 1])
    down_2, up_2, oq = hold(call, (down_2, up_2, oq))
    sum_oq = scattered(oq)
    down_2, up_2 = send(down_2, y_first, 1), send(up_2, z_first, 1)
    gkv, kvb, *kv = keys(
        call, head, y_first, low, len(bits) - 1, lengths, kf, value, kt, gk, gv, back, cs, expand,
        basis, normed, entered, state, came, flops=COST_KEYS,
    )
    kv_first = send(kv[0], y_first, 0)
    in_args = (inputs, gpre0, gpre1, gq, gkv, up_weight, w_perm)
    far, gain0, shift0 = inward(call, True, *in_args, after=(out_core,), flops=COST_FAR)
    cores = [[i, i + 1] for i in range(0, branch, 2)]
    far = lax.all_to_all(far, "branch", 0, 0, axis_index_groups=cores, tiled=True)
    (grad_far,) = far_sums(call, far, far)
    grad_chip = swapped(grad_far, "branch", 2)
    kv_2, down_3, up_3 = sums_of(
        call, [whole_of(kv[1]), (kv_first, 2, 0)],
        [(down[2], 1, 1), (down_first, 1, 3), (down_2, 1, 1)],
        [(up[2], 1, 1), (up_first, 1, 3), (up_2, 1, 1)],
    )
    kv_2, down_3, up_3 = send(kv_2, y_first, 1), send(down_3, y_first, 2), send(up_3, z_first, 2)
    near0, near1, grad_keep, gain1, shift1 = inward(call, False, *in_args, flops=COST_NEAR)
    (small,) = pack_small(
        call, head, branch, (gain0, gain1), (shift0, shift1), cb, qb, kvb, (ub0, ub1),
        after=(out_chip,),
    )
    came = swapped(small, "batch", 1)
    grad_core = swapped(near0, "branch", 1), swapped(near1, "branch", 1)
    output = finish_output(
        call, inputs, out_keep, out_core, out_chip, out_bias.reshape(1, model)
    )
    (small,) = sums_of(call, [whole_of(small), whole_of(came)])
    came = swapped(small, "batch", bits[1])
    down_sum, up_sum = finish_feed(
        call, sum0, (down, down_first, down_2, (down_3, 0)), (up, up_first, up_2, (up_3, 0))
    )
    for bit in bits[2:]:
        (small,) = sums_of(call, [whole_of(small), whole_of(came)])
        came = swapped(small, "batch", bit)
    (kv_3,) = sums_of(call, [(kv[2], 1, 1), (kv_first, 1, 3), (kv_2, 1, 1)])
    kv_3 = send(kv_3, y_first, 2)
    (small,) = sums_of(call, [whole_of(small), whole_of(came)])
    came = swapped(small, "branch", 1)
    (small,) = sums_of(call, [whole_of(small), whole_of(came)], flops=COST_END)
    came = swapped(small, "branch", 2)
    input_grad = finish_input(
        call, inputs, cotangent, gain, grad_keep, grad_core, grad_chip, after=(sum_oq,)
    )
    small = finish_small(call, small, came, [model, model, model, 3 * width * branch, up_bias.size * branch])
    out_sum, qkv_sum = finish_heads(call, head, sum_oq, (kv, kv_first, kv_2, kv_3))
    down_sum, out_sum = finish(down_sum, 1, low), finish(out_sum, 1, low)
    up_sum, qkv_sum = finish(up_sum, 0, low), finish(qkv_sum, 0, low)

    gain_grad, shift_grad, out_bias_grad, qkv_bias_grad, up_bias_grad = small
    return (
        output,
        input_grad,
        gain_grad,
        shift_grad,
        qkv_sum,
        qkv_bias_grad,
        out_sum,
        up_sum,
        up_bias_grad,
        down_sum,
        out_bias_grad,
    )


def solution(mesh):
    placed = (
        P("batch", None),
        P(),
        P(),
        P(None, "branch"),
        P("branch"),
        P("branch", None),
        P(None, "branch"),
        P("branch"),
        P("branch", None),
        P(),
        P(),
        P(),
        P("batch", None),
    )
    return jax.shard_map(
        per_device,
        mesh=mesh,
        in_specs=placed,
        out_specs=(
            P(("batch", "branch"), None),
            P(("batch", "branch"), None),
            P(),
            P(),
            P("batch", "branch"),
            P(),
            P("branch", "batch"),
            P("batch", "branch"),
            P(),
            P("branch", "batch"),
            P(),
        ),
        check_vma=False,
    )
```
